512 devices in a mesh: ctx: 128 (over y_hi, z, x), kv: 4 (over y_lo, core).
Axes of the slice: x: 4, y: 8 (y_hi: 4, y_lo: 2; y = y_hi * 2 + y_lo), z: 8, core: 2. Of those that a mesh axis runs over, the one named last changes fastest.
Arguments:
- queries: bfloat16 [16384, 64, 128], P('ctx', 'kv'), may hold values from -64 to 64
- keys: bfloat16 [16384, 8, 128], P('ctx', 'kv'), may hold values from -6.5 to 6.5
- values: bfloat16 [16384, 8, 128], P('ctx', 'kv'), may hold values from -6 to 6
- block_start: int32 [128], replicated, may hold values from 0 to 16256, as said below
- depth_k: float32 [32, 128], replicated, may hold values from -1 to 1
- point_k: float32 [128, 128], replicated, may hold values from -0.5 to 0.5
- depth_v: float32 [32, 128], replicated, may hold values from -1 to 1
- point_v: float32 [128, 128], replicated, may hold values from -0.5 to 0.5
Outputs:
- attended: bfloat16 [16384, 8192], P(('ctx', 'kv'))
The draws below stay inside these ranges and needn't reach their ends.
Inputs may be any that keep to these rules, and one draw needn't show every extreme that they name: `block_start`: every entry is a multiple of 128; consecutive blocks of the array hold consecutive blocks of the document, the last block of the array followed by the first, starting at a drawn block, so the entries are 0 to 16256 each once.
All inputs are finite; a program needn't handle non-finite values.
Results may differ from the reference program's by a relative error of at most 0.014.
The reference program's roundings to bfloat16 on the way count: a program that leaves them out, or rounds other values in their place, can miss the bound.
Values may be sent and summed in bfloat16 or wider, within the bound.
No kernel may reach another device: no remote copies, remote signals or barrier semaphores. Data moves between devices by JAX's collectives and lax.ppermute only.
A program may use at most 64 MiB of HBM per device.

```python
import math
import jax
import jax.numpy as jnp
from jax import lax

HD = 128
QHEADS = 64
KVH = 8
TOK_DEV = 128
STRIDE = 32
BLOCKS = 128
SEQ = 16384
WIN_BLOCKS = 8


def joint_base(key):
    base_k = jnp.clip(jax.random.normal(jax.random.fold_in(key, 11), (SEQ, KVH, HD), jnp.float32), -4.5, 4.5)
    base_q = 1.5 * jnp.clip(jax.random.normal(jax.random.fold_in(key, 12), (SEQ, QHEADS, HD), jnp.float32), -4.0, 4.0)
    return (base_q, base_k)


def draw_keys(key, part):
    base_q, base_k = joint_base(key)
    return base_k.astype(jnp.bfloat16)


def draw_queries(key, part):
    base_q, base_k = joint_base(key)
    return base_q.astype(jnp.bfloat16)


def draw_block_start(key, part):
    turn = jax.random.randint(jax.random.fold_in(key, 21), (), 0, BLOCKS, dtype=jnp.int32)
    return ((jnp.arange(BLOCKS, dtype=jnp.int32) + turn) % BLOCKS * TOK_DEV).astype(jnp.int32)


def levels(rng, extent, cuts, smallest, high):
    def one(position, parts):
        draws = jax.random.uniform(jax.random.fold_in(jax.random.fold_in(rng, 6), position), (parts,), jnp.float32, smallest / len(cuts), high / len(cuts))
        return jnp.repeat(jnp.exp(draws), extent[position] // parts).reshape((-1,) + (1,) * (len(extent) - position - 1))

    loudness = one(*cuts[0])
    for cut in cuts[1:]:
        loudness = loudness * one(*cut)
    return loudness


def normal_values(stream_key, extent, scale, reach, pieces=(), kind=jnp.bfloat16):
    level = levels(stream_key, extent, pieces, -0.22, 0.18) if pieces else 1.0
    drawn = jax.random.normal(stream_key, extent, jnp.float32) * scale * level
    return jnp.minimum(jnp.maximum(drawn, -reach), reach).astype(kind)


def setup_inputs(seed: int = 0) -> dict:
    streams_of = jax.random.split(jax.random.key(seed), 9)
    return {
        "queries": draw_queries(jax.random.fold_in(streams_of[8], 71), 0),
        "keys": draw_keys(jax.random.fold_in(streams_of[8], 71), 0),
        "values": normal_values(streams_of[2], (SEQ, KVH, HD), 1.0, 6.0, ((0, 128), (1, 4))),
        "block_start": draw_block_start(jax.random.fold_in(streams_of[8], 71), 0),
        "depth_k": normal_values(streams_of[4], (STRIDE, HD), STRIDE ** -0.5, 1.0, (), jnp.float32),
        "point_k": normal_values(streams_of[5], (HD, HD), HD ** -0.5, 0.5, (), jnp.float32),
        "depth_v": normal_values(streams_of[6], (STRIDE, HD), STRIDE ** -0.5, 1.0, (), jnp.float32),
        "point_v": normal_values(streams_of[7], (HD, HD), HD ** -0.5, 0.5, (), jnp.float32),
    }


rope_base = 500000.0
orig_context = 8192.0
yarn_factor = 16.0
beta_fast = 32.0
beta_slow = 1.0
neg_large = -1e+30

def yarn_table(width):
    index = jnp.arange(width // 2, dtype=jnp.float32)
    inverse = jnp.exp(-(2.0 * index / width) * math.log(rope_base))
    ratio = orig_context * inverse / (2.0 * math.pi)
    ramp = jnp.clip((ratio - beta_slow) / (beta_fast - beta_slow), 0.0, 1.0)
    return inverse * (ramp + (1.0 - ramp) / yarn_factor)

def rotary(field, places, freqs):
    angle = places.astype(jnp.float32)[:, None] * freqs[None, :]
    cosine = jnp.cos(angle)[:, None, :]
    sine = jnp.sin(angle)[:, None, :]
    half = field.shape[-1] // 2
    data = field.astype(jnp.float32)
    first = data[..., :half]
    second = data[..., half:]
    mscale = 1.0 + 0.1 * math.log(yarn_factor)
    turned = jnp.concatenate([first * cosine - second * sine, second * cosine + first * sine], axis=-1) * mscale
    return lax.optimization_barrier(turned.astype(jnp.bfloat16))

def compress(field, depth, point):
    rows, heads, width = field.shape
    stride = depth.shape[0]
    grouped = field.astype(jnp.float32).reshape(rows // stride, stride, heads, width)
    pooled = lax.optimization_barrier(jnp.sum(grouped * depth[None, :, None, :], axis=1))
    mixed = jnp.dot(pooled.reshape(-1, width), point, precision=lax.Precision.HIGHEST, preferred_element_type=jnp.float32)
    return lax.optimization_barrier(mixed.reshape(rows // stride, heads, width).astype(jnp.bfloat16))

def reference(queries, keys, values, block_start, depth_k, point_k, depth_v, point_v):
    rows = jnp.arange(SEQ, dtype=jnp.int32)
    places = (block_start[rows // TOK_DEV] + rows % TOK_DEV).astype(jnp.int32)
    freqs = yarn_table(HD)
    rot_q = rotary(queries, places, freqs)
    rot_k = rotary(keys, places, freqs)
    mem_k = compress(rot_k, depth_k, point_k)
    mem_v = compress(values, depth_v, point_v)
    slot_end = places[::STRIDE] + STRIDE
    window = WIN_BLOCKS * TOK_DEV
    group = QHEADS // KVH
    scale = 1.0 / math.sqrt(HD)

    def one_block(block):
        first_row = (block * TOK_DEV).astype(jnp.int32)
        q_rows = lax.dynamic_slice_in_dim(rot_q, first_row, TOK_DEV, 0).astype(jnp.float32).reshape(TOK_DEV, KVH, group, HD)
        q_places = lax.dynamic_slice_in_dim(places, first_row, TOK_DEV, 0)
        key_list = []
        value_list = []
        place_list = []
        for back in range(WIN_BLOCKS + 1):
            source = ((block - back) % BLOCKS * TOK_DEV).astype(jnp.int32)
            key_list.append(lax.dynamic_slice_in_dim(rot_k, source, TOK_DEV, 0))
            value_list.append(lax.dynamic_slice_in_dim(values, source, TOK_DEV, 0))
            place_list.append(lax.dynamic_slice_in_dim(places, source, TOK_DEV, 0))
        all_keys = jnp.concatenate(key_list + [mem_k], axis=0).astype(jnp.float32)
        all_values = jnp.concatenate(value_list + [mem_v], axis=0).astype(jnp.float32)
        raw_places = jnp.concatenate(place_list, axis=0)
        raw_ok = (raw_places[None, :] <= q_places[:, None]) & (raw_places[None, :] > q_places[:, None] - window)
        mem_ok = slot_end[None, :] <= q_places[:, None] + 1
        valid = jnp.concatenate([raw_ok, mem_ok], axis=1)[:, None, None, :]
        scores = jnp.einsum('tgqd,sgd->tgqs', q_rows, all_keys) * scale
        masked = jnp.where(valid, scores, neg_large)
        highest = lax.optimization_barrier(jnp.max(masked, axis=-1, keepdims=True))
        weight = jnp.where(valid, jnp.exp(masked - highest), 0.0)
        total = lax.optimization_barrier(jnp.sum(weight, axis=-1))
        rounded = lax.optimization_barrier(weight.astype(jnp.bfloat16)).astype(jnp.float32)
        mixed = jnp.einsum('tgqs,sgd->tgqd', rounded, all_values)
        return (mixed / total[..., None]).astype(jnp.bfloat16).reshape(TOK_DEV, QHEADS * HD)
    outputs = lax.map(one_block, jnp.arange(BLOCKS, dtype=jnp.int32))
    return outputs.reshape(SEQ, QHEADS * HD)
```

```python
import math

import jax
import jax.numpy as jnp
import numpy as np
from jax import lax
from jax.experimental import pallas as pl
from jax.experimental.pallas import tpu as pltpu
from jax.sharding import PartitionSpec as P

HD = 128
TOK = 128
STRIDE = 32
SLOTS = TOK // STRIDE
WIN = 8
WINDOW = WIN * TOK
BLOCKS = 128
SEQ = BLOCKS * TOK
HEADS = 16
GROUPS = 2
KV = 4
MSCALE = 1.0 + 0.1 * math.log(16.0)
SCALE2 = math.log2(math.e) / math.sqrt(HD)
NEG = -1e30
BF = jnp.bfloat16
F32 = jnp.float32


def yarn_freqs():
    index = np.arange(HD // 2, dtype=np.float32)
    inverse = np.exp(np.float32(-(2.0 / HD) * math.log(500000.0)) * index).astype(np.float32)
    ratio = np.float32(8192.0) * inverse / np.float32(2.0 * math.pi)
    ramp = np.clip((ratio - 1.0) / 31.0, 0.0, 1.0).astype(np.float32)
    freqs = inverse * (ramp + (1.0 - ramp) / np.float32(16.0))
    return np.tile(np.concatenate([freqs, freqs])[None, :], (8, 1)).astype(np.float32)


def turn_tables(place0, freqs):
    places = (place0 + lax.broadcasted_iota(jnp.int32, (TOK, HD), 0)).astype(F32)
    angle = places * freqs
    first = lax.broadcasted_iota(jnp.int32, (TOK, HD), 1) < HD // 2
    sine = jnp.sin(angle)
    return jnp.cos(angle), jnp.where(first, -sine, sine)


def turn(x, cosine, sine):
    return ((x * cosine + pltpu.roll(x, HD // 2, 1) * sine) * MSCALE).astype(BF)


def prep_kernel(bs, freqs, k, v, dk, pk, dv, pv, own, mem, scr, pool):
    me = lax.axis_index("ctx")
    cosine, sine = turn_tables(bs[me], freqs[0:1, :])
    scr[...] = k[...].astype(F32)
    for g in range(GROUPS):
        rot = turn(scr[:, g, :], cosine, sine)
        own[g * TOK : (g + 1) * TOK, :] = rot
        grouped = rot.astype(F32).reshape(SLOTS, STRIDE, HD)
        pool[g * SLOTS : (g + 1) * SLOTS, :] = jnp.sum(grouped * dk[...][None], axis=1)
    scr[...] = v[...].astype(F32)
    for g in range(GROUPS):
        val = scr[:, g, :]
        own[(GROUPS + g) * TOK : (GROUPS + g + 1) * TOK, :] = val.astype(BF)
        grouped = val.reshape(SLOTS, STRIDE, HD)
        at = (GROUPS + g) * SLOTS
        pool[at : at + SLOTS, :] = jnp.sum(grouped * dv[...][None], axis=1)
    half = GROUPS * SLOTS
    mk = jnp.dot(pool[:half, :], pk[...], precision=lax.Precision.HIGHEST, preferred_element_type=F32)
    mv = jnp.dot(pool[half:, :], pv[...], precision=lax.Precision.HIGHEST, preferred_element_type=F32)
    both = jnp.concatenate([mk, mv], axis=0).astype(BF)
    mem[...] = jnp.broadcast_to(both[None], mem.shape)


def query_kernel(bs, freqs, q, rotq, scr):
    me = lax.axis_index("ctx")
    cosine, sine = turn_tables(bs[me], freqs[0:1, :])
    scr[...] = q[...].astype(F32)
    for h in range(HEADS):
        rotq[h * TOK : (h + 1) * TOK, :] = turn(scr[:, h, :], cosine, sine)


def octet_kernel(own, prev, out):
    me = lax.rem(lax.axis_index("ctx"), 8)
    for d in range(8):

        @pl.when(me <= d)
        def _():
            out[d] = own[...]

        @pl.when(me > d)
        def _():
            out[d] = prev[...]


def unit_rows(rows):
    r = lax.broadcasted_iota(jnp.int32, (rows, TOK), 0) & (TOK - 1)
    c = lax.broadcasted_iota(jnp.int32, (rows, TOK), 1)
    return jnp.where(r == c, 1.0, 0.0).astype(BF)


def attend(qa, keys, high):
    s = lax.dot_general(qa, keys, (((1,), (1,)), ((), ())), preferred_element_type=F32)
    top = jnp.max(s, axis=1, keepdims=True)
    if high is not None:
        top = jnp.maximum(top, high)
    return jnp.exp2((s - top) * SCALE2).astype(BF), top


ROWS = 256


def window_kernel(bs, rotq, recv, prev, acc, high, kaug, vaug):
    me = lax.axis_index("ctx")
    pos = lax.rem(me, 8)
    place = bs[me] + lax.broadcasted_iota(jnp.int32, (TOK, TOK), 1)
    row = lax.broadcasted_iota(jnp.int32, (TOK, TOK), 0)
    ones = jnp.ones((TOK, HD), BF)
    for b in range(WIN + 1):
        back = WIN if b == WIN else lax.rem(pos - b + 8, 8)
        there = bs[lax.rem(me - back + BLOCKS, BLOCKS)] + row
        ok = (there <= place) & (there > place - WINDOW)
        bias = jnp.where(ok, 0.0, NEG).astype(BF)
        span = slice(b * TOK, (b + 1) * TOK)
        for g in range(GROUPS):
            ks = slice(g * TOK, (g + 1) * TOK)
            vs = slice((GROUPS + g) * TOK, (GROUPS + g + 1) * TOK)
            kaug[g, span, :HD] = prev[ks, :] if b == WIN else recv[b, ks, :]
            kaug[g, span, HD:] = bias
            vaug[g, span, :HD] = prev[vs, :] if b == WIN else recv[b, vs, :]
            vaug[g, span, HD:] = ones
    unit = unit_rows(ROWS)
    for c in range(HEADS * TOK // ROWS):
        at = slice(c * ROWS, (c + 1) * ROWS)
        g = c * ROWS // (HEADS // GROUPS * TOK)
        qa = jnp.concatenate([rotq[at, :], unit], axis=1)
        w, top = attend(qa, kaug[g], None)
        acc[at, :] = jnp.dot(w, vaug[g], preferred_element_type=F32)
        high[at, :] = jnp.broadcast_to(top, (ROWS, HD))


def memory_kernel(bs, rotq, mem, acc, high, out, scr, kaug, vaug):
    me = lax.axis_index("ctx")
    place = bs[me] + lax.broadcasted_iota(jnp.int32, (BLOCKS, TOK), 1)
    start = (bs[0] + TOK * lax.broadcasted_iota(jnp.int32, (BLOCKS, TOK), 0)) & (SEQ - 1)
    scr[...] = mem[...].astype(F32)
    ones = jnp.ones((BLOCKS, HD), BF)
    for j in range(SLOTS):
        ok = start + (j + 1) * STRIDE <= place + 1
        bias = jnp.where(ok, 0.0, NEG).astype(BF)
        span = slice(j * BLOCKS, (j + 1) * BLOCKS)
        for g in range(GROUPS):
            kaug[g, span, :HD] = scr[:, g * SLOTS + j, :].astype(BF)
            kaug[g, span, HD:] = bias
            vaug[g, span, :HD] = scr[:, (GROUPS + g) * SLOTS + j, :].astype(BF)
            vaug[g, span, HD:] = ones
    unit = unit_rows(ROWS)
    rows = TOK // KV
    for c in range(HEADS * TOK // ROWS):
        at = slice(c * ROWS, (c + 1) * ROWS)
        g = c * ROWS // (HEADS // GROUPS * TOK)
        qa = jnp.concatenate([rotq[at, :], unit], axis=1)
        before = high[at, :]
        w, top = attend(qa, kaug[g], before[:, :1])
        keep = jnp.exp2((before - top) * SCALE2)
        new = jnp.dot(w, vaug[g], preferred_element_type=F32)
        old = acc[at, :]
        mixed = old[:, :HD] * keep + new[:, :HD]
        total = old[:, HD:] * keep + new[:, HD:]
        res = (mixed / total).astype(BF)
        for i in range(ROWS // TOK):
            h = c * (ROWS // TOK) + i
            for d in range(KV):
                lo = i * TOK + d * rows
                out[d, :, h * HD : (h + 1) * HD] = res[lo : lo + rows, :]


def call(kernel, out_shape, scratch, flops, *args):
    specs = [
        pl.BlockSpec(memory_space=pltpu.SMEM if i == 0 else pltpu.VMEM) for i in range(len(args))
    ]
    if kernel is octet_kernel:
        specs[0] = pl.BlockSpec(memory_space=pltpu.VMEM)
    multi = isinstance(out_shape, tuple)
    vm = pl.BlockSpec(memory_space=pltpu.VMEM)
    return pl.pallas_call(
        kernel,
        out_shape=out_shape,
        in_specs=specs,
        out_specs=(vm,) * len(out_shape) if multi else vm,
        scratch_shapes=scratch,
        compiler_params=pltpu.CompilerParams(vmem_limit_bytes=32 * 2**20),
        cost_estimate=pl.CostEstimate(flops=flops, bytes_accessed=2**20, transcendentals=0),
    )(*args)


def shape(*dims, dtype=BF):
    return jax.ShapeDtypeStruct(dims, dtype)


octets = [[8 * o + p for p in range(8)] for o in range(BLOCKS // 8)]


def shards(queries, keys, values, block_start, depth_k, point_k, depth_v, point_v):
    freqs = jnp.asarray(yarn_freqs())
    pack = 2 * GROUPS
    own, mem = call(
        prep_kernel,
        (shape(pack * TOK, HD), shape(BLOCKS, pack * SLOTS, HD)),
        [pltpu.VMEM((TOK, GROUPS, HD), F32), pltpu.VMEM((pack * SLOTS, HD), F32)],
        10**9,
        block_start, freqs, keys, values, depth_k, point_k, depth_v, point_v,
    )
    prev = lax.ppermute(own, "ctx", [((i - WIN) % BLOCKS, i) for i in range(BLOCKS)])
    mem = lax.all_to_all(mem, "ctx", 0, 0)
    rotq = call(
        query_kernel, shape(HEADS * TOK, HD), [pltpu.VMEM((TOK, HEADS, HD), F32)], 10**9,
        block_start, freqs, queries,
    )
    sent = call(octet_kernel, shape(8, pack * TOK, HD), [], 10**8, own, prev)
    recv = lax.all_to_all(sent, "ctx", 0, 0, axis_index_groups=octets)
    raw = (WIN + 1) * TOK
    acc, high = call(
        window_kernel,
        (shape(HEADS * TOK, 2 * HD, dtype=F32), shape(HEADS * TOK, HD, dtype=F32)),
        [pltpu.VMEM((GROUPS, raw, 2 * HD), BF), pltpu.VMEM((GROUPS, raw, 2 * HD), BF)],
        10**10,
        block_start, rotq, recv, prev,
    )
    slots = BLOCKS * SLOTS
    out = call(
        memory_kernel,
        shape(KV, TOK // KV, HEADS * HD),
        [
            pltpu.VMEM((BLOCKS, pack * SLOTS, HD), F32),
            pltpu.VMEM((GROUPS, slots, 2 * HD), BF),
            pltpu.VMEM((GROUPS, slots, 2 * HD), BF),
        ],
        5 * 10**9,
        block_start, rotq, mem, acc, high,
    )
    got = lax.all_to_all(out, "kv", 0, 0)
    return got.transpose(1, 0, 2).reshape(TOK // KV, KV * HEADS * HD)


def solution(mesh):
    placed = (
        P("ctx", "kv", None),
        P("ctx", "kv", None),
        P("ctx", "kv", None),
        P(),
        P(),
        P(),
        P(),
        P(),
    )
    return jax.shard_map(
        shards, mesh=mesh, in_specs=placed, out_specs=P(("ctx", "kv"), None), check_vma=False
    )
```

```python
import functools
import math

import jax
import jax.numpy as jnp
import numpy as np
from jax import lax
from jax.experimental import pallas as pl
from jax.experimental.pallas import tpu as pltpu
from jax.sharding import PartitionSpec as P

HD = 128
TOK = 128
STRIDE = 32
SLOTS = TOK // STRIDE
WIN = 8
WINDOW = WIN * TOK
BLOCKS = 128
SEQ = BLOCKS * TOK
HEADS = 16
GROUPS = 2
KV = 4
OCT = 8
NOCT = BLOCKS // OCT
ROWS = TOK // KV
RAW = (WIN + 1) * TOK
MSCALE = 1.0 + 0.1 * math.log(16.0)
SCALE2 = math.log2(math.e) / math.sqrt(HD)
NEG = -1e30
BF = jnp.bfloat16
F32 = jnp.float32


def yarn_freqs():
    index = np.arange(HD // 2, dtype=np.float32)
    inverse = np.exp(np.float32(-(2.0 / HD) * math.log(500000.0)) * index).astype(np.float32)
    ratio = np.float32(8192.0) * inverse / np.float32(2.0 * math.pi)
    ramp = np.clip((ratio - 1.0) / 31.0, 0.0, 1.0).astype(np.float32)
    freqs = inverse * (ramp + (1.0 - ramp) / np.float32(16.0))
    return np.tile(np.concatenate([freqs, freqs])[None, :], (8, 1)).astype(np.float32)


def turn_tables(place0, freqs):
    places = (place0 + lax.broadcasted_iota(jnp.int32, (TOK, HD), 0)).astype(F32)
    angle = places * freqs
    first = lax.broadcasted_iota(jnp.int32, (TOK, HD), 1) < HD // 2
    sine = jnp.sin(angle)
    return jnp.cos(angle), jnp.where(first, -sine, sine)


def turn(x, cosine, sine):
    return ((x * cosine + pltpu.roll(x, HD // 2, 1) * sine) * MSCALE).astype(BF)


def prep_kernel(bs, freqs, k, v, dk, pk, dv, pv, own, mem, *scratch):
    scr, pool, s_bs, s_freqs, s_k, s_v, s_dk, s_pk, s_dv, s_pv, sem = scratch
    pairs = (
        (bs, s_bs), (freqs, s_freqs), (k, s_k), (v, s_v),
        (dk, s_dk), (pk, s_pk), (dv, s_dv), (pv, s_pv),
    )
    copies = [pltpu.make_async_copy(a, b, sem.at[i]) for i, (a, b) in enumerate(pairs)]
    for c in copies:
        c.start()
    for c in copies:
        c.wait()
    me = lax.axis_index("ctx")
    cosine, sine = turn_tables(s_bs[me], s_freqs[0:1, :])
    scr[...] = s_k[...].astype(F32)
    for g in range(GROUPS):
        rot = turn(scr[:, g, :], cosine, sine)
        own[g * TOK : (g + 1) * TOK, :] = rot
        grouped = rot.astype(F32).reshape(SLOTS, STRIDE, HD)
        pool[g * SLOTS : (g + 1) * SLOTS, :] = jnp.sum(grouped * s_dk[...][None], axis=1)
    scr[...] = s_v[...].astype(F32)
    for g in range(GROUPS):
        val = scr[:, g, :]
        own[(GROUPS + g) * TOK : (GROUPS + g + 1) * TOK, :] = val.astype(BF)
        grouped = val.reshape(SLOTS, STRIDE, HD)
        at = (GROUPS + g) * SLOTS
        pool[at : at + SLOTS, :] = jnp.sum(grouped * s_dv[...][None], axis=1)
    half = GROUPS * SLOTS
    mk = jnp.dot(pool[:half, :], s_pk[...], precision=lax.Precision.HIGHEST, preferred_element_type=F32)
    mv = jnp.dot(pool[half:, :], s_pv[...], precision=lax.Precision.HIGHEST, preferred_element_type=F32)
    both = jnp.concatenate([mk, mv], axis=0).astype(BF)
    mem[...] = jnp.broadcast_to(both[None], mem.shape)


def query_kernel(bs, freqs, q, rotq, scr):
    me = lax.axis_index("ctx")
    cosine, sine = turn_tables(bs[me], freqs[0:1, :])
    scr[...] = q[...].astype(F32)
    for h in range(HEADS):
        rotq[h] = turn(scr[:, h, :], cosine, sine)


def octet_kernel(own, prev, mem, out, scr):
    me = lax.rem(lax.axis_index("ctx"), OCT)
    scr[...] = mem[...].astype(F32)
    kinds = 2 * GROUPS * SLOTS
    slots = jnp.concatenate([scr[:, r, :] for r in range(kinds)], axis=0).astype(BF)
    raw = own.shape[0]
    for d in range(OCT):
        out[d, raw:, :] = slots

        @pl.when(me <= d)
        def _():
            out[d, :raw, :] = own[...]

        @pl.when(me > d)
        def _():
            out[d, :raw, :] = prev[...]


def build_kernel(bs, recv, prev, kaug, vaug):
    me = lax.axis_index("ctx")
    pos = lax.rem(me, OCT)
    place = bs[me] + lax.broadcasted_iota(jnp.int32, (TOK, TOK), 1)
    row = lax.broadcasted_iota(jnp.int32, (TOK, TOK), 0)
    ones = jnp.ones((TOK, HD), BF)
    for b in range(WIN + 1):
        back = WIN if b == WIN else lax.rem(pos - b + OCT, OCT)
        there = bs[lax.rem(me - back + BLOCKS, BLOCKS)] + row
        ok = (there <= place) & (there > place - WINDOW)
        bias = jnp.where(ok, 0.0, NEG).astype(BF)
        span = slice(b * TOK, (b + 1) * TOK)
        for g in range(GROUPS):
            ks = slice(g * TOK, (g + 1) * TOK)
            vs = slice((GROUPS + g) * TOK, (GROUPS + g + 1) * TOK)
            kaug[g, span, :HD] = prev[ks, :] if b == WIN else recv[b, ks, :]
            kaug[g, span, HD:] = bias
            vaug[g, span, :HD] = prev[vs, :] if b == WIN else recv[b, vs, :]
            vaug[g, span, HD:] = ones
    many = SLOTS * NOCT
    slot = lax.broadcasted_iota(jnp.int32, (many, TOK), 0) // NOCT
    octet = lax.broadcasted_iota(jnp.int32, (many, TOK), 0) & (NOCT - 1)
    place = bs[me] + lax.broadcasted_iota(jnp.int32, (many, TOK), 1)
    for p in range(OCT):
        end = ((bs[p] + OCT * TOK * octet) & (SEQ - 1)) + (slot + 1) * STRIDE
        bias = jnp.where(end <= place + 1, 0.0, NEG).astype(BF)
        lo = RAW + p * many
        span = slice(lo, lo + many)
        for g in range(GROUPS):
            at = 2 * GROUPS * TOK + g * many
            kaug[g, span, :HD] = recv[p, at : at + many, :]
            kaug[g, span, HD:] = bias
            at += GROUPS * many
            vaug[g, span, :HD] = recv[p, at : at + many, :]
            vaug[g, span, HD:] = ones[:many, :]


def chunk_kernel(off, rotq, kaug, vaug, *rest):
    out = rest[-1]
    dest = lax.axis_index("kv") ^ off
    first = pl.multiple_of(dest * ROWS, ROWS)
    heads = HEADS // GROUPS
    r = lax.broadcasted_iota(jnp.int32, (heads * ROWS, TOK), 0) & (ROWS - 1)
    c = lax.broadcasted_iota(jnp.int32, (heads * ROWS, TOK), 1)
    unit = jnp.where(r + first == c, 1.0, 0.0).astype(BF)
    for g in range(GROUPS):
        q = jnp.concatenate(
            [rotq[g * heads + i, pl.ds(first, ROWS), :] for i in range(heads)], axis=0
        )
        qa = jnp.concatenate([q, unit], axis=1)
        s = lax.dot_general(qa, kaug[g], (((1,), (1,)), ((), ())), preferred_element_type=F32)
        top = jnp.max(s, axis=1, keepdims=True)
        w = jnp.exp2((s - top) * SCALE2).astype(BF)
        mixed = jnp.dot(w, vaug[g], preferred_element_type=F32)
        res = (mixed[:, :HD] / mixed[:, HD:]).astype(BF)
        for i in range(heads):
            h = g * heads + i
            out[:, h * HD : (h + 1) * HD] = res[i * ROWS : (i + 1) * ROWS, :]


def join_kernel(a, b, c, d, out, sem):
    me = lax.axis_index("kv")
    wide = HEADS * HD
    copies = []
    for off, part in enumerate((a, b, c, d)):
        lane = pl.multiple_of((me ^ off) * wide, wide)
        copies.append(pltpu.make_async_copy(part, out.at[:, pl.ds(lane, wide)], sem.at[off]))
    for x in copies:
        x.start()
    for x in copies:
        x.wait()


def call(kernel, out_shape, scratch, flops, spaces, *args, out_space=pltpu.VMEM, grant=32):
    multi = isinstance(out_shape, tuple)
    vm = pl.BlockSpec(memory_space=out_space)
    return pl.pallas_call(
        kernel,
        out_shape=out_shape,
        in_specs=[pl.BlockSpec(memory_space=s) for s in spaces],
        out_specs=(vm,) * len(out_shape) if multi else vm,
        scratch_shapes=scratch,
        compiler_params=pltpu.CompilerParams(vmem_limit_bytes=grant * 2**20),
        cost_estimate=pl.CostEstimate(flops=flops, bytes_accessed=2**10, transcendentals=0),
    )(*args)


def shape(*dims, dtype=BF):
    return jax.ShapeDtypeStruct(dims, dtype)


octets = [[OCT * o + p for p in range(OCT)] for o in range(NOCT)]
strided = [[OCT * o + p for o in range(NOCT)] for p in range(OCT)]
SM, VM, HB = pltpu.SMEM, pltpu.VMEM, pltpu.HBM


def shards(queries, keys, values, block_start, depth_k, point_k, depth_v, point_v):
    freqs = jnp.asarray(yarn_freqs())
    pack = 2 * GROUPS
    params = (block_start, freqs, keys, values, depth_k, point_k, depth_v, point_v)
    own, mem = call(
        prep_kernel,
        (shape(pack * TOK, HD), shape(NOCT, pack * SLOTS, HD)),
        [pltpu.VMEM((TOK, GROUPS, HD), F32), pltpu.VMEM((pack * SLOTS, HD), F32)]
        + [(pltpu.SMEM if i == 0 else pltpu.VMEM)(x.shape, x.dtype) for i, x in enumerate(params)]
        + [pltpu.SemaphoreType.DMA((len(params),))],
        10**9,
        (HB,) * len(params),
        *params,
        grant=60,
    )
    prev = lax.ppermute(own, "ctx", [((i - WIN) % BLOCKS, i) for i in range(BLOCKS)])
    mem = lax.all_to_all(mem, "ctx", 0, 0, axis_index_groups=strided)
    rotq = call(
        query_kernel, shape(HEADS, TOK, HD), [pltpu.VMEM((TOK, HEADS, HD), F32)], 10**9,
        (SM, VM, VM),
        block_start, freqs, queries,
    )
    rows = pack * TOK + pack * SLOTS * NOCT
    sent = call(
        octet_kernel, shape(OCT, rows, HD), [pltpu.VMEM((NOCT, pack * SLOTS, HD), F32)], 10**8,
        (VM,) * 3, own, prev, mem,
    )
    recv = lax.all_to_all(sent, "ctx", 0, 0, axis_index_groups=octets)
    wide = shape(GROUPS, RAW + BLOCKS * SLOTS, 2 * HD)
    kaug, vaug = call(build_kernel, (wide, wide), [], 10**9, (SM, VM, VM), block_start, recv, prev)
    parts = []
    for off in (3, 2, 1, 0):
        after = parts[-2:-1]
        part = call(
            functools.partial(chunk_kernel, off), shape(ROWS, HEADS * HD), [], 10**6,
            (VM,) * 3 + (pl.ANY,) * len(after), rotq, kaug, vaug, *after,
        )
        if off:
            part = lax.ppermute(part, "kv", [(i, i ^ off) for i in range(KV)])
        parts.append(part)
    return call(
        join_kernel, shape(ROWS, KV * HEADS * HD), [pltpu.SemaphoreType.DMA((KV,))], 10**8,
        (VM,) * 4, *parts[::-1], out_space=HB,
    )


def solution(mesh):
    placed = (
        P("ctx", "kv", None),
        P("ctx", "kv", None),
        P("ctx", "kv", None),
        P(),
        P(),
        P(),
        P(),
        P(),
    )
    return jax.shard_map(
        shards, mesh=mesh, in_specs=placed, out_specs=P(("ctx", "kv"), None), check_vma=False
    )
```

```python
import functools
import math

import jax
import jax.numpy as jnp
import numpy as np
from jax import lax
from jax.experimental import pallas as pl
from jax.experimental.pallas import tpu as pltpu
from jax.sharding import PartitionSpec as P

HD = 128
TOK = 128
STRIDE = 32
SLOTS = TOK // STRIDE
WIN = 8
WINDOW = WIN * TOK
BLOCKS = 128
SEQ = BLOCKS * TOK
HEADS = 16
GROUPS = 2
KV = 4
OCT = 8
NOCT = BLOCKS // OCT
ROWS = TOK // KV
RAW = (WIN + 1) * TOK
MANY = SLOTS * NOCT
KEYS = RAW + BLOCKS * SLOTS
TILE = 256
MSCALE = 1.0 + 0.1 * math.log(16.0)
SCALE2 = math.log2(math.e) / math.sqrt(HD)
NEG = -1e30
BF = jnp.bfloat16
F32 = jnp.float32


def yarn_freqs():
    index = np.arange(HD // 2, dtype=np.float32)
    inverse = np.exp(np.float32(-(2.0 / HD) * math.log(500000.0)) * index).astype(np.float32)
    ratio = np.float32(8192.0) * inverse / np.float32(2.0 * math.pi)
    ramp = np.clip((ratio - 1.0) / 31.0, 0.0, 1.0).astype(np.float32)
    freqs = inverse * (ramp + (1.0 - ramp) / np.float32(16.0))
    return np.tile(np.concatenate([freqs, freqs])[None, :], (8, 1)).astype(np.float32)


def turn_tables(place0, freqs):
    places = (place0 + lax.broadcasted_iota(jnp.int32, (TOK, HD), 0)).astype(F32)
    angle = places * freqs
    first = lax.broadcasted_iota(jnp.int32, (TOK, HD), 1) < HD // 2
    sine = jnp.sin(angle)
    return jnp.cos(angle), jnp.where(first, -sine, sine)


def turn(x, cosine, sine):
    return ((x * cosine + pltpu.roll(x, HD // 2, 1) * sine) * MSCALE).astype(BF)


def prep_kernel(bs, freqs, k, v, dk, pk, dv, pv, own, mem, *scratch):
    scr, pool, s_bs, s_freqs, s_k, s_v, s_dk, s_pk, s_dv, s_pv, sem = scratch
    pairs = (
        (bs, s_bs), (freqs, s_freqs), (k, s_k), (v, s_v),
        (dk, s_dk), (pk, s_pk), (dv, s_dv), (pv, s_pv),
    )
    copies = [pltpu.make_async_copy(a, b, sem.at[i]) for i, (a, b) in enumerate(pairs)]
    for c in copies:
        c.start()
    for c in copies:
        c.wait()
    me = lax.axis_index("ctx")
    cosine, sine = turn_tables(s_bs[me], s_freqs[0:1, :])
    scr[...] = s_k[...].astype(F32)
    for g in range(GROUPS):
        rot = turn(scr[:, g, :], cosine, sine)
        own[g * TOK : (g + 1) * TOK, :] = rot
        grouped = rot.astype(F32).reshape(SLOTS, STRIDE, HD)
        pool[g * SLOTS : (g + 1) * SLOTS, :] = jnp.sum(grouped * s_dk[...][None], axis=1)
    scr[...] = s_v[...].astype(F32)
    for g in range(GROUPS):
        val = scr[:, g, :]
        own[(GROUPS + g) * TOK : (GROUPS + g + 1) * TOK, :] = val.astype(BF)
        grouped = val.reshape(SLOTS, STRIDE, HD)
        at = (GROUPS + g) * SLOTS
        pool[at : at + SLOTS, :] = jnp.sum(grouped * s_dv[...][None], axis=1)
    half = GROUPS * SLOTS
    mk = jnp.dot(pool[:half, :], s_pk[...], precision=lax.Precision.HIGHEST, preferred_element_type=F32)
    mv = jnp.dot(pool[half:, :], s_pv[...], precision=lax.Precision.HIGHEST, preferred_element_type=F32)
    both = jnp.concatenate([mk, mv], axis=0).astype(BF)
    mem[...] = jnp.broadcast_to(both[None], mem.shape)


def query_kernel(bs, freqs, q, rotq, scr):
    me = lax.axis_index("ctx")
    cosine, sine = turn_tables(bs[me], freqs[0:1, :])
    scr[...] = q[...].astype(F32)
    for h in range(HEADS):
        rotq[h] = turn(scr[:, h, :], cosine, sine)


def raw_kernel(own, prev, rotq, bias, out):
    me = lax.rem(lax.axis_index("ctx"), OCT)
    raw = own.shape[0]
    for d in range(OCT):

        @pl.when(me <= d)
        def _():
            out[d, :raw, :] = own[...]

        @pl.when(me > d)
        def _():
            out[d, :raw, :] = prev[...]


def slot_kernel(mem, sent, out, scr):
    scr[...] = mem[...].astype(F32)
    kinds = 2 * GROUPS * SLOTS
    slots = jnp.concatenate([scr[:, r, :] for r in range(kinds)], axis=0).astype(BF)
    raw = 2 * GROUPS * TOK
    for d in range(OCT):
        out[d, raw:, :] = slots


def bias_kernel(bs, bias):
    me = lax.axis_index("ctx")
    pos = lax.rem(me, OCT)
    place = bs[me] + lax.broadcasted_iota(jnp.int32, (TOK, TOK), 1)
    row = lax.broadcasted_iota(jnp.int32, (TOK, TOK), 0)
    for b in range(WIN + 1):
        back = WIN if b == WIN else lax.rem(pos - b + OCT, OCT)
        there = bs[lax.rem(me - back + BLOCKS, BLOCKS)] + row
        ok = (there <= place) & (there > place - WINDOW)
        bias[b * TOK : (b + 1) * TOK, :] = jnp.where(ok, 0.0, NEG).astype(BF)
    slot = lax.broadcasted_iota(jnp.int32, (MANY, TOK), 0) // NOCT
    octet = lax.broadcasted_iota(jnp.int32, (MANY, TOK), 0) & (NOCT - 1)
    place = bs[me] + lax.broadcasted_iota(jnp.int32, (MANY, TOK), 1)
    for p in range(OCT):
        end = ((bs[p] + OCT * TOK * octet) & (SEQ - 1)) + (slot + 1) * STRIDE
        lo = RAW + p * MANY
        bias[lo : lo + MANY, :] = jnp.where(end <= place + 1, 0.0, NEG).astype(BF)


def key_tiles():
    raw = [("r", b) for b in range(OCT)] + [("p", 0)]
    rows = [(x, TOK) for x in raw] + [(("m", p), MANY) for p in range(OCT)]
    tiles, tile, size, lo, start = [], [], 0, 0, 0
    for x, n in rows:
        tile.append(x)
        size += n
        if size == TILE or x == ("m", OCT - 1):
            tiles.append((lo, size, tile))
            lo, size, tile = lo + size, 0, []
    return tiles


def gather_tile(recv, prev, tile, raw_at, slot_at):
    parts = []
    for kind, i in tile:
        if kind == "r":
            parts.append(recv[i, raw_at : raw_at + TOK, :])
        elif kind == "p":
            parts.append(prev[raw_at : raw_at + TOK, :])
        else:
            parts.append(recv[i, slot_at : slot_at + MANY, :])
    return jnp.concatenate(parts, axis=0)


def chunk_kernel(off, rotq, bias, recv, prev, *rest):
    out, s = rest[-2:]
    dest = lax.axis_index("kv") ^ off
    first = pl.multiple_of(dest * ROWS, ROWS)
    heads = HEADS // GROUPS
    r = lax.broadcasted_iota(jnp.int32, (heads * ROWS, TOK), 0) & (ROWS - 1)
    c = lax.broadcasted_iota(jnp.int32, (heads * ROWS, TOK), 1)
    unit = jnp.where(r + first == c, 1.0, 0.0).astype(BF)
    slots = 2 * GROUPS * TOK
    for g in range(GROUPS):
        q = jnp.concatenate(
            [rotq[g * heads + i, pl.ds(first, ROWS), :] for i in range(heads)], axis=0
        )
        qa = jnp.concatenate([q, unit], axis=1)
        high = None
        for lo, size, tile in key_tiles():
            k = gather_tile(recv, prev, tile, g * TOK, slots + g * MANY)
            ka = jnp.concatenate([k, bias[lo : lo + size, :]], axis=1)
            x = lax.dot_general(qa, ka, (((1,), (1,)), ((), ())), preferred_element_type=F32)
            s[g, :, lo : lo + size] = x
            for i in range(size // HD):
                part = x[:, i * HD : (i + 1) * HD]
                high = part if high is None else jnp.maximum(high, part)
        top = jnp.max(high, axis=1, keepdims=True)
        mixed = None
        for lo, size, tile in key_tiles():
            w = jnp.exp2((s[g, :, lo : lo + size] - top) * SCALE2).astype(BF)
            v = gather_tile(recv, prev, tile, (GROUPS + g) * TOK, slots + (GROUPS + g) * MANY)
            va = jnp.concatenate([v, jnp.ones((size, HD), BF)], axis=1)
            part = jnp.dot(w, va, preferred_element_type=F32)
            mixed = part if mixed is None else mixed + part
        res = (mixed[:, :HD] / mixed[:, HD:]).astype(BF)
        for i in range(heads):
            h = g * heads + i
            out[:, h * HD : (h + 1) * HD] = res[i * ROWS : (i + 1) * ROWS, :]


def join_kernel(a, b, c, d, out, sem):
    me = lax.axis_index("kv")
    wide = HEADS * HD
    copies = []
    for off, part in enumerate((a, b, c, d)):
        lane = pl.multiple_of((me ^ off) * wide, wide)
        copies.append(pltpu.make_async_copy(part, out.at[:, pl.ds(lane, wide)], sem.at[off]))
    for x in copies:
        x.start()
    for x in copies:
        x.wait()


def call(kernel, out_shape, scratch, flops, spaces, *args, out_space=pltpu.VMEM, grant=32, alias=None):
    multi = isinstance(out_shape, tuple)
    vm = pl.BlockSpec(memory_space=out_space)
    return pl.pallas_call(
        kernel,
        out_shape=out_shape,
        in_specs=[pl.BlockSpec(memory_space=s) for s in spaces],
        out_specs=(vm,) * len(out_shape) if multi else vm,
        scratch_shapes=scratch,
        input_output_aliases=alias or {},
        compiler_params=pltpu.CompilerParams(vmem_limit_bytes=grant * 2**20),
        cost_estimate=pl.CostEstimate(flops=flops, bytes_accessed=2**10, transcendentals=0),
    )(*args)


def shape(*dims, dtype=BF):
    return jax.ShapeDtypeStruct(dims, dtype)


octets = [[OCT * o + p for p in range(OCT)] for o in range(NOCT)]
strided = [[OCT * o + p for o in range(NOCT)] for p in range(OCT)]
SM, VM, HB = pltpu.SMEM, pltpu.VMEM, pltpu.HBM


def shards(queries, keys, values, block_start, depth_k, point_k, depth_v, point_v):
    freqs = jnp.asarray(yarn_freqs())
    pack = 2 * GROUPS
    params = (block_start, freqs, keys, values, depth_k, point_k, depth_v, point_v)
    own, mem = call(
        prep_kernel,
        (shape(pack * TOK, HD), shape(NOCT, pack * SLOTS, HD)),
        [pltpu.VMEM((TOK, GROUPS, HD), F32), pltpu.VMEM((pack * SLOTS, HD), F32)]
        + [(pltpu.SMEM if i == 0 else pltpu.VMEM)(x.shape, x.dtype) for i, x in enumerate(params)]
        + [pltpu.SemaphoreType.DMA((len(params),))],
        10**9,
        (HB,) * len(params),
        *params,
        grant=60,
    )
    prev = lax.ppermute(own, "ctx", [((i - WIN) % BLOCKS, i) for i in range(BLOCKS)])
    mem = lax.all_to_all(mem, "ctx", 0, 0, axis_index_groups=strided)
    rotq = call(
        query_kernel, shape(HEADS, TOK, HD), [pltpu.VMEM((TOK, HEADS, HD), F32)], 10**9,
        (SM, VM, VM),
        block_start, freqs, queries,
    )
    bias = call(bias_kernel, shape(KEYS, TOK), [], 10**8, (SM,), block_start)
    rows = pack * TOK + pack * MANY
    sent = call(
        raw_kernel, shape(OCT, rows, HD), [], 10**8, (VM, VM, pl.ANY, pl.ANY), own, prev, rotq, bias
    )
    sent = call(
        slot_kernel, shape(OCT, rows, HD), [pltpu.VMEM((NOCT, pack * SLOTS, HD), F32)], 10**8,
        (VM, VM), mem, sent, alias={1: 0},
    )
    recv = lax.all_to_all(sent, "ctx", 0, 0, axis_index_groups=octets)
    parts = []
    for off in (3, 2, 1, 0):
        after = parts[-2:-1]
        part = call(
            functools.partial(chunk_kernel, off), shape(ROWS, HEADS * HD),
            [pltpu.VMEM((GROUPS, HEADS // GROUPS * ROWS, KEYS), F32)], 10**6,
            (VM,) * 4 + (pl.ANY,) * len(after), rotq, bias, recv, prev, *after,
        )
        if off:
            part = lax.ppermute(part, "kv", [(i, i ^ off) for i in range(KV)])
        parts.append(part)
    return call(
        join_kernel, shape(ROWS, KV * HEADS * HD), [pltpu.SemaphoreType.DMA((KV,))], 10**8,
        (VM,) * 4, *parts[::-1], out_space=HB,
    )


def solution(mesh):
    placed = (
        P("ctx", "kv", None),
        P("ctx", "kv", None),
        P("ctx", "kv", None),
        P(),
        P(),
        P(),
        P(),
        P(),
    )
    return jax.shard_map(
        shards, mesh=mesh, in_specs=placed, out_specs=P(("ctx", "kv"), None), check_vma=False
    )
```

```python
import functools
import math

import jax
import jax.numpy as jnp
import numpy as np
from jax import lax
from jax.experimental import pallas as pl
from jax.experimental.pallas import tpu as pltpu
from jax.sharding import PartitionSpec as P

HD = 128
TOK = 128
STRIDE = 32
SLOTS = TOK // STRIDE
WIN = 8
WINDOW = WIN * TOK
BLOCKS = 128
SEQ = BLOCKS * TOK
HEADS = 16
GROUPS = 2
KV = 4
RING = 4
ROWS = TOK // KV
RAW = (WIN + 1) * TOK
TOKP = 2 * GROUPS * TOK
KEYS = RAW + BLOCKS * SLOTS
MSCALE = 1.0 + 0.1 * math.log(16.0)
SCALE2 = math.log2(math.e) / math.sqrt(HD)
NEG = -1e30
BF = jnp.bfloat16
F32 = jnp.float32


def yarn_freqs():
    index = np.arange(HD // 2, dtype=np.float32)
    inverse = np.exp(np.float32(-(2.0 / HD) * math.log(500000.0)) * index).astype(np.float32)
    ratio = np.float32(8192.0) * inverse / np.float32(2.0 * math.pi)
    ramp = np.clip((ratio - 1.0) / 31.0, 0.0, 1.0).astype(np.float32)
    freqs = inverse * (ramp + (1.0 - ramp) / np.float32(16.0))
    return np.tile(np.concatenate([freqs, freqs])[None, :], (8, 1)).astype(np.float32)


def turn_tables(place0, freqs):
    places = (place0 + lax.broadcasted_iota(jnp.int32, (TOK, HD), 0)).astype(F32)
    angle = places * freqs
    first = lax.broadcasted_iota(jnp.int32, (TOK, HD), 1) < HD // 2
    sine = jnp.sin(angle)
    return jnp.cos(angle), jnp.where(first, -sine, sine)


def turn(x, cosine, sine):
    return ((x * cosine + pltpu.roll(x, HD // 2, 1) * sine) * MSCALE).astype(BF)


def prep_kernel(bs, freqs, k, v, dk, pk, dv, pv, own, mem, *scratch):
    scr, pool, s_bs, s_freqs, s_k, s_v, s_dk, s_pk, s_dv, s_pv, sem = scratch
    pairs = (
        (bs, s_bs), (freqs, s_freqs), (k, s_k), (v, s_v),
        (dk, s_dk), (pk, s_pk), (dv, s_dv), (pv, s_pv),
    )
    copies = [pltpu.make_async_copy(a, b, sem.at[i]) for i, (a, b) in enumerate(pairs)]
    for c in copies:
        c.start()
    for c in copies:
        c.wait()
    me = lax.axis_index("ctx")
    cosine, sine = turn_tables(s_bs[me], s_freqs[0:1, :])
    scr[...] = s_k[...].astype(F32)
    for g in range(GROUPS):
        rot = turn(scr[:, g, :], cosine, sine)
        own[g * TOK : (g + 1) * TOK, :] = rot
        grouped = rot.astype(F32).reshape(SLOTS, STRIDE, HD)
        pool[g * SLOTS : (g + 1) * SLOTS, :] = jnp.sum(grouped * s_dk[...][None], axis=1)
    scr[...] = s_v[...].astype(F32)
    for g in range(GROUPS):
        val = scr[:, g, :]
        own[(GROUPS + g) * TOK : (GROUPS + g + 1) * TOK, :] = val.astype(BF)
        grouped = val.reshape(SLOTS, STRIDE, HD)
        at = (GROUPS + g) * SLOTS
        pool[at : at + SLOTS, :] = jnp.sum(grouped * s_dv[...][None], axis=1)
    half = GROUPS * SLOTS
    mk = jnp.dot(pool[:half, :], s_pk[...], precision=lax.Precision.HIGHEST, preferred_element_type=F32)
    mv = jnp.dot(pool[half:, :], s_pv[...], precision=lax.Precision.HIGHEST, preferred_element_type=F32)
    both = jnp.concatenate([mk, mv], axis=0).astype(BF)
    mem[...] = jnp.broadcast_to(both[None], mem.shape)


def query_kernel(bs, freqs, q, rotq, scr):
    me = lax.axis_index("ctx")
    cosine, sine = turn_tables(bs[me], freqs[0:1, :])
    scr[...] = q[...].astype(F32)
    for h in range(HEADS):
        rotq[h] = turn(scr[:, h, :], cosine, sine)


def ring_kernel(own, row1, row2, rotq, bias, *outs):
    me = lax.rem(lax.axis_index("ctx"), RING)
    for s, out in enumerate(outs, 1):
        out[TOKP:, :] = row1[...]

        @pl.when(me + s < RING)
        def _():
            out[:TOKP, :] = own[...]

        @pl.when(me + s >= RING)
        def _():
            out[:TOKP, :] = row2[...]


def slot_kernel(mem, out, scr):
    scr[...] = mem[...].astype(F32)
    for kind in range(2 * GROUPS):
        for j in range(SLOTS):
            out[kind, j * BLOCKS : (j + 1) * BLOCKS, :] = scr[:, kind * SLOTS + j, :].astype(BF)


def bias_kernel(bs, bias):
    me = lax.axis_index("ctx")
    pos = lax.rem(me, RING)
    place = bs[me] + lax.broadcasted_iota(jnp.int32, (TOK, TOK), 1)
    row = lax.broadcasted_iota(jnp.int32, (TOK, TOK), 0)
    backs = [0, RING]
    for s in range(1, RING):
        wrapped = pos < s
        backs += [jnp.where(wrapped, RING + s, s), jnp.where(wrapped, s, RING + s)]
    backs += [WIN]
    for b, back in enumerate(backs):
        there = bs[lax.rem(me - back + BLOCKS, BLOCKS)] + row
        ok = (there <= place) & (there > place - WINDOW)
        bias[b * TOK : (b + 1) * TOK, :] = jnp.where(ok, 0.0, NEG).astype(BF)
    start = (bs[0] + TOK * row) & (SEQ - 1)
    for j in range(SLOTS):
        ok = start + (j + 1) * STRIDE <= place + 1
        lo = RAW + j * BLOCKS
        bias[lo : lo + BLOCKS, :] = jnp.where(ok, 0.0, NEG).astype(BF)


def key_tiles():
    half = SLOTS * BLOCKS // 2
    tiles = [(0, [("own", 0, TOK), ("row1", 0, TOK)])]
    for s in range(1, RING):
        tiles.append((2 * s * TOK, [(s, 0, TOK), (s, TOKP, TOK)]))
    tiles.append((RAW, [("mem", 0, half)]))
    tiles.append((RAW + half, [("mem", half, half)]))
    tiles.append((RAW - TOK, [("row2", 0, TOK)]))
    return [(lo, sum(n for _, _, n in tile), tile) for lo, tile in tiles]


def gather_tile(refs, tile, kind):
    parts = []
    for name, lo, n in tile:
        if name == "mem":
            parts.append(refs[name][kind, lo : lo + n, :])
        else:
            at = lo + kind * TOK
            parts.append(refs[name][at : at + n, :])
    return parts[0] if len(parts) == 1 else jnp.concatenate(parts, axis=0)


def chunk_kernel(off, rotq, bias, own, row1, row2, r1, r2, r3, mem, *rest):
    refs = {"own": own, "row1": row1, "row2": row2, 1: r1, 2: r2, 3: r3, "mem": mem}
    out, s = rest[-2:]
    dest = lax.axis_index("kv") ^ off
    first = pl.multiple_of(dest * ROWS, ROWS)
    heads = HEADS // GROUPS
    r = lax.broadcasted_iota(jnp.int32, (heads * ROWS, TOK), 0) & (ROWS - 1)
    c = lax.broadcasted_iota(jnp.int32, (heads * ROWS, TOK), 1)
    unit = jnp.where(r + first == c, 1.0, 0.0).astype(BF)
    for g in range(GROUPS):
        q = jnp.concatenate(
            [rotq[g * heads + i, pl.ds(first, ROWS), :] for i in range(heads)], axis=0
        )
        qa = jnp.concatenate([q, unit], axis=1)
        high = None
        for lo, size, tile in key_tiles():
            k = gather_tile(refs, tile, g)
            ka = jnp.concatenate([k, bias[lo : lo + size, :]], axis=1)
            x = lax.dot_general(qa, ka, (((1,), (1,)), ((), ())), preferred_element_type=F32)
            s[g, :, lo : lo + size] = x
            for i in range(size // HD):
                part = x[:, i * HD : (i + 1) * HD]
                high = part if high is None else jnp.maximum(high, part)
        top = jnp.max(high, axis=1, keepdims=True)
        mixed = None
        for lo, size, tile in key_tiles():
            w = jnp.exp2((s[g, :, lo : lo + size] - top) * SCALE2).astype(BF)
            v = gather_tile(refs, tile, GROUPS + g)
            va = jnp.concatenate([v, jnp.ones((size, HD), BF)], axis=1)
            part = jnp.dot(w, va, preferred_element_type=F32)
            mixed = part if mixed is None else mixed + part
        res = (mixed[:, :HD] / mixed[:, HD:]).astype(BF)
        for i in range(heads):
            h = g * heads + i
            out[:, h * HD : (h + 1) * HD] = res[i * ROWS : (i + 1) * ROWS, :]


def join_kernel(a, b, c, d, out, sem):
    me = lax.axis_index("kv")
    wide = HEADS * HD
    copies = []
    for off, part in enumerate((a, b, c, d)):
        lane = pl.multiple_of((me ^ off) * wide, wide)
        copies.append(pltpu.make_async_copy(part, out.at[:, pl.ds(lane, wide)], sem.at[off]))
    for x in copies:
        x.start()
    for x in copies:
        x.wait()


def call(kernel, out_shape, scratch, flops, spaces, *args, out_space=pltpu.VMEM, grant=32, alias=None):
    multi = isinstance(out_shape, tuple)
    vm = pl.BlockSpec(memory_space=out_space)
    return pl.pallas_call(
        kernel,
        out_shape=out_shape,
        in_specs=[pl.BlockSpec(memory_space=s) for s in spaces],
        out_specs=(vm,) * len(out_shape) if multi else vm,
        scratch_shapes=scratch,
        input_output_aliases=alias or {},
        compiler_params=pltpu.CompilerParams(vmem_limit_bytes=grant * 2**20),
        cost_estimate=pl.CostEstimate(flops=flops, bytes_accessed=2**10, transcendentals=0),
    )(*args)


def shape(*dims, dtype=BF):
    return jax.ShapeDtypeStruct(dims, dtype)


SM, VM, HB = pltpu.SMEM, pltpu.VMEM, pltpu.HBM


def shards(queries, keys, values, block_start, depth_k, point_k, depth_v, point_v):
    freqs = jnp.asarray(yarn_freqs())
    pack = 2 * GROUPS
    params = (block_start, freqs, keys, values, depth_k, point_k, depth_v, point_v)
    own, mem = call(
        prep_kernel,
        (shape(pack * TOK, HD), shape(BLOCKS, pack * SLOTS, HD)),
        [pltpu.VMEM((TOK, GROUPS, HD), F32), pltpu.VMEM((pack * SLOTS, HD), F32)]
        + [(pltpu.SMEM if i == 0 else pltpu.VMEM)(x.shape, x.dtype) for i, x in enumerate(params)]
        + [pltpu.SemaphoreType.DMA((len(params),))],
        10**9,
        (HB,) * len(params),
        *params,
        grant=60,
    )
    row1, row2 = (
        lax.ppermute(own, "ctx", [((i - d) % BLOCKS, i) for i in range(BLOCKS)])
        for d in (RING, 2 * RING)
    )
    mem = lax.all_to_all(mem, "ctx", 0, 0)
    rotq = call(
        query_kernel, shape(HEADS, TOK, HD), [pltpu.VMEM((TOK, HEADS, HD), F32)], 10**3,
        (SM, VM, VM),
        block_start, freqs, queries,
    )
    bias = call(bias_kernel, shape(KEYS, TOK), [], 10**3, (SM,), block_start)
    rings = call(
        ring_kernel, (shape(2 * TOKP, HD),) * (RING - 1), [], 10**3, (VM,) * 3 + (pl.ANY,) * 2,
        own, row1, row2, rotq, bias,
    )
    rings = [
        lax.ppermute(x, "ctx", [(i, i // RING * RING + (i + s) % RING) for i in range(BLOCKS)])
        for s, x in enumerate(rings, 1)
    ]
    mem = call(
        slot_kernel, shape(pack, BLOCKS * SLOTS, HD),
        [pltpu.VMEM((BLOCKS, pack * SLOTS, HD), F32)], 10**6, (VM,), mem,
    )
    parts = []
    for off in (3, 2, 1, 0):
        after = parts[-2:-1]
        part = call(
            functools.partial(chunk_kernel, off), shape(ROWS, HEADS * HD),
            [pltpu.VMEM((GROUPS, HEADS // GROUPS * ROWS, KEYS), F32)], 10**6,
            (VM,) * 9 + (pl.ANY,) * len(after), rotq, bias, own, row1, row2, *rings, mem, *after,
        )
        if off:
            part = lax.ppermute(part, "kv", [(i, i ^ off) for i in range(KV)])
        parts.append(part)
    return call(
        join_kernel, shape(ROWS, KV * HEADS * HD), [pltpu.SemaphoreType.DMA((KV,))], 10**8,
        (VM,) * 4, *parts[::-1], out_space=HB,
    )


def solution(mesh):
    placed = (
        P("ctx", "kv", None),
        P("ctx", "kv", None),
        P("ctx", "kv", None),
        P(),
        P(),
        P(),
        P(),
        P(),
    )
    return jax.shard_map(
        shards, mesh=mesh, in_specs=placed, out_specs=P(("ctx", "kv"), None), check_vma=False
    )
```

```python
import functools
import math

import jax
import jax.numpy as jnp
import numpy as np
from jax import lax
from jax.experimental import pallas as pl
from jax.experimental.pallas import tpu as pltpu
from jax.sharding import PartitionSpec as P

HD = 128
TOK = 128
STRIDE = 32
SLOTS = TOK // STRIDE
WIN = 8
WINDOW = WIN * TOK
BLOCKS = 128
SEQ = BLOCKS * TOK
HEADS = 16
GROUPS = 2
KV = 4
RING = 4
NEAR = 8
FAR = BLOCKS // NEAR
ROWS = TOK // KV
RAW = (WIN + 1) * TOK
TOKP = 2 * GROUPS * TOK
PIECE = SLOTS * NEAR
KEYS = RAW + BLOCKS * SLOTS
MSCALE = 1.0 + 0.1 * math.log(16.0)
SCALE2 = math.log2(math.e) / math.sqrt(HD)
NEG = -1e30
BF = jnp.bfloat16
F32 = jnp.float32


def yarn_freqs():
    index = np.arange(HD // 2, dtype=np.float32)
    inverse = np.exp(np.float32(-(2.0 / HD) * math.log(500000.0)) * index).astype(np.float32)
    ratio = np.float32(8192.0) * inverse / np.float32(2.0 * math.pi)
    ramp = np.clip((ratio - 1.0) / 31.0, 0.0, 1.0).astype(np.float32)
    freqs = inverse * (ramp + (1.0 - ramp) / np.float32(16.0))
    return np.tile(np.concatenate([freqs, freqs])[None, :], (8, 1)).astype(np.float32)


def turn_tables(place0, freqs):
    places = (place0 + lax.broadcasted_iota(jnp.int32, (TOK, HD), 0)).astype(F32)
    angle = places * freqs
    first = lax.broadcasted_iota(jnp.int32, (TOK, HD), 1) < HD // 2
    sine = jnp.sin(angle)
    return jnp.cos(angle), jnp.where(first, -sine, sine)


def turn(x, cosine, sine):
    return ((x * cosine + pltpu.roll(x, HD // 2, 1) * sine) * MSCALE).astype(BF)


def prep_kernel(bs, freqs, k, v, dk, pk, dv, pv, own, mem, *scratch):
    scr, pool, s_bs, s_freqs, s_k, s_v, s_dk, s_pk, s_dv, s_pv, sem = scratch
    pairs = (
        (bs, s_bs), (freqs, s_freqs), (k, s_k), (v, s_v),
        (dk, s_dk), (pk, s_pk), (dv, s_dv), (pv, s_pv),
    )
    copies = [pltpu.make_async_copy(a, b, sem.at[i]) for i, (a, b) in enumerate(pairs)]
    for c in copies:
        c.start()
    for c in copies:
        c.wait()
    me = lax.axis_index("ctx")
    cosine, sine = turn_tables(s_bs[me], s_freqs[0:1, :])
    scr[...] = s_k[...].astype(F32)
    for g in range(GROUPS):
        rot = turn(scr[:, g, :], cosine, sine)
        own[g * TOK : (g + 1) * TOK, :] = rot
        grouped = rot.astype(F32).reshape(SLOTS, STRIDE, HD)
        pool[g * SLOTS : (g + 1) * SLOTS, :] = jnp.sum(grouped * s_dk[...][None], axis=1)
    scr[...] = s_v[...].astype(F32)
    for g in range(GROUPS):
        val = scr[:, g, :]
        own[(GROUPS + g) * TOK : (GROUPS + g + 1) * TOK, :] = val.astype(BF)
        grouped = val.reshape(SLOTS, STRIDE, HD)
        at = (GROUPS + g) * SLOTS
        pool[at : at + SLOTS, :] = jnp.sum(grouped * s_dv[...][None], axis=1)
    half = GROUPS * SLOTS
    mk = jnp.dot(pool[:half, :], s_pk[...], precision=lax.Precision.HIGHEST, preferred_element_type=F32)
    mv = jnp.dot(pool[half:, :], s_pv[...], precision=lax.Precision.HIGHEST, preferred_element_type=F32)
    both = jnp.concatenate([mk, mv], axis=0).astype(BF)
    mem[...] = jnp.broadcast_to(both[None], mem.shape)


def query_kernel(bs, freqs, q, rotq, scr):
    me = lax.axis_index("ctx")
    cosine, sine = turn_tables(bs[me], freqs[0:1, :])
    scr[...] = q[...].astype(F32)
    for h in range(HEADS):
        rotq[h] = turn(scr[:, h, :], cosine, sine)


def ring_kernel(own, row1, row2, mem, r1, r2, r3, far, scr):
    me = lax.rem(lax.axis_index("ctx"), RING)
    scr[...] = mem[...].astype(F32)
    kinds = 2 * GROUPS * SLOTS
    slots = jnp.concatenate([scr[:, r, :] for r in range(kinds)], axis=0).astype(BF)
    far[...] = jnp.broadcast_to(slots[None], far.shape)
    for s, out in enumerate((r1, r2, r3), 1):
        out[TOKP:, :] = row1[...]

        @pl.when(me + s < RING)
        def _():
            out[:TOKP, :] = own[...]

        @pl.when(me + s >= RING)
        def _():
            out[:TOKP, :] = row2[...]


def bias_kernel(bs, bias):
    me = lax.axis_index("ctx")
    pos = lax.rem(me, RING)
    place = bs[me] + lax.broadcasted_iota(jnp.int32, (TOK, TOK), 1)
    row = lax.broadcasted_iota(jnp.int32, (TOK, TOK), 0)
    backs = [0, RING]
    for s in range(1, RING):
        wrapped = pos < s
        backs += [jnp.where(wrapped, RING + s, s), jnp.where(wrapped, s, RING + s)]
    backs += [WIN]
    for b, back in enumerate(backs):
        there = bs[lax.rem(me - back + BLOCKS, BLOCKS)] + row
        ok = (there <= place) & (there > place - WINDOW)
        bias[b * TOK : (b + 1) * TOK, :] = jnp.where(ok, 0.0, NEG).astype(BF)
    for lo in range(0, BLOCKS * SLOTS, TOK):
        at = lo + row
        block = at // PIECE * NEAR + (at & (NEAR - 1))
        slot = (at & (PIECE - 1)) // NEAR
        ok = ((bs[0] + TOK * block) & (SEQ - 1)) + (slot + 1) * STRIDE <= place + 1
        bias[RAW + lo : RAW + lo + TOK, :] = jnp.where(ok, 0.0, NEG).astype(BF)


def key_tiles():
    half = SLOTS * BLOCKS // 2
    tiles = [(0, [("own", 0, TOK), ("row1", 0, TOK)])]
    for s in range(1, RING):
        tiles.append((2 * s * TOK, [(s, 0, TOK), (s, TOKP, TOK)]))
    tiles.append((RAW, [("mem", 0, half)]))
    tiles.append((RAW + half, [("mem", half, half)]))
    tiles.append((RAW - TOK, [("row2", 0, TOK)]))
    return [(lo, sum(n for _, _, n in tile), tile) for lo, tile in tiles]


def gather_tile(refs, tile, kind):
    parts = []
    for name, lo, n in tile:
        if name == "mem":
            rows = slice(kind * PIECE, (kind + 1) * PIECE)
            parts += [refs[name][i, rows, :] for i in range(lo // PIECE, (lo + n) // PIECE)]
        else:
            at = lo + kind * TOK
            parts.append(refs[name][at : at + n, :])
    return parts[0] if len(parts) == 1 else jnp.concatenate(parts, axis=0)


def chunk_kernel(off, rotq, bias, own, row1, row2, r1, r2, r3, mem, *rest):
    refs = {"own": own, "row1": row1, "row2": row2, 1: r1, 2: r2, 3: r3, "mem": mem}
    out, s = rest[-2:]
    dest = lax.axis_index("kv") ^ off
    first = pl.multiple_of(dest * ROWS, ROWS)
    heads = HEADS // GROUPS
    r = lax.broadcasted_iota(jnp.int32, (heads * ROWS, TOK), 0) & (ROWS - 1)
    c = lax.broadcasted_iota(jnp.int32, (heads * ROWS, TOK), 1)
    unit = jnp.where(r + first == c, 1.0, 0.0).astype(BF)
    for g in range(GROUPS):
        q = jnp.concatenate(
            [rotq[g * heads + i, pl.ds(first, ROWS), :] for i in range(heads)], axis=0
        )
        qa = jnp.concatenate([q, unit], axis=1)
        high = None
        for lo, size, tile in key_tiles():
            k = gather_tile(refs, tile, g)
            ka = jnp.concatenate([k, bias[lo : lo + size, :]], axis=1)
            x = lax.dot_general(qa, ka, (((1,), (1,)), ((), ())), preferred_element_type=F32)
            s[g, :, lo : lo + size] = x
            for i in range(size // HD):
                part = x[:, i * HD : (i + 1) * HD]
                high = part if high is None else jnp.maximum(high, part)
        top = jnp.max(high, axis=1, keepdims=True)
        mixed = None
        for lo, size, tile in key_tiles():
            w = jnp.exp2((s[g, :, lo : lo + size] - top) * SCALE2).astype(BF)
            v = gather_tile(refs, tile, GROUPS + g)
            va = jnp.concatenate([v, jnp.ones((size, HD), BF)], axis=1)
            part = jnp.dot(w, va, preferred_element_type=F32)
            mixed = part if mixed is None else mixed + part
        res = (mixed[:, :HD] / mixed[:, HD:]).astype(BF)
        for i in range(heads):
            h = g * heads + i
            out[:, h * HD : (h + 1) * HD] = res[i * ROWS : (i + 1) * ROWS, :]


def join_kernel(a, b, c, d, out, sem):
    me = lax.axis_index("kv")
    wide = HEADS * HD
    copies = []
    for off, part in enumerate((a, b, c, d)):
        lane = pl.multiple_of((me ^ off) * wide, wide)
        copies.append(pltpu.make_async_copy(part, out.at[:, pl.ds(lane, wide)], sem.at[off]))
    for x in copies:
        x.start()
    for x in copies:
        x.wait()


def call(kernel, out_shape, scratch, flops, spaces, *args, out_space=pltpu.VMEM, grant=32, alias=None):
    multi = isinstance(out_shape, tuple)
    vm = pl.BlockSpec(memory_space=out_space)
    return pl.pallas_call(
        kernel,
        out_shape=out_shape,
        in_specs=[pl.BlockSpec(memory_space=s) for s in spaces],
        out_specs=(vm,) * len(out_shape) if multi else vm,
        scratch_shapes=scratch,
        input_output_aliases=alias or {},
        compiler_params=pltpu.CompilerParams(vmem_limit_bytes=grant * 2**20),
        cost_estimate=pl.CostEstimate(flops=flops, bytes_accessed=2**10, transcendentals=0),
    )(*args)


def shape(*dims, dtype=BF):
    return jax.ShapeDtypeStruct(dims, dtype)


near = [[NEAR * o + p for p in range(NEAR)] for o in range(FAR)]
strided = [[NEAR * o + p for o in range(FAR)] for p in range(NEAR)]
SM, VM, HB = pltpu.SMEM, pltpu.VMEM, pltpu.HBM


def shards(queries, keys, values, block_start, depth_k, point_k, depth_v, point_v):
    freqs = jnp.asarray(yarn_freqs())
    pack = 2 * GROUPS
    params = (block_start, freqs, keys, values, depth_k, point_k, depth_v, point_v)
    own, mem = call(
        prep_kernel,
        (shape(pack * TOK, HD), shape(NEAR, pack * SLOTS, HD)),
        [pltpu.VMEM((TOK, GROUPS, HD), F32), pltpu.VMEM((pack * SLOTS, HD), F32)]
        + [(pltpu.SMEM if i == 0 else pltpu.VMEM)(x.shape, x.dtype) for i, x in enumerate(params)]
        + [pltpu.SemaphoreType.DMA((len(params),))],
        10**9,
        (HB,) * len(params),
        *params,
        grant=60,
    )
    row1, row2 = (
        lax.ppermute(own, "ctx", [((i - d) % BLOCKS, i) for i in range(BLOCKS)])
        for d in (RING, 2 * RING)
    )
    mem = lax.all_to_all(mem, "ctx", 0, 0, axis_index_groups=near)
    rotq = call(
        query_kernel, shape(HEADS, TOK, HD), [pltpu.VMEM((TOK, HEADS, HD), F32)], 10**3,
        (SM, VM, VM),
        block_start, freqs, queries,
    )
    bias = call(bias_kernel, shape(KEYS, TOK), [], 10**3, (SM,), block_start)
    *rings, far = call(
        ring_kernel,
        (shape(2 * TOKP, HD),) * (RING - 1) + (shape(FAR, pack * PIECE, HD),),
        [pltpu.VMEM((NEAR, pack * SLOTS, HD), F32)], 10**3, (VM,) * 4,
        own, row1, row2, mem,
    )
    mem = lax.all_to_all(far, "ctx", 0, 0, axis_index_groups=strided)
    rings = [
        lax.ppermute(x, "ctx", [(i, i // RING * RING + (i + s) % RING) for i in range(BLOCKS)])
        for s, x in enumerate(rings, 1)
    ]
    parts = []
    for off in (3, 2, 1, 0):
        after = parts[-2:-1]
        part = call(
            functools.partial(chunk_kernel, off), shape(ROWS, HEADS * HD),
            [pltpu.VMEM((GROUPS, HEADS // GROUPS * ROWS, KEYS), F32)], 10**6,
            (VM,) * 9 + (pl.ANY,) * len(after), rotq, bias, own, row1, row2, *rings, mem, *after,
        )
        if off:
            part = lax.ppermute(part, "kv", [(i, i ^ off) for i in range(KV)])
        parts.append(part)
    return call(
        join_kernel, shape(ROWS, KV * HEADS * HD), [pltpu.SemaphoreType.DMA((KV,))], 10**8,
        (VM,) * 4, *parts[::-1], out_space=HB,
    )


def solution(mesh):
    placed = (
        P("ctx", "kv", None),
        P("ctx", "kv", None),
        P("ctx", "kv", None),
        P(),
        P(),
        P(),
        P(),
        P(),
    )
    return jax.shard_map(
        shards, mesh=mesh, in_specs=placed, out_specs=P(("ctx", "kv"), None), check_vma=False
    )
```

```python
import functools
import math

import jax
import jax.numpy as jnp
import numpy as np
from jax import lax
from jax.experimental import pallas as pl
from jax.experimental.pallas import tpu as pltpu
from jax.sharding import PartitionSpec as P

HD = 128
TOK = 128
STRIDE = 32
SLOTS = TOK // STRIDE
WIN = 8
WINDOW = WIN * TOK
BLOCKS = 128
SEQ = BLOCKS * TOK
HEADS = 16
GROUPS = 2
KV = 4
RING = 4
BATCH = 4
NEAR = 8
FAR = BLOCKS // NEAR
ROWS = TOK // KV
RAW = (WIN + 1) * TOK
TOKP = 2 * GROUPS * TOK
PIECE = SLOTS * NEAR
KEYS = RAW + BLOCKS * SLOTS
MSCALE = 1.0 + 0.1 * math.log(16.0)
SCALE2 = math.log2(math.e) / math.sqrt(HD)
NEG = -1e30
BF = jnp.bfloat16
F32 = jnp.float32


def yarn_freqs():
    index = np.arange(HD // 2, dtype=np.float32)
    inverse = np.exp(np.float32(-(2.0 / HD) * math.log(500000.0)) * index).astype(np.float32)
    ratio = np.float32(8192.0) * inverse / np.float32(2.0 * math.pi)
    ramp = np.clip((ratio - 1.0) / 31.0, 0.0, 1.0).astype(np.float32)
    freqs = inverse * (ramp + (1.0 - ramp) / np.float32(16.0))
    return np.tile(np.concatenate([freqs, freqs])[None, :], (8, 1)).astype(np.float32)


def turn_tables(place0, freqs):
    places = (place0 + lax.broadcasted_iota(jnp.int32, (TOK, HD), 0)).astype(F32)
    angle = places * freqs
    first = lax.broadcasted_iota(jnp.int32, (TOK, HD), 1) < HD // 2
    sine = jnp.sin(angle)
    return jnp.cos(angle), jnp.where(first, -sine, sine)


def turn(x, cosine, sine):
    return ((x * cosine + pltpu.roll(x, HD // 2, 1) * sine) * MSCALE).astype(BF)


def prep_kernel(bs, freqs, k, v, dk, pk, dv, pv, own, mem, *scratch):
    scr, pool, s_bs, s_freqs, s_k, s_v, s_dk, s_pk, s_dv, s_pv, sem = scratch
    pairs = (
        (bs, s_bs), (freqs, s_freqs), (k, s_k), (v, s_v),
        (dk, s_dk), (pk, s_pk), (dv, s_dv), (pv, s_pv),
    )
    copies = [pltpu.make_async_copy(a, b, sem.at[i]) for i, (a, b) in enumerate(pairs)]
    for c in copies:
        c.start()
    for c in copies:
        c.wait()
    me = lax.axis_index("ctx")
    cosine, sine = turn_tables(s_bs[me], s_freqs[0:1, :])
    scr[...] = s_k[...].astype(F32)
    for g in range(GROUPS):
        rot = turn(scr[:, g, :], cosine, sine)
        own[g * TOK : (g + 1) * TOK, :] = rot
        grouped = rot.astype(F32).reshape(SLOTS, STRIDE, HD)
        pool[g * SLOTS : (g + 1) * SLOTS, :] = jnp.sum(grouped * s_dk[...][None], axis=1)
    scr[...] = s_v[...].astype(F32)
    for g in range(GROUPS):
        val = scr[:, g, :]
        own[(GROUPS + g) * TOK : (GROUPS + g + 1) * TOK, :] = val.astype(BF)
        grouped = val.reshape(SLOTS, STRIDE, HD)
        at = (GROUPS + g) * SLOTS
        pool[at : at + SLOTS, :] = jnp.sum(grouped * s_dv[...][None], axis=1)
    half = GROUPS * SLOTS
    mk = jnp.dot(pool[:half, :], s_pk[...], precision=lax.Precision.HIGHEST, preferred_element_type=F32)
    mv = jnp.dot(pool[half:, :], s_pv[...], precision=lax.Precision.HIGHEST, preferred_element_type=F32)
    both = jnp.concatenate([mk, mv], axis=0).astype(BF)
    mem[...] = jnp.broadcast_to(both[None], mem.shape)


def query_kernel(bs, freqs, q, rotq, scr):
    me = lax.axis_index("ctx")
    cosine, sine = turn_tables(bs[me], freqs[0:1, :])
    scr[...] = q[...].astype(F32)
    for h in range(HEADS):
        rotq[h] = turn(scr[:, h, :], cosine, sine)


def ring_kernel(own, row1, row2, mem, r1, r2, r3, far, scr):
    me = lax.rem(lax.axis_index("ctx"), RING)
    scr[...] = mem[...].astype(F32)
    kinds = 2 * GROUPS * SLOTS
    slots = jnp.concatenate([scr[:, r, :] for r in range(kinds)], axis=0).astype(BF)
    far[...] = jnp.broadcast_to(slots[None], far.shape)
    for s, out in enumerate((r1, r2, r3), 1):
        out[TOKP:, :] = row1[...]

        @pl.when(me + s < RING)
        def _():
            out[:TOKP, :] = own[...]

        @pl.when(me + s >= RING)
        def _():
            out[:TOKP, :] = row2[...]


def bias_kernel(bs, bias):
    me = lax.axis_index("ctx")
    pos = lax.rem(me, RING)
    place = bs[me] + lax.broadcasted_iota(jnp.int32, (TOK, TOK), 1)
    row = lax.broadcasted_iota(jnp.int32, (TOK, TOK), 0)
    backs = [0, RING]
    for s in range(1, RING):
        wrapped = pos < s
        backs += [jnp.where(wrapped, RING + s, s), jnp.where(wrapped, s, RING + s)]
    backs += [WIN]
    for b, back in enumerate(backs):
        there = bs[lax.rem(me - back + BLOCKS, BLOCKS)] + row
        ok = (there <= place) & (there > place - WINDOW)
        bias[b * TOK : (b + 1) * TOK, :] = jnp.where(ok, 0.0, NEG).astype(BF)
    for lo in range(0, BLOCKS * SLOTS, TOK):
        at = lo + row
        block = at // PIECE * NEAR + (at & (NEAR - 1))
        slot = (at & (PIECE - 1)) // NEAR
        ok = ((bs[0] + TOK * block) & (SEQ - 1)) + (slot + 1) * STRIDE <= place + 1
        bias[RAW + lo : RAW + lo + TOK, :] = jnp.where(ok, 0.0, NEG).astype(BF)


def score(qa, k, bias):
    ka = jnp.concatenate([k, bias], axis=1)
    return lax.dot_general(qa, ka, (((1,), (1,)), ((), ())), preferred_element_type=F32)


def tile_max(high, x):
    for i in range(x.shape[1] // HD):
        part = x[:, i * HD : (i + 1) * HD]
        high = part if high is None else jnp.maximum(high, part)
    return high


def weigh(x, top, v):
    w = jnp.exp2((x - top) * SCALE2).astype(BF)
    va = jnp.concatenate([v, jnp.ones(v.shape, BF)], axis=1)
    return jnp.dot(w, va, preferred_element_type=F32)


def window_kernel(rotq, bias, own, row1, row2, r1, r2, r3, acc, high, s):
    tiles = [(0, ((own, 0), (row1, 0)))]
    for i, r in enumerate((r1, r2, r3), 1):
        tiles.append((2 * i * TOK, ((r, 0), (r, TOKP))))
    tiles.append((RAW - TOK, ((row2, 0),)))

    def rows_of(parts, kind):
        got = [r[lo + kind * TOK : lo + (kind + 1) * TOK, :] for r, lo in parts]
        return jnp.concatenate(got, axis=0) if len(got) > 1 else got[0]

    r = lax.broadcasted_iota(jnp.int32, (BATCH * TOK, TOK), 0) & (TOK - 1)
    c = lax.broadcasted_iota(jnp.int32, (BATCH * TOK, TOK), 1)
    unit = jnp.where(r == c, 1.0, 0.0).astype(BF)
    for first in range(0, HEADS, BATCH):
        g = first // (HEADS // GROUPS)
        slot = first // BATCH % 2
        q = rotq[first : first + BATCH].reshape(BATCH * TOK, HD)
        qa = jnp.concatenate([q, unit], axis=1)
        top = None
        for lo, parts in tiles:
            size = len(parts) * TOK
            x = score(qa, rows_of(parts, g), bias[lo : lo + size, :])
            s[slot, :, lo : lo + size] = x
            top = tile_max(top, x)
        top = jnp.max(top, axis=1, keepdims=True)
        mixed = None
        for lo, parts in tiles:
            size = len(parts) * TOK
            part = weigh(s[slot, :, lo : lo + size], top, rows_of(parts, GROUPS + g))
            mixed = part if mixed is None else mixed + part
        acc[first : first + BATCH] = mixed.reshape(BATCH, TOK, 2 * HD)
        high[first : first + BATCH] = jnp.broadcast_to(top, (BATCH * TOK, HD)).reshape(
            BATCH, TOK, HD
        )


def chunk_kernel(off, rotq, bias, mem, acc, high, *rest):
    out = rest[-1]
    dest = lax.axis_index("kv") ^ off
    first = pl.multiple_of(dest * ROWS, ROWS)
    heads = HEADS // GROUPS
    r = lax.broadcasted_iota(jnp.int32, (heads * ROWS, TOK), 0) & (ROWS - 1)
    c = lax.broadcasted_iota(jnp.int32, (heads * ROWS, TOK), 1)
    unit = jnp.where(r + first == c, 1.0, 0.0).astype(BF)
    half = BLOCKS * SLOTS // 2

    def rows_of(lo, kind):
        span = slice(kind * PIECE, (kind + 1) * PIECE)
        return jnp.concatenate(
            [mem[i, span, :] for i in range(lo // PIECE, (lo + half) // PIECE)], axis=0
        )

    def heads_of(ref, g):
        return jnp.concatenate(
            [ref[g * heads + i, pl.ds(first, ROWS), :] for i in range(heads)], axis=0
        )

    for g in range(GROUPS):
        qa = jnp.concatenate([heads_of(rotq, g), unit], axis=1)
        xs = [
            score(qa, rows_of(lo, g), bias[RAW + lo : RAW + lo + half, :]) for lo in (0, half)
        ]
        top = tile_max(tile_max(None, xs[0]), xs[1])
        before = heads_of(high, g)
        top = jnp.maximum(jnp.max(top, axis=1, keepdims=True), before)
        keep = jnp.exp2((before - top) * SCALE2)
        old = heads_of(acc, g)
        mixed, total = old[:, :HD] * keep, old[:, HD:] * keep
        wide = jnp.concatenate([top] * (half // HD), axis=1)
        new = weigh(xs[0], wide, rows_of(0, GROUPS + g)) + weigh(
            xs[1], wide, rows_of(half, GROUPS + g)
        )
        res = ((mixed + new[:, :HD]) / (total + new[:, HD:])).astype(BF)
        for i in range(heads):
            h = g * heads + i
            out[:, h * HD : (h + 1) * HD] = res[i * ROWS : (i + 1) * ROWS, :]


def join_kernel(a, b, c, d, out, sem):
    me = lax.axis_index("kv")
    wide = HEADS * HD
    copies = []
    for off, part in enumerate((a, b, c, d)):
        lane = pl.multiple_of((me ^ off) * wide, wide)
        copies.append(pltpu.make_async_copy(part, out.at[:, pl.ds(lane, wide)], sem.at[off]))
    for x in copies:
        x.start()
    for x in copies:
        x.wait()


def call(kernel, out_shape, scratch, flops, spaces, *args, out_space=pltpu.VMEM, grant=32, alias=None):
    multi = isinstance(out_shape, tuple)
    vm = pl.BlockSpec(memory_space=out_space)
    return pl.pallas_call(
        kernel,
        out_shape=out_shape,
        in_specs=[pl.BlockSpec(memory_space=s) for s in spaces],
        out_specs=(vm,) * len(out_shape) if multi else vm,
        scratch_shapes=scratch,
        input_output_aliases=alias or {},
        compiler_params=pltpu.CompilerParams(vmem_limit_bytes=grant * 2**20),
        cost_estimate=pl.CostEstimate(flops=flops, bytes_accessed=2**10, transcendentals=0),
    )(*args)


def shape(*dims, dtype=BF):
    return jax.ShapeDtypeStruct(dims, dtype)


near = [[NEAR * o + p for p in range(NEAR)] for o in range(FAR)]
strided = [[NEAR * o + p for o in range(FAR)] for p in range(NEAR)]
SM, VM, HB = pltpu.SMEM, pltpu.VMEM, pltpu.HBM


def shards(queries, keys, values, block_start, depth_k, point_k, depth_v, point_v):
    freqs = jnp.asarray(yarn_freqs())
    pack = 2 * GROUPS
    params = (block_start, freqs, keys, values, depth_k, point_k, depth_v, point_v)
    own, mem = call(
        prep_kernel,
        (shape(pack * TOK, HD), shape(NEAR, pack * SLOTS, HD)),
        [pltpu.VMEM((TOK, GROUPS, HD), F32), pltpu.VMEM((pack * SLOTS, HD), F32)]
        + [(pltpu.SMEM if i == 0 else pltpu.VMEM)(x.shape, x.dtype) for i, x in enumerate(params)]
        + [pltpu.SemaphoreType.DMA((len(params),))],
        10**9,
        (HB,) * len(params),
        *params,
        grant=60,
    )
    row1, row2 = (
        lax.ppermute(own, "ctx", [((i - d) % BLOCKS, i) for i in range(BLOCKS)])
        for d in (RING, 2 * RING)
    )
    mem = lax.all_to_all(mem, "ctx", 0, 0, axis_index_groups=near)
    rotq = call(
        query_kernel, shape(HEADS, TOK, HD), [pltpu.VMEM((TOK, HEADS, HD), F32)], 10**3,
        (SM, VM, VM),
        block_start, freqs, queries,
    )
    bias = call(bias_kernel, shape(KEYS, TOK), [], 10**3, (SM,), block_start)
    *rings, far = call(
        ring_kernel,
        (shape(2 * TOKP, HD),) * (RING - 1) + (shape(FAR, pack * PIECE, HD),),
        [pltpu.VMEM((NEAR, pack * SLOTS, HD), F32)], 10**3, (VM,) * 4,
        own, row1, row2, mem,
    )
    mem = lax.all_to_all(far, "ctx", 0, 0, axis_index_groups=strided)
    rings = [
        lax.ppermute(x, "ctx", [(i, i // RING * RING + (i + s) % RING) for i in range(BLOCKS)])
        for s, x in enumerate(rings, 1)
    ]
    acc, high = call(
        window_kernel,
        (shape(HEADS, TOK, 2 * HD, dtype=F32), shape(HEADS, TOK, HD, dtype=F32)),
        [pltpu.VMEM((2, BATCH * TOK, RAW), F32)], 10**10, (VM,) * 8,
        rotq, bias, own, row1, row2, *rings, grant=16,
    )
    parts = []
    for off in (3, 2, 1, 0):
        after = parts[-2:-1]
        part = call(
            functools.partial(chunk_kernel, off), shape(ROWS, HEADS * HD), [], 10**6,
            (VM,) * 5 + (pl.ANY,) * len(after), rotq, bias, mem, acc, high, *after, grant=16,
        )
        if off:
            part = lax.ppermute(part, "kv", [(i, i ^ off) for i in range(KV)])
        parts.append(part)
    return call(
        join_kernel, shape(ROWS, KV * HEADS * HD), [pltpu.SemaphoreType.DMA((KV,))], 10**8,
        (VM,) * 4, *parts[::-1], out_space=HB,
    )


def solution(mesh):
    placed = (
        P("ctx", "kv", None),
        P("ctx", "kv", None),
        P("ctx", "kv", None),
        P(),
        P(),
        P(),
        P(),
        P(),
    )
    return jax.shard_map(
        shards, mesh=mesh, in_specs=placed, out_specs=P(("ctx", "kv"), None), check_vma=False
    )
```

```python
import functools
import math

import jax
import jax.numpy as jnp
import numpy as np
from jax import lax
from jax.experimental import pallas as pl
from jax.experimental.pallas import tpu as pltpu
from jax.sharding import PartitionSpec as P

HD = 128
TOK = 128
STRIDE = 32
SLOTS = TOK // STRIDE
WIN = 8
WINDOW = WIN * TOK
BLOCKS = 128
SEQ = BLOCKS * TOK
HEADS = 16
GROUPS = 2
KV = 4
RING = 4
NEAR = 8
FAR = BLOCKS // NEAR
ROWS = TOK // KV
RAW = (WIN + 1) * TOK
TOKP = 2 * GROUPS * TOK
PIECE = SLOTS * NEAR
KEYS = RAW + BLOCKS * SLOTS
MSCALE = 1.0 + 0.1 * math.log(16.0)
SCALE2 = math.log2(math.e) / math.sqrt(HD)
NEG = -1e30
BF = jnp.bfloat16
F32 = jnp.float32


def yarn_freqs():
    index = np.arange(HD // 2, dtype=np.float32)
    inverse = np.exp(np.float32(-(2.0 / HD) * math.log(500000.0)) * index).astype(np.float32)
    ratio = np.float32(8192.0) * inverse / np.float32(2.0 * math.pi)
    ramp = np.clip((ratio - 1.0) / 31.0, 0.0, 1.0).astype(np.float32)
    freqs = inverse * (ramp + (1.0 - ramp) / np.float32(16.0))
    return np.tile(np.concatenate([freqs, freqs])[None, :], (8, 1)).astype(np.float32)


def turn_tables(place0, freqs):
    places = (place0 + lax.broadcasted_iota(jnp.int32, (TOK, HD), 0)).astype(F32)
    angle = places * freqs
    first = lax.broadcasted_iota(jnp.int32, (TOK, HD), 1) < HD // 2
    sine = jnp.sin(angle)
    return jnp.cos(angle), jnp.where(first, -sine, sine)


def turn(x, cosine, sine, scale=MSCALE):
    return ((x * cosine + pltpu.roll(x, HD // 2, 1) * sine) * scale).astype(BF)


def prep_kernel(bs, freqs, k, v, dk, pk, dv, pv, own, mem, *scratch):
    scr, pool, s_bs, s_freqs, s_k, s_v, s_dk, s_pk, s_dv, s_pv, sem = scratch
    pairs = (
        (bs, s_bs), (freqs, s_freqs), (k, s_k), (v, s_v),
        (dk, s_dk), (pk, s_pk), (dv, s_dv), (pv, s_pv),
    )
    copies = [pltpu.make_async_copy(a, b, sem.at[i]) for i, (a, b) in enumerate(pairs)]
    for c in copies:
        c.start()
    for c in copies:
        c.wait()
    me = lax.axis_index("ctx")
    cosine, sine = turn_tables(s_bs[me], s_freqs[0:1, :])
    scr[...] = s_k[...].astype(F32)
    for g in range(GROUPS):
        rot = turn(scr[:, g, :], cosine, sine)
        own[g * TOK : (g + 1) * TOK, :] = rot
        grouped = rot.astype(F32).reshape(SLOTS, STRIDE, HD)
        pool[g * SLOTS : (g + 1) * SLOTS, :] = jnp.sum(grouped * s_dk[...][None], axis=1)
    scr[...] = s_v[...].astype(F32)
    for g in range(GROUPS):
        val = scr[:, g, :]
        own[(GROUPS + g) * TOK : (GROUPS + g + 1) * TOK, :] = val.astype(BF)
        grouped = val.reshape(SLOTS, STRIDE, HD)
        at = (GROUPS + g) * SLOTS
        pool[at : at + SLOTS, :] = jnp.sum(grouped * s_dv[...][None], axis=1)
    half = GROUPS * SLOTS
    mk = jnp.dot(pool[:half, :], s_pk[...], precision=lax.Precision.HIGHEST, preferred_element_type=F32)
    mv = jnp.dot(pool[half:, :], s_pv[...], precision=lax.Precision.HIGHEST, preferred_element_type=F32)
    both = jnp.concatenate([mk, mv], axis=0).astype(BF)
    mem[...] = jnp.broadcast_to(both[None], mem.shape)


def query_kernel(bs, freqs, q, after, rotq, scr):
    me = lax.axis_index("ctx")
    cosine, sine = turn_tables(bs[me], freqs[0:1, :])
    scr[...] = q[...].astype(F32)
    for h in range(HEADS):
        rotq[h] = turn(scr[:, h, :], cosine, sine, MSCALE * SCALE2)


def ring_kernel(own, row1, row2, mem, r1, r2, r3, far, scr):
    me = lax.rem(lax.axis_index("ctx"), RING)
    scr[...] = mem[...].astype(F32)
    kinds = 2 * GROUPS * SLOTS
    slots = jnp.concatenate([scr[:, r, :] for r in range(kinds)], axis=0).astype(BF)
    far[...] = jnp.broadcast_to(slots[None], far.shape)
    for s, out in enumerate((r1, r2, r3), 1):
        out[TOKP:, :] = row1[...]

        @pl.when(me + s < RING)
        def _():
            out[:TOKP, :] = own[...]

        @pl.when(me + s >= RING)
        def _():
            out[:TOKP, :] = row2[...]


def bias_kernel(bs, bias):
    me = lax.axis_index("ctx")
    pos = lax.rem(me, RING)
    place = bs[me] + lax.broadcasted_iota(jnp.int32, (TOK, TOK), 1)
    row = lax.broadcasted_iota(jnp.int32, (TOK, TOK), 0)
    backs = [0, RING]
    for s in range(1, RING):
        wrapped = pos < s
        backs += [jnp.where(wrapped, RING + s, s), jnp.where(wrapped, s, RING + s)]
    backs += [WIN]
    for b, back in enumerate(backs):
        there = bs[lax.rem(me - back + BLOCKS, BLOCKS)] + row
        ok = (there <= place) & (there > place - WINDOW)
        bias[b * TOK : (b + 1) * TOK, :] = jnp.where(ok, 0.0, NEG).astype(BF)
    for lo in range(0, BLOCKS * SLOTS, TOK):
        at = lo + row
        block = at // PIECE * NEAR + (at & (NEAR - 1))
        slot = (at & (PIECE - 1)) // NEAR
        ok = ((bs[0] + TOK * block) & (SEQ - 1)) + (slot + 1) * STRIDE <= place + 1
        bias[RAW + lo : RAW + lo + TOK, :] = jnp.where(ok, 0.0, NEG).astype(BF)


def key_tiles():
    half = SLOTS * BLOCKS // 2
    tiles = [(0, [("own", 0, TOK), ("row1", 0, TOK)])]
    for s in range(1, RING):
        tiles.append((2 * s * TOK, [(s, 0, TOK), (s, TOKP, TOK)]))
    tiles.append((RAW, [("mem", 0, half)]))
    tiles.append((RAW + half, [("mem", half, half)]))
    tiles.append((RAW - TOK, [("row2", 0, TOK)]))
    return [(lo, sum(n for _, _, n in tile), tile) for lo, tile in tiles]


def gather_tile(refs, tile, kind):
    parts = []
    for name, lo, n in tile:
        if name == "mem":
            rows = slice(kind * PIECE, (kind + 1) * PIECE)
            parts += [refs[name][i, rows, :] for i in range(lo // PIECE, (lo + n) // PIECE)]
        else:
            at = lo + kind * TOK
            parts.append(refs[name][at : at + n, :])
    return parts[0] if len(parts) == 1 else jnp.concatenate(parts, axis=0)


def chunk_kernel(off, rotq, bias, own, row1, row2, r1, r2, r3, mem, *rest):
    refs = {"own": own, "row1": row1, "row2": row2, 1: r1, 2: r2, 3: r3, "mem": mem}
    out, s = rest[-2:]
    dest = lax.axis_index("kv") ^ off
    first = pl.multiple_of(dest * ROWS, ROWS)
    heads = HEADS // GROUPS
    r = lax.broadcasted_iota(jnp.int32, (heads * ROWS, TOK), 0) & (ROWS - 1)
    c = lax.broadcasted_iota(jnp.int32, (heads * ROWS, TOK), 1)
    unit = jnp.where(r + first == c, 1.0, 0.0).astype(BF)
    for g in range(GROUPS):
        q = jnp.concatenate(
            [rotq[g * heads + i, pl.ds(first, ROWS), :] for i in range(heads)], axis=0
        )
        qa = jnp.concatenate([q, unit], axis=1)
        high = None
        for lo, size, tile in key_tiles():
            k = gather_tile(refs, tile, g)
            ka = jnp.concatenate([k, bias[lo : lo + size, :]], axis=1)
            x = lax.dot_general(qa, ka, (((1,), (1,)), ((), ())), preferred_element_type=F32)
            s[g, :, lo : lo + size] = x
            for i in range(size // HD):
                part = x[:, i * HD : (i + 1) * HD]
                high = part if high is None else jnp.maximum(high, part)
        top = jnp.max(high, axis=1, keepdims=True)
        mixed = None
        for lo, size, tile in key_tiles():
            w = jnp.exp2((s[g, :, lo : lo + size] - top).astype(BF))
            v = gather_tile(refs, tile, GROUPS + g)
            va = jnp.concatenate([v, jnp.ones((size, HD), BF)], axis=1)
            part = jnp.dot(w, va, preferred_element_type=F32)
            mixed = part if mixed is None else mixed + part
        res = (mixed[:, :HD] / mixed[:, HD:]).astype(BF)
        for i in range(heads):
            h = g * heads + i
            out[:, h * HD : (h + 1) * HD] = res[i * ROWS : (i + 1) * ROWS, :]


def join_kernel(a, b, c, d, out, sem):
    me = lax.axis_index("kv")
    wide = HEADS * HD
    copies = []
    for off, part in enumerate((a, b, c, d)):
        lane = pl.multiple_of((me ^ off) * wide, wide)
        copies.append(pltpu.make_async_copy(part, out.at[:, pl.ds(lane, wide)], sem.at[off]))
    for x in copies:
        x.start()
    for x in copies:
        x.wait()


def call(kernel, out_shape, scratch, flops, spaces, *args, out_space=pltpu.VMEM, grant=32, alias=None):
    multi = isinstance(out_shape, tuple)
    vm = pl.BlockSpec(memory_space=out_space)
    return pl.pallas_call(
        kernel,
        out_shape=out_shape,
        in_specs=[pl.BlockSpec(memory_space=s) for s in spaces],
        out_specs=(vm,) * len(out_shape) if multi else vm,
        scratch_shapes=scratch,
        input_output_aliases=alias or {},
        compiler_params=pltpu.CompilerParams(vmem_limit_bytes=grant * 2**20),
        cost_estimate=pl.CostEstimate(flops=flops, bytes_accessed=2**10, transcendentals=0),
    )(*args)


def shape(*dims, dtype=BF):
    return jax.ShapeDtypeStruct(dims, dtype)


near = [[NEAR * o + p for p in range(NEAR)] for o in range(FAR)]
strided = [[NEAR * o + p for o in range(FAR)] for p in range(NEAR)]
SM, VM, HB = pltpu.SMEM, pltpu.VMEM, pltpu.HBM


def shards(queries, keys, values, block_start, depth_k, point_k, depth_v, point_v):
    freqs = jnp.asarray(yarn_freqs())
    pack = 2 * GROUPS
    params = (block_start, freqs, keys, values, depth_k, point_k, depth_v, point_v)
    own, mem = call(
        prep_kernel,
        (shape(pack * TOK, HD), shape(NEAR, pack * SLOTS, HD)),
        [pltpu.VMEM((TOK, GROUPS, HD), F32), pltpu.VMEM((pack * SLOTS, HD), F32)]
        + [(pltpu.SMEM if i == 0 else pltpu.VMEM)(x.shape, x.dtype) for i, x in enumerate(params)]
        + [pltpu.SemaphoreType.DMA((len(params),))],
        10**9,
        (HB,) * len(params),
        *params,
        grant=60,
    )
    row1, row2 = (
        lax.ppermute(own, "ctx", [((i - d) % BLOCKS, i) for i in range(BLOCKS)])
        for d in (RING, 2 * RING)
    )
    mem = lax.all_to_all(mem, "ctx", 0, 0, axis_index_groups=near)
    bias = call(bias_kernel, shape(KEYS, TOK), [], 10**3, (SM,), block_start)
    *rings, far = call(
        ring_kernel,
        (shape(2 * TOKP, HD),) * (RING - 1) + (shape(FAR, pack * PIECE, HD),),
        [pltpu.VMEM((NEAR, pack * SLOTS, HD), F32)], 10**3, (VM,) * 4,
        own, row1, row2, mem,
    )
    mem = lax.all_to_all(far, "ctx", 0, 0, axis_index_groups=strided)
    turned = {
        s: lax.ppermute(
            rings[s - 1], "ctx", [(i, i // RING * RING + (i + s) % RING) for i in range(BLOCKS)]
        )
        for s in (2, 1, 3)
    }
    rings = [turned[s] for s in (1, 2, 3)]
    rotq = call(
        query_kernel, shape(HEADS, TOK, HD), [pltpu.VMEM((TOK, HEADS, HD), F32)], 10**10,
        (SM, VM, VM, pl.ANY),
        block_start, freqs, queries, turned[2],
    )
    parts = []
    for off in (3, 2, 1, 0):
        after = parts[-2:-1]
        part = call(
            functools.partial(chunk_kernel, off), shape(ROWS, HEADS * HD),
            [pltpu.VMEM((GROUPS, HEADS // GROUPS * ROWS, KEYS), F32)], 10**6,
            (VM,) * 9 + (pl.ANY,) * len(after), rotq, bias, own, row1, row2, *rings, mem, *after,
        )
        if off:
            part = lax.ppermute(part, "kv", [(i, i ^ off) for i in range(KV)])
        parts.append(part)
    return call(
        join_kernel, shape(ROWS, KV * HEADS * HD), [pltpu.SemaphoreType.DMA((KV,))], 10**8,
        (VM,) * 4, *parts[::-1], out_space=HB,
    )


def solution(mesh):
    placed = (
        P("ctx", "kv", None),
        P("ctx", "kv", None),
        P("ctx", "kv", None),
        P(),
        P(),
        P(),
        P(),
        P(),
    )
    return jax.shard_map(
        shards, mesh=mesh, in_specs=placed, out_specs=P(("ctx", "kv"), None), check_vma=False
    )
```

```python
import functools
import math

import jax
import jax.numpy as jnp
import numpy as np
from jax import lax
from jax.experimental import pallas as pl
from jax.experimental.pallas import tpu as pltpu
from jax.sharding import PartitionSpec as P

HD = 128
TOK = 128
STRIDE = 32
SLOTS = TOK // STRIDE
WIN = 8
WINDOW = WIN * TOK
BLOCKS = 128
SEQ = BLOCKS * TOK
HEADS = 16
GROUPS = 2
KV = 4
RING = 4
ORDER = (2, 1, 3)
NEAR = 8
FAR = BLOCKS // NEAR
ROWS = TOK // KV
RAW = (WIN + 1) * TOK
TOKP = 2 * GROUPS * TOK
PIECE = SLOTS * NEAR
KEYS = RAW + BLOCKS * SLOTS
MSCALE = 1.0 + 0.1 * math.log(16.0)
SCALE2 = math.log2(math.e) / math.sqrt(HD)
NEG = -1e30
BF = jnp.bfloat16
F32 = jnp.float32


def yarn_freqs():
    index = np.arange(HD // 2, dtype=np.float32)
    inverse = np.exp(np.float32(-(2.0 / HD) * math.log(500000.0)) * index).astype(np.float32)
    ratio = np.float32(8192.0) * inverse / np.float32(2.0 * math.pi)
    ramp = np.clip((ratio - 1.0) / 31.0, 0.0, 1.0).astype(np.float32)
    freqs = inverse * (ramp + (1.0 - ramp) / np.float32(16.0))
    return np.tile(np.concatenate([freqs, freqs])[None, :], (8, 1)).astype(np.float32)


def turn_tables(place0, freqs):
    places = (place0 + lax.broadcasted_iota(jnp.int32, (TOK, HD), 0)).astype(F32)
    angle = places * freqs
    first = lax.broadcasted_iota(jnp.int32, (TOK, HD), 1) < HD // 2
    sine = jnp.sin(angle)
    return jnp.cos(angle), jnp.where(first, -sine, sine)


def turn(x, cosine, sine, scale=MSCALE):
    return ((x * cosine + pltpu.roll(x, HD // 2, 1) * sine) * scale).astype(BF)


def prep_kernel(bs, freqs, k, v, dk, pk, dv, pv, own, mem, *scratch):
    scr, pool, s_bs, s_freqs, s_k, s_v, s_dk, s_pk, s_dv, s_pv, sem = scratch
    pairs = (
        (bs, s_bs), (freqs, s_freqs), (k, s_k), (v, s_v),
        (dk, s_dk), (pk, s_pk), (dv, s_dv), (pv, s_pv),
    )
    copies = [pltpu.make_async_copy(a, b, sem.at[i]) for i, (a, b) in enumerate(pairs)]
    for c in copies:
        c.start()
    for c in copies:
        c.wait()
    me = lax.axis_index("ctx")
    cosine, sine = turn_tables(s_bs[me], s_freqs[0:1, :])
    scr[...] = s_k[...].astype(F32)
    for g in range(GROUPS):
        rot = turn(scr[:, g, :], cosine, sine)
        own[g * TOK : (g + 1) * TOK, :] = rot
        grouped = rot.astype(F32).reshape(SLOTS, STRIDE, HD)
        pool[g * SLOTS : (g + 1) * SLOTS, :] = jnp.sum(grouped * s_dk[...][None], axis=1)
    scr[...] = s_v[...].astype(F32)
    for g in range(GROUPS):
        val = scr[:, g, :]
        own[(GROUPS + g) * TOK : (GROUPS + g + 1) * TOK, :] = val.astype(BF)
        grouped = val.reshape(SLOTS, STRIDE, HD)
        at = (GROUPS + g) * SLOTS
        pool[at : at + SLOTS, :] = jnp.sum(grouped * s_dv[...][None], axis=1)
    half = GROUPS * SLOTS
    mk = jnp.dot(pool[:half, :], s_pk[...], precision=lax.Precision.HIGHEST, preferred_element_type=F32)
    mv = jnp.dot(pool[half:, :], s_pv[...], precision=lax.Precision.HIGHEST, preferred_element_type=F32)
    both = jnp.concatenate([mk, mv], axis=0).astype(BF)
    mem[...] = jnp.broadcast_to(both[None], mem.shape)


def query_kernel(bs, freqs, q, rotq, scr):
    me = lax.axis_index("ctx")
    cosine, sine = turn_tables(bs[me], freqs[0:1, :])
    scr[...] = q[...].astype(F32)
    for h in range(HEADS):
        rotq[h] = turn(scr[:, h, :], cosine, sine, MSCALE * SCALE2)


def ring_kernel(own, row1, row2, mem, ra, rb, rc, far, scr):
    me = lax.rem(lax.axis_index("ctx"), RING)
    scr[...] = mem[...].astype(F32)
    kinds = 2 * GROUPS * SLOTS
    slots = jnp.concatenate([scr[:, r, :] for r in range(kinds)], axis=0).astype(BF)
    far[...] = jnp.broadcast_to(slots[None], far.shape)
    for s, out in zip(ORDER, (ra, rb, rc)):
        out[TOKP:, :] = row1[...]

        @pl.when(me + s < RING)
        def _():
            out[:TOKP, :] = own[...]

        @pl.when(me + s >= RING)
        def _():
            out[:TOKP, :] = row2[...]


def bias_kernel(bs, bias):
    me = lax.axis_index("ctx")
    pos = lax.rem(me, RING)
    place = bs[me] + lax.broadcasted_iota(jnp.int32, (TOK, TOK), 1)
    row = lax.broadcasted_iota(jnp.int32, (TOK, TOK), 0)
    backs = [0, RING]
    for s in range(1, RING):
        wrapped = pos < s
        backs += [jnp.where(wrapped, RING + s, s), jnp.where(wrapped, s, RING + s)]
    backs += [WIN]
    for b, back in enumerate(backs):
        there = bs[lax.rem(me - back + BLOCKS, BLOCKS)] + row
        ok = (there <= place) & (there > place - WINDOW)
        bias[b * TOK : (b + 1) * TOK, :] = jnp.where(ok, 0.0, NEG).astype(BF)
    for lo in range(0, BLOCKS * SLOTS, TOK):
        at = lo + row
        block = at // PIECE * NEAR + (at & (NEAR - 1))
        slot = (at & (PIECE - 1)) // NEAR
        ok = ((bs[0] + TOK * block) & (SEQ - 1)) + (slot + 1) * STRIDE <= place + 1
        bias[RAW + lo : RAW + lo + TOK, :] = jnp.where(ok, 0.0, NEG).astype(BF)


def key_tiles():
    half = SLOTS * BLOCKS // 2
    tiles = [(0, [("own", 0, TOK), ("row1", 0, TOK)])]
    for s in range(1, RING):
        tiles.append((2 * s * TOK, [(s, 0, TOK), (s, TOKP, TOK)]))
    tiles.append((RAW, [("mem", 0, half)]))
    tiles.append((RAW + half, [("mem", half, half)]))
    tiles.append((RAW - TOK, [("row2", 0, TOK)]))
    return [(lo, sum(n for _, _, n in tile), tile) for lo, tile in tiles]


def gather_tile(refs, tile, kind):
    parts = []
    for name, lo, n in tile:
        if name == "mem":
            rows = slice(kind * PIECE, (kind + 1) * PIECE)
            parts += [refs[name][i, rows, :] for i in range(lo // PIECE, (lo + n) // PIECE)]
        else:
            at = lo + kind * TOK
            parts.append(refs[name][at : at + n, :])
    return parts[0] if len(parts) == 1 else jnp.concatenate(parts, axis=0)


def chunk_kernel(offs, rotq, bias, own, row1, row2, r1, r2, r3, mem, *rest):
    refs = {"own": own, "row1": row1, "row2": row2, 1: r1, 2: r2, 3: r3, "mem": mem}
    outs, s = rest[-1 - len(offs) : -1], rest[-1]
    firsts = [pl.multiple_of((lax.axis_index("kv") ^ o) * ROWS, ROWS) for o in offs]
    heads = HEADS // GROUPS
    r = lax.broadcasted_iota(jnp.int32, (heads * ROWS, TOK), 0) & (ROWS - 1)
    c = lax.broadcasted_iota(jnp.int32, (heads * ROWS, TOK), 1)
    unit = jnp.concatenate([jnp.where(r + f == c, 1.0, 0.0).astype(BF) for f in firsts], axis=0)
    for g in range(GROUPS):
        q = jnp.concatenate(
            [rotq[g * heads + i, pl.ds(f, ROWS), :] for f in firsts for i in range(heads)], axis=0
        )
        qa = jnp.concatenate([q, unit], axis=1)
        high = None
        for lo, size, tile in key_tiles():
            k = gather_tile(refs, tile, g)
            ka = jnp.concatenate([k, bias[lo : lo + size, :]], axis=1)
            x = lax.dot_general(qa, ka, (((1,), (1,)), ((), ())), preferred_element_type=F32)
            s[g, :, lo : lo + size] = x
            for i in range(size // HD):
                part = x[:, i * HD : (i + 1) * HD]
                high = part if high is None else jnp.maximum(high, part)
        top = jnp.max(high, axis=1, keepdims=True)
        mixed = None
        for lo, size, tile in key_tiles():
            w = jnp.exp2(s[g, :, lo : lo + size] - top).astype(BF)
            v = gather_tile(refs, tile, GROUPS + g)
            va = jnp.concatenate([v, jnp.ones((size, HD), BF)], axis=1)
            part = jnp.dot(w, va, preferred_element_type=F32)
            mixed = part if mixed is None else mixed + part
        res = (mixed[:, :HD] / mixed[:, HD:]).astype(BF)
        for n, out in enumerate(outs):
            for i in range(heads):
                h, at = g * heads + i, (n * heads + i) * ROWS
                out[:, h * HD : (h + 1) * HD] = res[at : at + ROWS, :]


def join_kernel(a, b, c, d, out, sem):
    me = lax.axis_index("kv")
    wide = HEADS * HD
    copies = []
    for off, part in enumerate((a, b, c, d)):
        lane = pl.multiple_of((me ^ off) * wide, wide)
        copies.append(pltpu.make_async_copy(part, out.at[:, pl.ds(lane, wide)], sem.at[off]))
    for x in copies:
        x.start()
    for x in copies:
        x.wait()


def call(kernel, out_shape, scratch, flops, spaces, *args, out_space=pltpu.VMEM, grant=32, alias=None):
    multi = isinstance(out_shape, tuple)
    vm = pl.BlockSpec(memory_space=out_space)
    return pl.pallas_call(
        kernel,
        out_shape=out_shape,
        in_specs=[pl.BlockSpec(memory_space=s) for s in spaces],
        out_specs=(vm,) * len(out_shape) if multi else vm,
        scratch_shapes=scratch,
        input_output_aliases=alias or {},
        compiler_params=pltpu.CompilerParams(vmem_limit_bytes=grant * 2**20),
        cost_estimate=pl.CostEstimate(flops=flops, bytes_accessed=2**10, transcendentals=0),
    )(*args)


def shape(*dims, dtype=BF):
    return jax.ShapeDtypeStruct(dims, dtype)


near = [[NEAR * o + p for p in range(NEAR)] for o in range(FAR)]
strided = [[NEAR * o + p for o in range(FAR)] for p in range(NEAR)]
SM, VM, HB = pltpu.SMEM, pltpu.VMEM, pltpu.HBM


def shards(queries, keys, values, block_start, depth_k, point_k, depth_v, point_v):
    freqs = jnp.asarray(yarn_freqs())
    pack = 2 * GROUPS
    params = (block_start, freqs, keys, values, depth_k, point_k, depth_v, point_v)
    own, mem = call(
        prep_kernel,
        (shape(pack * TOK, HD), shape(NEAR, pack * SLOTS, HD)),
        [pltpu.VMEM((TOK, GROUPS, HD), F32), pltpu.VMEM((pack * SLOTS, HD), F32)]
        + [(pltpu.SMEM if i == 0 else pltpu.VMEM)(x.shape, x.dtype) for i, x in enumerate(params)]
        + [pltpu.SemaphoreType.DMA((len(params),))],
        10**9,
        (HB,) * len(params),
        *params,
        grant=60,
    )
    row1, row2 = (
        lax.ppermute(own, "ctx", [((i - d) % BLOCKS, i) for i in range(BLOCKS)])
        for d in (RING, 2 * RING)
    )
    mem = lax.all_to_all(mem, "ctx", 0, 0, axis_index_groups=near)
    rotq = call(
        query_kernel, shape(HEADS, TOK, HD), [pltpu.VMEM((TOK, HEADS, HD), F32)], 10**3,
        (SM, VM, VM),
        block_start, freqs, queries,
    )
    bias = call(bias_kernel, shape(KEYS, TOK), [], 10**3, (SM,), block_start)
    *rings, far = call(
        ring_kernel,
        (shape(2 * TOKP, HD),) * (RING - 1) + (shape(FAR, pack * PIECE, HD),),
        [pltpu.VMEM((NEAR, pack * SLOTS, HD), F32)], 10**3, (VM,) * 4,
        own, row1, row2, mem,
    )
    mem = lax.all_to_all(far, "ctx", 0, 0, axis_index_groups=strided)
    turned = {
        s: lax.ppermute(
            x, "ctx", [(i, i // RING * RING + (i + s) % RING) for i in range(BLOCKS)]
        )
        for s, x in zip(ORDER, rings)
    }
    rings = [turned[s] for s in (1, 2, 3)]
    parts = {}
    part = None
    for offs in ((3, 2), (1, 0)):
        got = call(
            functools.partial(chunk_kernel, offs), (shape(ROWS, HEADS * HD),) * len(offs),
            [pltpu.VMEM((GROUPS, len(offs) * HEADS // GROUPS * ROWS, KEYS), F32)], 10**6,
            (VM,) * 9 + (pl.ANY,) * (part is not None),
            rotq, bias, own, row1, row2, *rings, mem, *([] if part is None else [part]),
        )
        for off, part in zip(offs, got):
            if off:
                part = lax.ppermute(part, "kv", [(i, i ^ off) for i in range(KV)])
            parts[off] = part
        part = parts[offs[0]]
    return call(
        join_kernel, shape(ROWS, KV * HEADS * HD), [pltpu.SemaphoreType.DMA((KV,))], 10**8,
        (VM,) * 4, *(parts[i] for i in range(KV)), out_space=HB,
    )


def solution(mesh):
    placed = (
        P("ctx", "kv", None),
        P("ctx", "kv", None),
        P("ctx", "kv", None),
        P(),
        P(),
        P(),
        P(),
        P(),
    )
    return jax.shard_map(
        shards, mesh=mesh, in_specs=placed, out_specs=P(("ctx", "kv"), None), check_vma=False
    )
```

```python
import functools
import math

import jax
import jax.numpy as jnp
import numpy as np
from jax import lax
from jax.experimental import pallas as pl
from jax.experimental.pallas import tpu as pltpu
from jax.sharding import PartitionSpec as P

HD = 128
TOK = 128
STRIDE = 32
SLOTS = TOK // STRIDE
WIN = 8
WINDOW = WIN * TOK
BLOCKS = 128
SEQ = BLOCKS * TOK
HEADS = 16
GROUPS = 2
KV = 4
OCT = 8
NOCT = BLOCKS // OCT
ROWS = TOK // KV
RAW = (WIN + 1) * TOK
MANY = SLOTS * NOCT
KEYS = RAW + BLOCKS * SLOTS
TILE = 256
MSCALE = 1.0 + 0.1 * math.log(16.0)
SCALE2 = math.log2(math.e) / math.sqrt(HD)
NEG = -1e30
BF = jnp.bfloat16
F32 = jnp.float32


def yarn_freqs():
    index = np.arange(HD // 2, dtype=np.float32)
    inverse = np.exp(np.float32(-(2.0 / HD) * math.log(500000.0)) * index).astype(np.float32)
    ratio = np.float32(8192.0) * inverse / np.float32(2.0 * math.pi)
    ramp = np.clip((ratio - 1.0) / 31.0, 0.0, 1.0).astype(np.float32)
    freqs = inverse * (ramp + (1.0 - ramp) / np.float32(16.0))
    return np.tile(np.concatenate([freqs, freqs])[None, :], (8, 1)).astype(np.float32)


def turn_tables(place0, freqs):
    places = (place0 + lax.broadcasted_iota(jnp.int32, (TOK, HD), 0)).astype(F32)
    angle = places * freqs
    first = lax.broadcasted_iota(jnp.int32, (TOK, HD), 1) < HD // 2
    sine = jnp.sin(angle)
    return jnp.cos(angle), jnp.where(first, -sine, sine)


def turn(x, cosine, sine):
    return ((x * cosine + pltpu.roll(x, HD // 2, 1) * sine) * MSCALE).astype(BF)


def prep_kernel(bs, freqs, k, v, dk, pk, dv, pv, own, mem, *scratch):
    scr, pool, s_bs, s_freqs, s_k, s_v, s_dk, s_pk, s_dv, s_pv, sem = scratch
    pairs = (
        (bs, s_bs), (freqs, s_freqs), (k, s_k), (v, s_v),
        (dk, s_dk), (pk, s_pk), (dv, s_dv), (pv, s_pv),
    )
    copies = [pltpu.make_async_copy(a, b, sem.at[i]) for i, (a, b) in enumerate(pairs)]
    for c in copies:
        c.start()
    for c in copies:
        c.wait()
    me = lax.axis_index("ctx")
    cosine, sine = turn_tables(s_bs[me], s_freqs[0:1, :])
    scr[...] = s_k[...].astype(F32)
    for g in range(GROUPS):
        rot = turn(scr[:, g, :], cosine, sine)
        own[g * TOK : (g + 1) * TOK, :] = rot
        grouped = rot.astype(F32).reshape(SLOTS, STRIDE, HD)
        pool[g * SLOTS : (g + 1) * SLOTS, :] = jnp.sum(grouped * s_dk[...][None], axis=1)
    scr[...] = s_v[...].astype(F32)
    for g in range(GROUPS):
        val = scr[:, g, :]
        own[(GROUPS + g) * TOK : (GROUPS + g + 1) * TOK, :] = val.astype(BF)
        grouped = val.reshape(SLOTS, STRIDE, HD)
        at = (GROUPS + g) * SLOTS
        pool[at : at + SLOTS, :] = jnp.sum(grouped * s_dv[...][None], axis=1)
    half = GROUPS * SLOTS
    mk = jnp.dot(pool[:half, :], s_pk[...], precision=lax.Precision.HIGHEST, preferred_element_type=F32)
    mv = jnp.dot(pool[half:, :], s_pv[...], precision=lax.Precision.HIGHEST, preferred_element_type=F32)
    both = jnp.concatenate([mk, mv], axis=0).astype(BF)
    mem[...] = jnp.broadcast_to(both[None], mem.shape)


def query_kernel(bs, freqs, q, rotq, scr):
    me = lax.axis_index("ctx")
    cosine, sine = turn_tables(bs[me], freqs[0:1, :])
    scr[...] = q[...].astype(F32)
    for h in range(HEADS):
        rotq[h] = turn(scr[:, h, :], cosine, sine)


def raw_kernel(own, prev, rotq, bias, out):
    me = lax.rem(lax.axis_index("ctx"), OCT)
    raw = own.shape[0]
    for d in range(OCT):

        @pl.when(me <= d)
        def _():
            out[d, :raw, :] = own[...]

        @pl.when(me > d)
        def _():
            out[d, :raw, :] = prev[...]


def slot_kernel(mem, sent, out, scr):
    scr[...] = mem[...].astype(F32)
    kinds = 2 * GROUPS * SLOTS
    slots = jnp.concatenate([scr[:, r, :] for r in range(kinds)], axis=0).astype(BF)
    raw = 2 * GROUPS * TOK
    for d in range(OCT):
        out[d, raw:, :] = slots


def bias_kernel(bs, bias):
    me = lax.axis_index("ctx")
    pos = lax.rem(me, OCT)
    place = bs[me] + lax.broadcasted_iota(jnp.int32, (TOK, TOK), 1)
    row = lax.broadcasted_iota(jnp.int32, (TOK, TOK), 0)
    for b in range(WIN + 1):
        back = WIN if b == WIN else lax.rem(pos - b + OCT, OCT)
        there = bs[lax.rem(me - back + BLOCKS, BLOCKS)] + row
        ok = (there <= place) & (there > place - WINDOW)
        bias[b * TOK : (b + 1) * TOK, :] = jnp.where(ok, 0.0, NEG).astype(BF)
    slot = lax.broadcasted_iota(jnp.int32, (MANY, TOK), 0) // NOCT
    octet = lax.broadcasted_iota(jnp.int32, (MANY, TOK), 0) & (NOCT - 1)
    place = bs[me] + lax.broadcasted_iota(jnp.int32, (MANY, TOK), 1)
    for p in range(OCT):
        end = ((bs[p] + OCT * TOK * octet) & (SEQ - 1)) + (slot + 1) * STRIDE
        lo = RAW + p * MANY
        bias[lo : lo + MANY, :] = jnp.where(end <= place + 1, 0.0, NEG).astype(BF)


def key_tiles():
    raw = [("r", b) for b in range(OCT)] + [("p", 0)]
    rows = [(x, TOK) for x in raw] + [(("m", p), MANY) for p in range(OCT)]
    tiles, tile, size, lo, start = [], [], 0, 0, 0
    for x, n in rows:
        tile.append(x)
        size += n
        if size == TILE or x == ("m", OCT - 1):
            tiles.append((lo, size, tile))
            lo, size, tile = lo + size, 0, []
    return tiles


def gather_tile(recv, prev, tile, raw_at, slot_at):
    parts = []
    for kind, i in tile:
        if kind == "r":
            parts.append(recv[i, raw_at : raw_at + TOK, :])
        elif kind == "p":
            parts.append(prev[raw_at : raw_at + TOK, :])
        else:
            parts.append(recv[i, slot_at : slot_at + MANY, :])
    return jnp.concatenate(parts, axis=0)


def chunk_kernel(offs, rotq, bias, recv, prev, *rest):
    outs, s = rest[:-1], rest[-1]
    firsts = [pl.multiple_of((lax.axis_index("kv") ^ o) * ROWS, ROWS) for o in offs]
    heads = HEADS // GROUPS
    r = lax.broadcasted_iota(jnp.int32, (heads * ROWS, TOK), 0) & (ROWS - 1)
    c = lax.broadcasted_iota(jnp.int32, (heads * ROWS, TOK), 1)
    unit = jnp.concatenate([jnp.where(r + f == c, 1.0, 0.0).astype(BF) for f in firsts], axis=0)
    slots = 2 * GROUPS * TOK
    tops = []
    for g in range(GROUPS):
        q = jnp.concatenate(
            [rotq[g * heads + i, pl.ds(f, ROWS), :] for f in firsts for i in range(heads)], axis=0
        )
        qa = jnp.concatenate([q, unit], axis=1)
        high = None
        for lo, size, tile in key_tiles():
            k = gather_tile(recv, prev, tile, g * TOK, slots + g * MANY)
            ka = jnp.concatenate([k, bias[lo : lo + size, :]], axis=1)
            x = lax.dot_general(qa, ka, (((1,), (1,)), ((), ())), preferred_element_type=F32)
            s[g, :, lo : lo + size] = x
            for i in range(size // HD):
                part = x[:, i * HD : (i + 1) * HD]
                high = part if high is None else jnp.maximum(high, part)
        tops.append(jnp.max(high, axis=1, keepdims=True))
    for g in range(GROUPS):
        mixed = None
        for lo, size, tile in key_tiles():
            w = jnp.exp2((s[g, :, lo : lo + size] - tops[g]) * SCALE2).astype(BF)
            v = gather_tile(recv, prev, tile, (GROUPS + g) * TOK, slots + (GROUPS + g) * MANY)
            va = jnp.concatenate([v, jnp.ones((size, HD), BF)], axis=1)
            part = jnp.dot(w, va, preferred_element_type=F32)
            mixed = part if mixed is None else mixed + part
        res = (mixed[:, :HD] / mixed[:, HD:]).astype(BF)
        for n, out in enumerate(outs):
            for i in range(heads):
                h, at = g * heads + i, (n * heads + i) * ROWS
                out[:, h * HD : (h + 1) * HD] = res[at : at + ROWS, :]


def join_kernel(a, b, c, d, out, sem):
    me = lax.axis_index("kv")
    wide = HEADS * HD
    copies = []
    for off, part in enumerate((a, b, c, d)):
        lane = pl.multiple_of((me ^ off) * wide, wide)
        copies.append(pltpu.make_async_copy(part, out.at[:, pl.ds(lane, wide)], sem.at[off]))
    for x in copies:
        x.start()
    for x in copies:
        x.wait()


def call(kernel, out_shape, scratch, flops, spaces, *args, out_space=pltpu.VMEM, grant=32, alias=None):
    multi = isinstance(out_shape, tuple)
    vm = pl.BlockSpec(memory_space=out_space)
    return pl.pallas_call(
        kernel,
        out_shape=out_shape,
        in_specs=[pl.BlockSpec(memory_space=s) for s in spaces],
        out_specs=(vm,) * len(out_shape) if multi else vm,
        scratch_shapes=scratch,
        input_output_aliases=alias or {},
        compiler_params=pltpu.CompilerParams(vmem_limit_bytes=grant * 2**20),
        cost_estimate=pl.CostEstimate(flops=flops, bytes_accessed=2**10, transcendentals=0),
    )(*args)


def shape(*dims, dtype=BF):
    return jax.ShapeDtypeStruct(dims, dtype)


octets = [[OCT * o + p for p in range(OCT)] for o in range(NOCT)]
strided = [[OCT * o + p for o in range(NOCT)] for p in range(OCT)]
SM, VM, HB = pltpu.SMEM, pltpu.VMEM, pltpu.HBM


def shards(queries, keys, values, block_start, depth_k, point_k, depth_v, point_v):
    freqs = jnp.asarray(yarn_freqs())
    pack = 2 * GROUPS
    params = (block_start, freqs, keys, values, depth_k, point_k, depth_v, point_v)
    own, mem = call(
        prep_kernel,
        (shape(pack * TOK, HD), shape(NOCT, pack * SLOTS, HD)),
        [pltpu.VMEM((TOK, GROUPS, HD), F32), pltpu.VMEM((pack * SLOTS, HD), F32)]
        + [(pltpu.SMEM if i == 0 else pltpu.VMEM)(x.shape, x.dtype) for i, x in enumerate(params)]
        + [pltpu.SemaphoreType.DMA((len(params),))],
        10**9,
        (HB,) * len(params),
        *params,
        grant=60,
    )
    prev = lax.ppermute(own, "ctx", [((i - WIN) % BLOCKS, i) for i in range(BLOCKS)])
    mem = lax.all_to_all(mem, "ctx", 0, 0, axis_index_groups=strided)
    rotq = call(
        query_kernel, shape(HEADS, TOK, HD), [pltpu.VMEM((TOK, HEADS, HD), F32)], 10**9,
        (SM, VM, VM),
        block_start, freqs, queries,
    )
    bias = call(bias_kernel, shape(KEYS, TOK), [], 10**8, (SM,), block_start)
    rows = pack * TOK + pack * MANY
    sent = call(
        raw_kernel, shape(OCT, rows, HD), [], 10**8, (VM, VM, pl.ANY, pl.ANY), own, prev, rotq, bias
    )
    sent = call(
        slot_kernel, shape(OCT, rows, HD), [pltpu.VMEM((NOCT, pack * SLOTS, HD), F32)], 10**8,
        (VM, VM), mem, sent, alias={1: 0},
    )
    recv = lax.all_to_all(sent, "ctx", 0, 0, axis_index_groups=octets)
    parts = {}
    for offs in ((3, 2), (1, 0)):
        got = call(
            functools.partial(chunk_kernel, offs), (shape(ROWS, HEADS * HD),) * len(offs),
            [pltpu.VMEM((GROUPS, len(offs) * HEADS // GROUPS * ROWS, KEYS), F32)], 10**6,
            (VM,) * 4, rotq, bias, recv, prev,
        )
        for off, part in zip(offs, got):
            if off:
                part = lax.ppermute(part, "kv", [(i, i ^ off) for i in range(KV)])
            parts[off] = part
    return call(
        join_kernel, shape(ROWS, KV * HEADS * HD), [pltpu.SemaphoreType.DMA((KV,))], 10**8,
        (VM,) * 4, *(parts[i] for i in range(KV)), out_space=HB,
    )


def solution(mesh):
    placed = (
        P("ctx", "kv", None),
        P("ctx", "kv", None),
        P("ctx", "kv", None),
        P(),
        P(),
        P(),
        P(),
        P(),
    )
    return jax.shard_map(
        shards, mesh=mesh, in_specs=placed, out_specs=P(("ctx", "kv"), None), check_vma=False
    )
```

```python
import functools
import math

import jax
import jax.numpy as jnp
import numpy as np
from jax import lax
from jax.experimental import pallas as pl
from jax.experimental.pallas import tpu as pltpu
from jax.sharding import PartitionSpec as P

HD = 128
TOK = 128
STRIDE = 32
SLOTS = TOK // STRIDE
WIN = 8
WINDOW = WIN * TOK
BLOCKS = 128
SEQ = BLOCKS * TOK
HEADS = 16
GROUPS = 2
KV = 4
RING = 4
ORDER = (2, 1, 3)
NEAR = 8
FAR = BLOCKS // NEAR
ROWS = TOK // KV
RAW = (WIN + 1) * TOK
TOKP = 2 * GROUPS * TOK
PIECE = SLOTS * NEAR
KEYS = RAW + BLOCKS * SLOTS
MSCALE = 1.0 + 0.1 * math.log(16.0)
SCALE2 = math.log2(math.e) / math.sqrt(HD)
NEG = -1e30
BF = jnp.bfloat16
F32 = jnp.float32


def yarn_freqs():
    index = np.arange(HD // 2, dtype=np.float32)
    inverse = np.exp(np.float32(-(2.0 / HD) * math.log(500000.0)) * index).astype(np.float32)
    ratio = np.float32(8192.0) * inverse / np.float32(2.0 * math.pi)
    ramp = np.clip((ratio - 1.0) / 31.0, 0.0, 1.0).astype(np.float32)
    freqs = inverse * (ramp + (1.0 - ramp) / np.float32(16.0))
    return np.tile(np.concatenate([freqs, freqs])[None, :], (8, 1)).astype(np.float32)


def turn_tables(place0, freqs):
    places = (place0 + lax.broadcasted_iota(jnp.int32, (TOK, HD), 0)).astype(F32)
    angle = places * freqs
    first = lax.broadcasted_iota(jnp.int32, (TOK, HD), 1) < HD // 2
    sine = jnp.sin(angle)
    return jnp.cos(angle), jnp.where(first, -sine, sine)


def turn(x, cosine, sine, scale=MSCALE):
    return ((x * cosine + pltpu.roll(x, HD // 2, 1) * sine) * scale).astype(BF)


def prep_kernel(bs, freqs, k, v, dk, pk, dv, pv, own, mem, *scratch):
    scr, pool, s_bs, s_freqs, s_k, s_v, s_dk, s_pk, s_dv, s_pv, sem = scratch
    pairs = (
        (bs, s_bs), (freqs, s_freqs), (k, s_k), (v, s_v),
        (dk, s_dk), (pk, s_pk), (dv, s_dv), (pv, s_pv),
    )
    copies = [pltpu.make_async_copy(a, b, sem.at[i]) for i, (a, b) in enumerate(pairs)]
    for c in copies:
        c.start()
    for c in copies:
        c.wait()
    me = lax.axis_index("ctx")
    cosine, sine = turn_tables(s_bs[me], s_freqs[0:1, :])
    scr[...] = s_k[...].astype(F32)
    for g in range(GROUPS):
        rot = turn(scr[:, g, :], cosine, sine)
        own[g * TOK : (g + 1) * TOK, :] = rot
        grouped = rot.astype(F32).reshape(SLOTS, STRIDE, HD)
        pool[g * SLOTS : (g + 1) * SLOTS, :] = jnp.sum(grouped * s_dk[...][None], axis=1)
    scr[...] = s_v[...].astype(F32)
    for g in range(GROUPS):
        val = scr[:, g, :]
        own[(GROUPS + g) * TOK : (GROUPS + g + 1) * TOK, :] = val.astype(BF)
        grouped = val.reshape(SLOTS, STRIDE, HD)
        at = (GROUPS + g) * SLOTS
        pool[at : at + SLOTS, :] = jnp.sum(grouped * s_dv[...][None], axis=1)
    half = GROUPS * SLOTS
    mk = jnp.dot(pool[:half, :], s_pk[...], precision=lax.Precision.HIGHEST, preferred_element_type=F32)
    mv = jnp.dot(pool[half:, :], s_pv[...], precision=lax.Precision.HIGHEST, preferred_element_type=F32)
    both = jnp.concatenate([mk, mv], axis=0).astype(BF)
    mem[...] = jnp.broadcast_to(both[None], mem.shape)


def query_kernel(bs, freqs, q, rotq, scr):
    me = lax.axis_index("ctx")
    cosine, sine = turn_tables(bs[me], freqs[0:1, :])
    scr[...] = q[...].astype(F32)
    for h in range(HEADS):
        rotq[h] = turn(scr[:, h, :], cosine, sine)


def far_kernel(mem, row1, row2, far, scr):
    scr[...] = mem[...].astype(F32)
    kinds = 2 * GROUPS * SLOTS
    slots = jnp.concatenate([scr[:, r, :] for r in range(kinds)], axis=0).astype(BF)
    far[...] = jnp.broadcast_to(slots[None], far.shape)


def ring_kernel(own, row1, row2, far, ra, rb, rc):
    me = lax.rem(lax.axis_index("ctx"), RING)
    for s, out in zip(ORDER, (ra, rb, rc)):
        out[TOKP:, :] = row1[...]

        @pl.when(me + s < RING)
        def _():
            out[:TOKP, :] = own[...]

        @pl.when(me + s >= RING)
        def _():
            out[:TOKP, :] = row2[...]


def bias_kernel(bs, bias):
    me = lax.axis_index("ctx")
    pos = lax.rem(me, RING)
    place = bs[me] + lax.broadcasted_iota(jnp.int32, (TOK, TOK), 1)
    row = lax.broadcasted_iota(jnp.int32, (TOK, TOK), 0)
    backs = [0, RING]
    for s in range(1, RING):
        wrapped = pos < s
        backs += [jnp.where(wrapped, RING + s, s), jnp.where(wrapped, s, RING + s)]
    backs += [WIN]
    for b, back in enumerate(backs):
        there = bs[lax.rem(me - back + BLOCKS, BLOCKS)] + row
        ok = (there <= place) & (there > place - WINDOW)
        bias[b * TOK : (b + 1) * TOK, :] = jnp.where(ok, 0.0, NEG).astype(BF)
    for lo in range(0, BLOCKS * SLOTS, TOK):
        at = lo + row
        block = at // PIECE * NEAR + (at & (NEAR - 1))
        slot = (at & (PIECE - 1)) // NEAR
        ok = ((bs[0] + TOK * block) & (SEQ - 1)) + (slot + 1) * STRIDE <= place + 1
        bias[RAW + lo : RAW + lo + TOK, :] = jnp.where(ok, 0.0, NEG).astype(BF)


def key_tiles():
    half = SLOTS * BLOCKS // 2
    tiles = [(0, [("own", 0, TOK), ("row1", 0, TOK)])]
    for s in range(1, RING):
        tiles.append((2 * s * TOK, [(s, 0, TOK), (s, TOKP, TOK)]))
    tiles.append((RAW, [("mem", 0, half)]))
    tiles.append((RAW + half, [("mem", half, half)]))
    tiles.append((RAW - TOK, [("row2", 0, TOK)]))
    return [(lo, sum(n for _, _, n in tile), tile) for lo, tile in tiles]


def gather_tile(refs, tile, kind):
    parts = []
    for name, lo, n in tile:
        if name == "mem":
            rows = slice(kind * PIECE, (kind + 1) * PIECE)
            parts += [refs[name][i, rows, :] for i in range(lo // PIECE, (lo + n) // PIECE)]
        else:
            at = lo + kind * TOK
            parts.append(refs[name][at : at + n, :])
    return parts[0] if len(parts) == 1 else jnp.concatenate(parts, axis=0)


def chunk_kernel(offs, rotq, bias, own, row1, row2, r1, r2, r3, mem, *rest):
    refs = {"own": own, "row1": row1, "row2": row2, 1: r1, 2: r2, 3: r3, "mem": mem}
    outs, s = rest[:-1], rest[-1]
    firsts = [pl.multiple_of((lax.axis_index("kv") ^ o) * ROWS, ROWS) for o in offs]
    heads = HEADS // GROUPS
    r = lax.broadcasted_iota(jnp.int32, (heads * ROWS, TOK), 0) & (ROWS - 1)
    c = lax.broadcasted_iota(jnp.int32, (heads * ROWS, TOK), 1)
    unit = jnp.concatenate([jnp.where(r + f == c, 1.0, 0.0).astype(BF) for f in firsts], axis=0)
    tops = []
    for g in range(GROUPS):
        q = jnp.concatenate(
            [rotq[g * heads + i, pl.ds(f, ROWS), :] for f in firsts for i in range(heads)], axis=0
        )
        qa = jnp.concatenate([q, unit], axis=1)
        high = None
        for lo, size, tile in key_tiles():
            k = gather_tile(refs, tile, g)
            ka = jnp.concatenate([k, bias[lo : lo + size, :]], axis=1)
            x = lax.dot_general(qa, ka, (((1,), (1,)), ((), ())), preferred_element_type=F32)
            s[g, :, lo : lo + size] = x
            for i in range(size // HD):
                part = x[:, i * HD : (i + 1) * HD]
                high = part if high is None else jnp.maximum(high, part)
        tops.append(jnp.max(high, axis=1, keepdims=True))
    for g in range(GROUPS):
        mixed = None
        for lo, size, tile in key_tiles():
            w = jnp.exp2((s[g, :, lo : lo + size] - tops[g]) * SCALE2).astype(BF)
            v = gather_tile(refs, tile, GROUPS + g)
            va = jnp.concatenate([v, jnp.ones((size, HD), BF)], axis=1)
            part = jnp.dot(w, va, preferred_element_type=F32)
            mixed = part if mixed is None else mixed + part
        res = (mixed[:, :HD] / mixed[:, HD:]).astype(BF)
        for n, out in enumerate(outs):
            for i in range(heads):
                h, at = g * heads + i, (n * heads + i) * ROWS
                out[:, h * HD : (h + 1) * HD] = res[at : at + ROWS, :]


def join_kernel(a, b, c, d, out, sem):
    me = lax.axis_index("kv")
    wide = HEADS * HD
    copies = []
    for off, part in enumerate((a, b, c, d)):
        lane = pl.multiple_of((me ^ off) * wide, wide)
        copies.append(pltpu.make_async_copy(part, out.at[:, pl.ds(lane, wide)], sem.at[off]))
    for x in copies:
        x.start()
    for x in copies:
        x.wait()


def call(kernel, out_shape, scratch, flops, spaces, *args, out_space=pltpu.VMEM, grant=32, alias=None):
    multi = isinstance(out_shape, tuple)
    vm = pl.BlockSpec(memory_space=out_space)
    return pl.pallas_call(
        kernel,
        out_shape=out_shape,
        in_specs=[pl.BlockSpec(memory_space=s) for s in spaces],
        out_specs=(vm,) * len(out_shape) if multi else vm,
        scratch_shapes=scratch,
        input_output_aliases=alias or {},
        compiler_params=pltpu.CompilerParams(vmem_limit_bytes=grant * 2**20),
        cost_estimate=pl.CostEstimate(flops=flops, bytes_accessed=2**10, transcendentals=0),
    )(*args)


def shape(*dims, dtype=BF):
    return jax.ShapeDtypeStruct(dims, dtype)


near = [[NEAR * o + p for p in range(NEAR)] for o in range(FAR)]
strided = [[NEAR * o + p for o in range(FAR)] for p in range(NEAR)]
SM, VM, HB = pltpu.SMEM, pltpu.VMEM, pltpu.HBM


def shards(queries, keys, values, block_start, depth_k, point_k, depth_v, point_v):
    freqs = jnp.asarray(yarn_freqs())
    pack = 2 * GROUPS
    params = (block_start, freqs, keys, values, depth_k, point_k, depth_v, point_v)
    own, mem = call(
        prep_kernel,
        (shape(pack * TOK, HD), shape(NEAR, pack * SLOTS, HD)),
        [pltpu.VMEM((TOK, GROUPS, HD), F32), pltpu.VMEM((pack * SLOTS, HD), F32)]
        + [(pltpu.SMEM if i == 0 else pltpu.VMEM)(x.shape, x.dtype) for i, x in enumerate(params)]
        + [pltpu.SemaphoreType.DMA((len(params),))],
        10**9,
        (HB,) * len(params),
        *params,
        grant=60,
    )
    row1, row2 = (
        lax.ppermute(own, "ctx", [((i - d) % BLOCKS, i) for i in range(BLOCKS)])
        for d in (RING, 2 * RING)
    )
    mem = lax.all_to_all(mem, "ctx", 0, 0, axis_index_groups=near)
    rotq = call(
        query_kernel, shape(HEADS, TOK, HD), [pltpu.VMEM((TOK, HEADS, HD), F32)], 10**3,
        (SM, VM, VM),
        block_start, freqs, queries,
    )
    bias = call(bias_kernel, shape(KEYS, TOK), [], 10**3, (SM,), block_start)
    far = call(
        far_kernel, shape(FAR, pack * PIECE, HD),
        [pltpu.VMEM((NEAR, pack * SLOTS, HD), F32)], 10**3, (VM, pl.ANY, pl.ANY), mem, row1, row2,
    )
    mem = lax.all_to_all(far, "ctx", 0, 0, axis_index_groups=strided)
    rings = call(
        ring_kernel, (shape(2 * TOKP, HD),) * (RING - 1), [], 10**3, (VM,) * 3 + (pl.ANY,),
        own, row1, row2, far,
    )
    turned = {
        s: lax.ppermute(
            x, "ctx", [(i, i // RING * RING + (i + s) % RING) for i in range(BLOCKS)]
        )
        for s, x in zip(ORDER, rings)
    }
    rings = [turned[s] for s in (1, 2, 3)]
    parts = {}
    for offs in ((3, 2), (1, 0)):
        got = call(
            functools.partial(chunk_kernel, offs), (shape(ROWS, HEADS * HD),) * len(offs),
            [pltpu.VMEM((GROUPS, len(offs) * HEADS // GROUPS * ROWS, KEYS), F32)], 10**6,
            (VM,) * 9, rotq, bias, own, row1, row2, *rings, mem,
        )
        for off, part in zip(offs, got):
            if off:
                part = lax.ppermute(part, "kv", [(i, i ^ off) for i in range(KV)])
            parts[off] = part
    return call(
        join_kernel, shape(ROWS, KV * HEADS * HD), [pltpu.SemaphoreType.DMA((KV,))], 10**8,
        (VM,) * 4, *(parts[i] for i in range(KV)), out_space=HB,
    )


def solution(mesh):
    placed = (
        P("ctx", "kv", None),
        P("ctx", "kv", None),
        P("ctx", "kv", None),
        P(),
        P(),
        P(),
        P(),
        P(),
    )
    return jax.shard_map(
        shards, mesh=mesh, in_specs=placed, out_specs=P(("ctx", "kv"), None), check_vma=False
    )
```

```python
import functools
import math

import jax
import jax.numpy as jnp
import numpy as np
from jax import lax
from jax.experimental import pallas as pl
from jax.experimental.pallas import tpu as pltpu
from jax.sharding import PartitionSpec as P

HD = 128
TOK = 128
STRIDE = 32
SLOTS = TOK // STRIDE
WIN = 8
WINDOW = WIN * TOK
BLOCKS = 128
SEQ = BLOCKS * TOK
HEADS = 16
GROUPS = 2
KV = 4
RING = 4
ORDER = (2, 1, 3)
NEAR = 4
FAR = BLOCKS // NEAR
ROWS = TOK // KV
RAW = (WIN + 1) * TOK
TOKP = 2 * GROUPS * TOK
PIECE = SLOTS * NEAR
KEYS = RAW + BLOCKS * SLOTS
MSCALE = 1.0 + 0.1 * math.log(16.0)
SCALE2 = math.log2(math.e) / math.sqrt(HD)
NEG = -1e30
BF = jnp.bfloat16
F32 = jnp.float32


def yarn_freqs():
    index = np.arange(HD // 2, dtype=np.float32)
    inverse = np.exp(np.float32(-(2.0 / HD) * math.log(500000.0)) * index).astype(np.float32)
    ratio = np.float32(8192.0) * inverse / np.float32(2.0 * math.pi)
    ramp = np.clip((ratio - 1.0) / 31.0, 0.0, 1.0).astype(np.float32)
    freqs = inverse * (ramp + (1.0 - ramp) / np.float32(16.0))
    return np.tile(np.concatenate([freqs, freqs])[None, :], (8, 1)).astype(np.float32)


def turn_tables(place0, freqs):
    places = (place0 + lax.broadcasted_iota(jnp.int32, (TOK, HD), 0)).astype(F32)
    angle = places * freqs
    first = lax.broadcasted_iota(jnp.int32, (TOK, HD), 1) < HD // 2
    sine = jnp.sin(angle)
    return jnp.cos(angle), jnp.where(first, -sine, sine)


def turn(x, cosine, sine, scale=MSCALE):
    return ((x * cosine + pltpu.roll(x, HD // 2, 1) * sine) * scale).astype(BF)


def prep_kernel(bs, freqs, k, v, dk, pk, dv, pv, own, mem, *scratch):
    scr, pool, s_bs, s_freqs, s_k, s_v, s_dk, s_pk, s_dv, s_pv, sem = scratch
    pairs = (
        (bs, s_bs), (freqs, s_freqs), (k, s_k), (v, s_v),
        (dk, s_dk), (pk, s_pk), (dv, s_dv), (pv, s_pv),
    )
    copies = [pltpu.make_async_copy(a, b, sem.at[i]) for i, (a, b) in enumerate(pairs)]
    for c in copies:
        c.start()
    for c in copies:
        c.wait()
    me = lax.axis_index("ctx")
    cosine, sine = turn_tables(s_bs[me], s_freqs[0:1, :])
    scr[...] = s_k[...].astype(F32)
    for g in range(GROUPS):
        rot = turn(scr[:, g, :], cosine, sine)
        own[g * TOK : (g + 1) * TOK, :] = rot
        grouped = rot.astype(F32).reshape(SLOTS, STRIDE, HD)
        pool[g * SLOTS : (g + 1) * SLOTS, :] = jnp.sum(grouped * s_dk[...][None], axis=1)
    scr[...] = s_v[...].astype(F32)
    for g in range(GROUPS):
        val = scr[:, g, :]
        own[(GROUPS + g) * TOK : (GROUPS + g + 1) * TOK, :] = val.astype(BF)
        grouped = val.reshape(SLOTS, STRIDE, HD)
        at = (GROUPS + g) * SLOTS
        pool[at : at + SLOTS, :] = jnp.sum(grouped * s_dv[...][None], axis=1)
    half = GROUPS * SLOTS
    mk = jnp.dot(pool[:half, :], s_pk[...], precision=lax.Precision.HIGHEST, preferred_element_type=F32)
    mv = jnp.dot(pool[half:, :], s_pv[...], precision=lax.Precision.HIGHEST, preferred_element_type=F32)
    both = jnp.concatenate([mk, mv], axis=0).astype(BF)
    mem[...] = jnp.broadcast_to(both[None], mem.shape)


def query_kernel(bs, freqs, q, rotq, scr):
    me = lax.axis_index("ctx")
    cosine, sine = turn_tables(bs[me], freqs[0:1, :])
    scr[...] = q[...].astype(F32)
    for h in range(HEADS):
        rotq[h] = turn(scr[:, h, :], cosine, sine)


def far_kernel(mem, row1, row2, far, scr):
    scr[...] = mem[...].astype(F32)
    kinds = 2 * GROUPS * SLOTS
    slots = jnp.concatenate([scr[:, r, :] for r in range(kinds)], axis=0).astype(BF)
    far[...] = jnp.broadcast_to(slots[None], far.shape)


def ring_kernel(own, row1, row2, far, ra, rb, rc):
    me = lax.rem(lax.axis_index("ctx"), RING)
    for s, out in zip(ORDER, (ra, rb, rc)):
        out[TOKP:, :] = row1[...]

        @pl.when(me + s < RING)
        def _():
            out[:TOKP, :] = own[...]

        @pl.when(me + s >= RING)
        def _():
            out[:TOKP, :] = row2[...]


def bias_kernel(bs, bias):
    me = lax.axis_index("ctx")
    pos = lax.rem(me, RING)
    place = bs[me] + lax.broadcasted_iota(jnp.int32, (TOK, TOK), 1)
    row = lax.broadcasted_iota(jnp.int32, (TOK, TOK), 0)
    backs = [0, RING]
    for s in range(1, RING):
        wrapped = pos < s
        backs += [jnp.where(wrapped, RING + s, s), jnp.where(wrapped, s, RING + s)]
    backs += [WIN]
    for b, back in enumerate(backs):
        there = bs[lax.rem(me - back + BLOCKS, BLOCKS)] + row
        ok = (there <= place) & (there > place - WINDOW)
        bias[b * TOK : (b + 1) * TOK, :] = jnp.where(ok, 0.0, NEG).astype(BF)
    for lo in range(0, BLOCKS * SLOTS, TOK):
        at = lo + row
        block = at // PIECE * NEAR + (at & (NEAR - 1))
        slot = (at & (PIECE - 1)) // NEAR
        ok = ((bs[0] + TOK * block) & (SEQ - 1)) + (slot + 1) * STRIDE <= place + 1
        bias[RAW + lo : RAW + lo + TOK, :] = jnp.where(ok, 0.0, NEG).astype(BF)


def key_tiles():
    half = SLOTS * BLOCKS // 2
    tiles = [(0, [("own", 0, TOK), ("row1", 0, TOK)])]
    for s in range(1, RING):
        tiles.append((2 * s * TOK, [(s, 0, TOK), (s, TOKP, TOK)]))
    tiles.append((RAW, [("mem", 0, half)]))
    tiles.append((RAW + half, [("mem", half, half)]))
    tiles.append((RAW - TOK, [("row2", 0, TOK)]))
    return [(lo, sum(n for _, _, n in tile), tile) for lo, tile in tiles]


def gather_tile(refs, tile, kind):
    parts = []
    for name, lo, n in tile:
        if name == "mem":
            rows = slice(kind * PIECE, (kind + 1) * PIECE)
            parts += [refs[name][i, rows, :] for i in range(lo // PIECE, (lo + n) // PIECE)]
        else:
            at = lo + kind * TOK
            parts.append(refs[name][at : at + n, :])
    return parts[0] if len(parts) == 1 else jnp.concatenate(parts, axis=0)


def chunk_kernel(offs, rotq, bias, own, row1, row2, r1, r2, r3, mem, *rest):
    refs = {"own": own, "row1": row1, "row2": row2, 1: r1, 2: r2, 3: r3, "mem": mem}
    outs, s = rest[:-1], rest[-1]
    firsts = [pl.multiple_of((lax.axis_index("kv") ^ o) * ROWS, ROWS) for o in offs]
    heads = HEADS // GROUPS
    r = lax.broadcasted_iota(jnp.int32, (heads * ROWS, TOK), 0) & (ROWS - 1)
    c = lax.broadcasted_iota(jnp.int32, (heads * ROWS, TOK), 1)
    unit = jnp.concatenate([jnp.where(r + f == c, 1.0, 0.0).astype(BF) for f in firsts], axis=0)
    tops = []
    for g in range(GROUPS):
        q = jnp.concatenate(
            [rotq[g * heads + i, pl.ds(f, ROWS), :] for f in firsts for i in range(heads)], axis=0
        )
        qa = jnp.concatenate([q, unit], axis=1)
        high = None
        for lo, size, tile in key_tiles():
            k = gather_tile(refs, tile, g)
            ka = jnp.concatenate([k, bias[lo : lo + size, :]], axis=1)
            x = lax.dot_general(qa, ka, (((1,), (1,)), ((), ())), preferred_element_type=F32)
            s[g, :, lo : lo + size] = x
            for i in range(size // HD):
                part = x[:, i * HD : (i + 1) * HD]
                high = part if high is None else jnp.maximum(high, part)
        tops.append(jnp.max(high, axis=1, keepdims=True))
    for g in range(GROUPS):
        mixed = None
        for lo, size, tile in key_tiles():
            w = jnp.exp2((s[g, :, lo : lo + size] - tops[g]) * SCALE2).astype(BF)
            v = gather_tile(refs, tile, GROUPS + g)
            va = jnp.concatenate([v, jnp.ones((size, HD), BF)], axis=1)
            part = jnp.dot(w, va, preferred_element_type=F32)
            mixed = part if mixed is None else mixed + part
        res = (mixed[:, :HD] / mixed[:, HD:]).astype(BF)
        for n, out in enumerate(outs):
            for i in range(heads):
                h, at = g * heads + i, (n * heads + i) * ROWS
                out[:, h * HD : (h + 1) * HD] = res[at : at + ROWS, :]


def join_kernel(a, b, c, d, out, sem):
    me = lax.axis_index("kv")
    wide = HEADS * HD
    copies = []
    for off, part in enumerate((a, b, c, d)):
        lane = pl.multiple_of((me ^ off) * wide, wide)
        copies.append(pltpu.make_async_copy(part, out.at[:, pl.ds(lane, wide)], sem.at[off]))
    for x in copies:
        x.start()
    for x in copies:
        x.wait()


def call(kernel, out_shape, scratch, flops, spaces, *args, out_space=pltpu.VMEM, grant=32, alias=None):
    multi = isinstance(out_shape, tuple)
    vm = pl.BlockSpec(memory_space=out_space)
    return pl.pallas_call(
        kernel,
        out_shape=out_shape,
        in_specs=[pl.BlockSpec(memory_space=s) for s in spaces],
        out_specs=(vm,) * len(out_shape) if multi else vm,
        scratch_shapes=scratch,
        input_output_aliases=alias or {},
        compiler_params=pltpu.CompilerParams(vmem_limit_bytes=grant * 2**20),
        cost_estimate=pl.CostEstimate(flops=flops, bytes_accessed=2**10, transcendentals=0),
    )(*args)


def shape(*dims, dtype=BF):
    return jax.ShapeDtypeStruct(dims, dtype)


near = [[NEAR * o + p for p in range(NEAR)] for o in range(FAR)]
strided = [[NEAR * o + p for o in range(FAR)] for p in range(NEAR)]
SM, VM, HB = pltpu.SMEM, pltpu.VMEM, pltpu.HBM


def shards(queries, keys, values, block_start, depth_k, point_k, depth_v, point_v):
    freqs = jnp.asarray(yarn_freqs())
    pack = 2 * GROUPS
    params = (block_start, freqs, keys, values, depth_k, point_k, depth_v, point_v)
    own, mem = call(
        prep_kernel,
        (shape(pack * TOK, HD), shape(NEAR, pack * SLOTS, HD)),
        [pltpu.VMEM((TOK, GROUPS, HD), F32), pltpu.VMEM((pack * SLOTS, HD), F32)]
        + [(pltpu.SMEM if i == 0 else pltpu.VMEM)(x.shape, x.dtype) for i, x in enumerate(params)]
        + [pltpu.SemaphoreType.DMA((len(params),))],
        10**9,
        (HB,) * len(params),
        *params,
        grant=60,
    )
    row1, row2 = (
        lax.ppermute(own, "ctx", [((i - d) % BLOCKS, i) for i in range(BLOCKS)])
        for d in (RING, 2 * RING)
    )
    mem = lax.all_to_all(mem, "ctx", 0, 0, axis_index_groups=near)
    rotq = call(
        query_kernel, shape(HEADS, TOK, HD), [pltpu.VMEM((TOK, HEADS, HD), F32)], 10**3,
        (SM, VM, VM),
        block_start, freqs, queries,
    )
    bias = call(bias_kernel, shape(KEYS, TOK), [], 10**3, (SM,), block_start)
    far = call(
        far_kernel, shape(FAR, pack * PIECE, HD),
        [pltpu.VMEM((NEAR, pack * SLOTS, HD), F32)], 10**3, (VM, pl.ANY, pl.ANY), mem, row1, row2,
    )
    mem = lax.all_to_all(far, "ctx", 0, 0, axis_index_groups=strided)
    rings = call(
        ring_kernel, (shape(2 * TOKP, HD),) * (RING - 1), [], 10**3, (VM,) * 3 + (pl.ANY,),
        own, row1, row2, far,
    )
    turned = {
        s: lax.ppermute(
            x, "ctx", [(i, i // RING * RING + (i + s) % RING) for i in range(BLOCKS)]
        )
        for s, x in zip(ORDER, rings)
    }
    rings = [turned[s] for s in (1, 2, 3)]
    parts = {}
    for offs in ((3, 2), (1, 0)):
        got = call(
            functools.partial(chunk_kernel, offs), (shape(ROWS, HEADS * HD),) * len(offs),
            [pltpu.VMEM((GROUPS, len(offs) * HEADS // GROUPS * ROWS, KEYS), F32)], 10**6,
            (VM,) * 9, rotq, bias, own, row1, row2, *rings, mem,
        )
        for off, part in zip(offs, got):
            if off:
                part = lax.ppermute(part, "kv", [(i, i ^ off) for i in range(KV)])
            parts[off] = part
    return call(
        join_kernel, shape(ROWS, KV * HEADS * HD), [pltpu.SemaphoreType.DMA((KV,))], 10**8,
        (VM,) * 4, *(parts[i] for i in range(KV)), out_space=HB,
    )


def solution(mesh):
    placed = (
        P("ctx", "kv", None),
        P("ctx", "kv", None),
        P("ctx", "kv", None),
        P(),
        P(),
        P(),
        P(),
        P(),
    )
    return jax.shard_map(
        shards, mesh=mesh, in_specs=placed, out_specs=P(("ctx", "kv"), None), check_vma=False
    )
```

```python
import functools
import math

import jax
import jax.numpy as jnp
import numpy as np
from jax import lax
from jax.experimental import pallas as pl
from jax.experimental.pallas import tpu as pltpu
from jax.sharding import PartitionSpec as P

HD = 128
TOK = 128
STRIDE = 32
SLOTS = TOK // STRIDE
WIN = 8
WINDOW = WIN * TOK
BLOCKS = 128
SEQ = BLOCKS * TOK
HEADS = 16
GROUPS = 2
KV = 4
RING = 4
ORDER = (3, 2, 1)
NEAR = 8
FAR = BLOCKS // NEAR
ROWS = TOK // KV
RAW = (WIN + 1) * TOK
TOKP = 2 * GROUPS * TOK
PIECE = SLOTS * NEAR
KEYS = RAW + BLOCKS * SLOTS
MSCALE = 1.0 + 0.1 * math.log(16.0)
SCALE2 = math.log2(math.e) / math.sqrt(HD)
NEG = -1e30
BF = jnp.bfloat16
F32 = jnp.float32


def yarn_freqs():
    index = np.arange(HD // 2, dtype=np.float32)
    inverse = np.exp(np.float32(-(2.0 / HD) * math.log(500000.0)) * index).astype(np.float32)
    ratio = np.float32(8192.0) * inverse / np.float32(2.0 * math.pi)
    ramp = np.clip((ratio - 1.0) / 31.0, 0.0, 1.0).astype(np.float32)
    freqs = inverse * (ramp + (1.0 - ramp) / np.float32(16.0))
    return np.tile(np.concatenate([freqs, freqs])[None, :], (8, 1)).astype(np.float32)


def turn_tables(place0, freqs):
    places = (place0 + lax.broadcasted_iota(jnp.int32, (TOK, HD), 0)).astype(F32)
    angle = places * freqs
    first = lax.broadcasted_iota(jnp.int32, (TOK, HD), 1) < HD // 2
    sine = jnp.sin(angle)
    return jnp.cos(angle), jnp.where(first, -sine, sine)


def turn(x, cosine, sine, scale=MSCALE):
    return ((x * cosine + pltpu.roll(x, HD // 2, 1) * sine) * scale).astype(BF)


def prep_kernel(bs, freqs, k, v, dk, pk, dv, pv, own, mem, *scratch):
    scr, pool, s_bs, s_freqs, s_k, s_v, s_dk, s_pk, s_dv, s_pv, sem = scratch
    pairs = (
        (bs, s_bs), (freqs, s_freqs), (k, s_k), (v, s_v),
        (dk, s_dk), (pk, s_pk), (dv, s_dv), (pv, s_pv),
    )
    copies = [pltpu.make_async_copy(a, b, sem.at[i]) for i, (a, b) in enumerate(pairs)]
    for c in copies:
        c.start()
    for c in copies:
        c.wait()
    me = lax.axis_index("ctx")
    cosine, sine = turn_tables(s_bs[me], s_freqs[0:1, :])
    scr[...] = s_k[...].astype(F32)
    for g in range(GROUPS):
        rot = turn(scr[:, g, :], cosine, sine)
        own[g * TOK : (g + 1) * TOK, :] = rot
        grouped = rot.astype(F32).reshape(SLOTS, STRIDE, HD)
        pool[g * SLOTS : (g + 1) * SLOTS, :] = jnp.sum(grouped * s_dk[...][None], axis=1)
    scr[...] = s_v[...].astype(F32)
    for g in range(GROUPS):
        val = scr[:, g, :]
        own[(GROUPS + g) * TOK : (GROUPS + g + 1) * TOK, :] = val.astype(BF)
        grouped = val.reshape(SLOTS, STRIDE, HD)
        at = (GROUPS + g) * SLOTS
        pool[at : at + SLOTS, :] = jnp.sum(grouped * s_dv[...][None], axis=1)
    half = GROUPS * SLOTS
    mk = jnp.dot(pool[:half, :], s_pk[...], precision=lax.Precision.HIGHEST, preferred_element_type=F32)
    mv = jnp.dot(pool[half:, :], s_pv[...], precision=lax.Precision.HIGHEST, preferred_element_type=F32)
    both = jnp.concatenate([mk, mv], axis=0).astype(BF)
    mem[...] = jnp.broadcast_to(both[None], mem.shape)


def query_kernel(bs, freqs, q, rotq, scr):
    me = lax.axis_index("ctx")
    cosine, sine = turn_tables(bs[me], freqs[0:1, :])
    scr[...] = q[...].astype(F32)
    for h in range(HEADS):
        rotq[h] = turn(scr[:, h, :], cosine, sine)


def far_kernel(mem, row1, row2, far, scr):
    scr[...] = mem[...].astype(F32)
    kinds = 2 * GROUPS * SLOTS
    slots = jnp.concatenate([scr[:, r, :] for r in range(kinds)], axis=0).astype(BF)
    far[...] = jnp.broadcast_to(slots[None], far.shape)


def ring_kernel(own, row1, row2, far, ra, rb, rc):
    me = lax.rem(lax.axis_index("ctx"), RING)
    for s, out in zip(ORDER, (ra, rb, rc)):
        if s != 2:
            out[TOKP:, :] = row1[...]

        @pl.when(me + s < RING)
        def _():
            out[:TOKP, :] = own[...]

        @pl.when(me + s >= RING)
        def _():
            out[:TOKP, :] = row2[...]


def bias_kernel(bs, bias):
    me = lax.axis_index("ctx")
    pos = lax.rem(me, RING)
    place = bs[me] + lax.broadcasted_iota(jnp.int32, (TOK, TOK), 1)
    row = lax.broadcasted_iota(jnp.int32, (TOK, TOK), 0)
    backs = [0, RING]
    for s in range(1, RING):
        wrapped = pos < s
        backs += [jnp.where(wrapped, RING + s, s), jnp.where(wrapped, s, RING + s)]
    backs += [WIN]
    for b, back in enumerate(backs):
        there = bs[lax.rem(me - back + BLOCKS, BLOCKS)] + row
        ok = (there <= place) & (there > place - WINDOW)
        bias[b * TOK : (b + 1) * TOK, :] = jnp.where(ok, 0.0, NEG).astype(BF)
    for lo in range(0, BLOCKS * SLOTS, TOK):
        at = lo + row
        block = at // PIECE * NEAR + (at & (NEAR - 1))
        slot = (at & (PIECE - 1)) // NEAR
        ok = ((bs[0] + TOK * block) & (SEQ - 1)) + (slot + 1) * STRIDE <= place + 1
        bias[RAW + lo : RAW + lo + TOK, :] = jnp.where(ok, 0.0, NEG).astype(BF)


def key_tiles():
    half = SLOTS * BLOCKS // 2
    tiles = [(0, [("own", 0, TOK), ("row1", 0, TOK)])]
    for s in range(1, RING):
        tiles.append((2 * s * TOK, [(s, 0, TOK), ("pass", 0, TOK) if s == 2 else (s, TOKP, TOK)]))
    tiles.append((RAW, [("mem", 0, half)]))
    tiles.append((RAW + half, [("mem", half, half)]))
    tiles.append((RAW - TOK, [("row2", 0, TOK)]))
    return [(lo, sum(n for _, _, n in tile), tile) for lo, tile in tiles]


def gather_tile(refs, tile, kind):
    parts = []
    for name, lo, n in tile:
        if name == "mem":
            rows = slice(kind * PIECE, (kind + 1) * PIECE)
            parts += [refs[name][i, rows, :] for i in range(lo // PIECE, (lo + n) // PIECE)]
        else:
            at = lo + kind * TOK
            parts.append(refs[name][at : at + n, :])
    return parts[0] if len(parts) == 1 else jnp.concatenate(parts, axis=0)


def chunk_kernel(offs, rotq, bias, own, row1, row2, r1, r2, r3, passed, mem, *rest):
    refs = {"own": own, "row1": row1, "row2": row2, 1: r1, 2: r2, 3: r3, "pass": passed, "mem": mem}
    outs, s = rest[:-1], rest[-1]
    firsts = [pl.multiple_of((lax.axis_index("kv") ^ o) * ROWS, ROWS) for o in offs]
    heads = HEADS // GROUPS
    r = lax.broadcasted_iota(jnp.int32, (heads * ROWS, TOK), 0) & (ROWS - 1)
    c = lax.broadcasted_iota(jnp.int32, (heads * ROWS, TOK), 1)
    unit = jnp.concatenate([jnp.where(r + f == c, 1.0, 0.0).astype(BF) for f in firsts], axis=0)
    tops = []
    for g in range(GROUPS):
        q = jnp.concatenate(
            [rotq[g * heads + i, pl.ds(f, ROWS), :] for f in firsts for i in range(heads)], axis=0
        )
        qa = jnp.concatenate([q, unit], axis=1)
        high = None
        for lo, size, tile in key_tiles():
            k = gather_tile(refs, tile, g)
            ka = jnp.concatenate([k, bias[lo : lo + size, :]], axis=1)
            x = lax.dot_general(qa, ka, (((1,), (1,)), ((), ())), preferred_element_type=F32)
            s[g, :, lo : lo + size] = x
            for i in range(size // HD):
                part = x[:, i * HD : (i + 1) * HD]
                high = part if high is None else jnp.maximum(high, part)
        tops.append(jnp.max(high, axis=1, keepdims=True))
    for g in range(GROUPS):
        mixed = None
        for lo, size, tile in key_tiles():
            w = jnp.exp2((s[g, :, lo : lo + size] - tops[g]) * SCALE2).astype(BF)
            v = gather_tile(refs, tile, GROUPS + g)
            va = jnp.concatenate([v, jnp.ones((size, HD), BF)], axis=1)
            part = jnp.dot(w, va, preferred_element_type=F32)
            mixed = part if mixed is None else mixed + part
        res = (mixed[:, :HD] / mixed[:, HD:]).astype(BF)
        for n, out in enumerate(outs):
            for i in range(heads):
                h, at = g * heads + i, (n * heads + i) * ROWS
                out[:, h * HD : (h + 1) * HD] = res[at : at + ROWS, :]


def join_kernel(a, b, c, d, out, sem):
    me = lax.axis_index("kv")
    wide = HEADS * HD
    copies = []
    for off, part in enumerate((a, b, c, d)):
        lane = pl.multiple_of((me ^ off) * wide, wide)
        copies.append(pltpu.make_async_copy(part, out.at[:, pl.ds(lane, wide)], sem.at[off]))
    for x in copies:
        x.start()
    for x in copies:
        x.wait()


def call(kernel, out_shape, scratch, flops, spaces, *args, out_space=pltpu.VMEM, grant=32, alias=None):
    multi = isinstance(out_shape, tuple)
    vm = pl.BlockSpec(memory_space=out_space)
    return pl.pallas_call(
        kernel,
        out_shape=out_shape,
        in_specs=[pl.BlockSpec(memory_space=s) for s in spaces],
        out_specs=(vm,) * len(out_shape) if multi else vm,
        scratch_shapes=scratch,
        input_output_aliases=alias or {},
        compiler_params=pltpu.CompilerParams(vmem_limit_bytes=grant * 2**20),
        cost_estimate=pl.CostEstimate(flops=flops, bytes_accessed=2**10, transcendentals=0),
    )(*args)


def shape(*dims, dtype=BF):
    return jax.ShapeDtypeStruct(dims, dtype)


near = [[NEAR * o + p for p in range(NEAR)] for o in range(FAR)]
strided = [[NEAR * o + p for o in range(FAR)] for p in range(NEAR)]
SM, VM, HB = pltpu.SMEM, pltpu.VMEM, pltpu.HBM


def shards(queries, keys, values, block_start, depth_k, point_k, depth_v, point_v):
    freqs = jnp.asarray(yarn_freqs())
    pack = 2 * GROUPS
    params = (block_start, freqs, keys, values, depth_k, point_k, depth_v, point_v)
    own, mem = call(
        prep_kernel,
        (shape(pack * TOK, HD), shape(NEAR, pack * SLOTS, HD)),
        [pltpu.VMEM((TOK, GROUPS, HD), F32), pltpu.VMEM((pack * SLOTS, HD), F32)]
        + [(pltpu.SMEM if i == 0 else pltpu.VMEM)(x.shape, x.dtype) for i, x in enumerate(params)]
        + [pltpu.SemaphoreType.DMA((len(params),))],
        10**9,
        (HB,) * len(params),
        *params,
        grant=60,
    )
    row1, row2 = (
        lax.ppermute(own, "ctx", [((i - d) % BLOCKS, i) for i in range(BLOCKS)])
        for d in (RING, 2 * RING)
    )
    mem = lax.all_to_all(mem, "ctx", 0, 0, axis_index_groups=near)
    rotq = call(
        query_kernel, shape(HEADS, TOK, HD), [pltpu.VMEM((TOK, HEADS, HD), F32)], 10**3,
        (SM, VM, VM),
        block_start, freqs, queries,
    )
    bias = call(bias_kernel, shape(KEYS, TOK), [], 10**3, (SM,), block_start)
    far = call(
        far_kernel, shape(FAR, pack * PIECE, HD),
        [pltpu.VMEM((NEAR, pack * SLOTS, HD), F32)], 10**3, (VM, pl.ANY, pl.ANY), mem, row1, row2,
    )
    mem = lax.all_to_all(far, "ctx", 0, 0, axis_index_groups=strided)
    rings = call(
        ring_kernel, tuple(shape(TOKP if s == 2 else 2 * TOKP, HD) for s in ORDER), [], 10**3, (VM,) * 3 + (pl.ANY,),
        own, row1, row2, far,
    )
    turned = {
        s: lax.ppermute(
            x, "ctx", [(i, i // RING * RING + (i + s) % RING) for i in range(BLOCKS)]
        )
        for s, x in zip(ORDER, rings)
    }
    passed = lax.ppermute(
        turned[3][TOKP:], "ctx", [(i, i // RING * RING + (i + 3) % RING) for i in range(BLOCKS)]
    )
    rings = [turned[s] for s in (1, 2, 3)] + [passed]
    parts = {}
    for offs in ((3, 2), (1, 0)):
        got = call(
            functools.partial(chunk_kernel, offs), (shape(ROWS, HEADS * HD),) * len(offs),
            [pltpu.VMEM((GROUPS, len(offs) * HEADS // GROUPS * ROWS, KEYS), F32)], 10**6,
            (VM,) * 10, rotq, bias, own, row1, row2, *rings, mem,
        )
        for off, part in zip(offs, got):
            if off:
                part = lax.ppermute(part, "kv", [(i, i ^ off) for i in range(KV)])
            parts[off] = part
    return call(
        join_kernel, shape(ROWS, KV * HEADS * HD), [pltpu.SemaphoreType.DMA((KV,))], 10**8,
        (VM,) * 4, *(parts[i] for i in range(KV)), out_space=HB,
    )


def solution(mesh):
    placed = (
        P("ctx", "kv", None),
        P("ctx", "kv", None),
        P("ctx", "kv", None),
        P(),
        P(),
        P(),
        P(),
        P(),
    )
    return jax.shard_map(
        shards, mesh=mesh, in_specs=placed, out_specs=P(("ctx", "kv"), None), check_vma=False
    )
```

```python
import functools
import math

import jax
import jax.numpy as jnp
import numpy as np
from jax import lax
from jax.experimental import pallas as pl
from jax.experimental.pallas import tpu as pltpu
from jax.sharding import PartitionSpec as P

HD = 128
TOK = 128
STRIDE = 32
SLOTS = TOK // STRIDE
WIN = 8
WINDOW = WIN * TOK
BLOCKS = 128
SEQ = BLOCKS * TOK
HEADS = 16
GROUPS = 2
KV = 4
RING = 4
ORDER = (3, 2, 1)
NEAR = 8
FAR = BLOCKS // NEAR
ROWS = TOK // KV
RAW = (WIN + 1) * TOK
TOKP = 2 * GROUPS * TOK
PIECE = SLOTS * NEAR
KEYS = RAW + BLOCKS * SLOTS
MSCALE = 1.0 + 0.1 * math.log(16.0)
SCALE2 = math.log2(math.e) / math.sqrt(HD)
NEG = -1e30
BF = jnp.bfloat16
F32 = jnp.float32


def yarn_freqs():
    index = np.arange(HD // 2, dtype=np.float32)
    inverse = np.exp(np.float32(-(2.0 / HD) * math.log(500000.0)) * index).astype(np.float32)
    ratio = np.float32(8192.0) * inverse / np.float32(2.0 * math.pi)
    ramp = np.clip((ratio - 1.0) / 31.0, 0.0, 1.0).astype(np.float32)
    freqs = inverse * (ramp + (1.0 - ramp) / np.float32(16.0))
    return np.tile(np.concatenate([freqs, freqs])[None, :], (8, 1)).astype(np.float32)


def turn_tables(place0, freqs):
    places = (place0 + lax.broadcasted_iota(jnp.int32, (TOK, HD), 0)).astype(F32)
    angle = places * freqs
    first = lax.broadcasted_iota(jnp.int32, (TOK, HD), 1) < HD // 2
    sine = jnp.sin(angle)
    return jnp.cos(angle), jnp.where(first, -sine, sine)


def turn(x, cosine, sine, scale=MSCALE):
    return ((x * cosine + pltpu.roll(x, HD // 2, 1) * sine) * scale).astype(BF)


def prep_kernel(bs, freqs, k, v, dk, pk, dv, pv, own, mem, *scratch):
    scr, pool, s_bs, s_freqs, s_k, s_v, s_dk, s_pk, s_dv, s_pv, sem = scratch
    pairs = (
        (bs, s_bs), (freqs, s_freqs), (k, s_k), (v, s_v),
        (dk, s_dk), (pk, s_pk), (dv, s_dv), (pv, s_pv),
    )
    copies = [pltpu.make_async_copy(a, b, sem.at[i]) for i, (a, b) in enumerate(pairs)]
    for c in copies:
        c.start()
    for c in copies:
        c.wait()
    me = lax.axis_index("ctx")
    cosine, sine = turn_tables(s_bs[me], s_freqs[0:1, :])
    scr[...] = s_k[...].astype(F32)
    for g in range(GROUPS):
        rot = turn(scr[:, g, :], cosine, sine)
        own[g * TOK : (g + 1) * TOK, :] = rot
        grouped = rot.astype(F32).reshape(SLOTS, STRIDE, HD)
        pool[g * SLOTS : (g + 1) * SLOTS, :] = jnp.sum(grouped * s_dk[...][None], axis=1)
    scr[...] = s_v[...].astype(F32)
    for g in range(GROUPS):
        val = scr[:, g, :]
        own[(GROUPS + g) * TOK : (GROUPS + g + 1) * TOK, :] = val.astype(BF)
        grouped = val.reshape(SLOTS, STRIDE, HD)
        at = (GROUPS + g) * SLOTS
        pool[at : at + SLOTS, :] = jnp.sum(grouped * s_dv[...][None], axis=1)
    half = GROUPS * SLOTS
    mk = jnp.dot(pool[:half, :], s_pk[...], precision=lax.Precision.HIGHEST, preferred_element_type=F32)
    mv = jnp.dot(pool[half:, :], s_pv[...], precision=lax.Precision.HIGHEST, preferred_element_type=F32)
    both = jnp.concatenate([mk, mv], axis=0).astype(BF)
    mem[...] = jnp.broadcast_to(both[None], mem.shape)


def query_kernel(bs, freqs, q, rotq, scr):
    me = lax.axis_index("ctx")
    cosine, sine = turn_tables(bs[me], freqs[0:1, :])
    scr[...] = q[...].astype(F32)
    for h in range(HEADS):
        rotq[h] = turn(scr[:, h, :], cosine, sine)


def far_kernel(mem, row1, row2, rotq, bias, far, scr):
    scr[...] = mem[...].astype(F32)
    kinds = 2 * GROUPS * SLOTS
    slots = jnp.concatenate([scr[:, r, :] for r in range(kinds)], axis=0).astype(BF)
    far[...] = jnp.broadcast_to(slots[None], far.shape)


def ring_kernel(own, row1, row2, far, ra, rb, rc):
    me = lax.rem(lax.axis_index("ctx"), RING)
    for s, out in zip(ORDER, (ra, rb, rc)):
        if s != 2:
            out[TOKP:, :] = row1[...]

        @pl.when(me + s < RING)
        def _():
            out[:TOKP, :] = own[...]

        @pl.when(me + s >= RING)
        def _():
            out[:TOKP, :] = row2[...]


def bias_kernel(bs, bias):
    me = lax.axis_index("ctx")
    pos = lax.rem(me, RING)
    place = bs[me] + lax.broadcasted_iota(jnp.int32, (TOK, TOK), 1)
    row = lax.broadcasted_iota(jnp.int32, (TOK, TOK), 0)
    backs = [0, RING]
    for s in range(1, RING):
        wrapped = pos < s
        backs += [jnp.where(wrapped, RING + s, s), jnp.where(wrapped, s, RING + s)]
    backs += [WIN]
    for b, back in enumerate(backs):
        there = bs[lax.rem(me - back + BLOCKS, BLOCKS)] + row
        ok = (there <= place) & (there > place - WINDOW)
        bias[b * TOK : (b + 1) * TOK, :] = jnp.where(ok, 0.0, NEG).astype(BF)
    for lo in range(0, BLOCKS * SLOTS, TOK):
        at = lo + row
        block = at // PIECE * NEAR + (at & (NEAR - 1))
        slot = (at & (PIECE - 1)) // NEAR
        ok = ((bs[0] + TOK * block) & (SEQ - 1)) + (slot + 1) * STRIDE <= place + 1
        bias[RAW + lo : RAW + lo + TOK, :] = jnp.where(ok, 0.0, NEG).astype(BF)


def key_tiles():
    half = SLOTS * BLOCKS // 2
    tiles = [(0, [("own", 0, TOK), ("row1", 0, TOK)])]
    for s in range(1, RING):
        tiles.append((2 * s * TOK, [(s, 0, TOK), ("pass", 0, TOK) if s == 2 else (s, TOKP, TOK)]))
    tiles.append((RAW, [("mem", 0, half)]))
    tiles.append((RAW + half, [("mem", half, half)]))
    tiles.append((RAW - TOK, [("row2", 0, TOK)]))
    return [(lo, sum(n for _, _, n in tile), tile) for lo, tile in tiles]


def gather_tile(refs, tile, kind):
    parts = []
    for name, lo, n in tile:
        if name == "mem":
            rows = slice(kind * PIECE, (kind + 1) * PIECE)
            parts += [refs[name][i, rows, :] for i in range(lo // PIECE, (lo + n) // PIECE)]
        else:
            at = lo + kind * TOK
            parts.append(refs[name][at : at + n, :])
    return parts[0] if len(parts) == 1 else jnp.concatenate(parts, axis=0)


def chunk_kernel(offs, rotq, bias, own, row1, row2, r1, r2, r3, passed, mem, *rest):
    refs = {"own": own, "row1": row1, "row2": row2, 1: r1, 2: r2, 3: r3, "pass": passed, "mem": mem}
    outs, s = rest[:-1], rest[-1]
    firsts = [pl.multiple_of((lax.axis_index("kv") ^ o) * ROWS, ROWS) for o in offs]
    heads = HEADS // GROUPS
    r = lax.broadcasted_iota(jnp.int32, (heads * ROWS, TOK), 0) & (ROWS - 1)
    c = lax.broadcasted_iota(jnp.int32, (heads * ROWS, TOK), 1)
    unit = jnp.concatenate([jnp.where(r + f == c, 1.0, 0.0).astype(BF) for f in firsts], axis=0)
    tops = []
    for g in range(GROUPS):
        q = jnp.concatenate(
            [rotq[g * heads + i, pl.ds(f, ROWS), :] for f in firsts for i in range(heads)], axis=0
        )
        qa = jnp.concatenate([q, unit], axis=1)
        high = None
        for lo, size, tile in key_tiles():
            k = gather_tile(refs, tile, g)
            ka = jnp.concatenate([k, bias[lo : lo + size, :]], axis=1)
            x = lax.dot_general(qa, ka, (((1,), (1,)), ((), ())), preferred_element_type=F32)
            s[g, :, lo : lo + size] = x
            for i in range(size // HD):
                part = x[:, i * HD : (i + 1) * HD]
                high = part if high is None else jnp.maximum(high, part)
        tops.append(jnp.max(high, axis=1, keepdims=True))
    for g in range(GROUPS):
        mixed = None
        for lo, size, tile in key_tiles():
            w = jnp.exp2((s[g, :, lo : lo + size] - tops[g]) * SCALE2).astype(BF)
            v = gather_tile(refs, tile, GROUPS + g)
            va = jnp.concatenate([v, jnp.ones((size, HD), BF)], axis=1)
            part = jnp.dot(w, va, preferred_element_type=F32)
            mixed = part if mixed is None else mixed + part
        res = (mixed[:, :HD] / mixed[:, HD:]).astype(BF)
        for n, out in enumerate(outs):
            for i in range(heads):
                h, at = g * heads + i, (n * heads + i) * ROWS
                out[:, h * HD : (h + 1) * HD] = res[at : at + ROWS, :]


def join_kernel(a, b, c, d, out, sem):
    me = lax.axis_index("kv")
    wide = HEADS * HD
    copies = []
    for off, part in enumerate((a, b, c, d)):
        lane = pl.multiple_of((me ^ off) * wide, wide)
        copies.append(pltpu.make_async_copy(part, out.at[:, pl.ds(lane, wide)], sem.at[off]))
    for x in copies:
        x.start()
    for x in copies:
        x.wait()


def call(kernel, out_shape, scratch, flops, spaces, *args, out_space=pltpu.VMEM, grant=32, alias=None):
    multi = isinstance(out_shape, tuple)
    vm = pl.BlockSpec(memory_space=out_space)
    return pl.pallas_call(
        kernel,
        out_shape=out_shape,
        in_specs=[pl.BlockSpec(memory_space=s) for s in spaces],
        out_specs=(vm,) * len(out_shape) if multi else vm,
        scratch_shapes=scratch,
        input_output_aliases=alias or {},
        compiler_params=pltpu.CompilerParams(vmem_limit_bytes=grant * 2**20),
        cost_estimate=pl.CostEstimate(flops=flops, bytes_accessed=2**10, transcendentals=0),
    )(*args)


def shape(*dims, dtype=BF):
    return jax.ShapeDtypeStruct(dims, dtype)


near = [[NEAR * o + p for p in range(NEAR)] for o in range(FAR)]
strided = [[NEAR * o + p for o in range(FAR)] for p in range(NEAR)]
SM, VM, HB = pltpu.SMEM, pltpu.VMEM, pltpu.HBM


def shards(queries, keys, values, block_start, depth_k, point_k, depth_v, point_v):
    freqs = jnp.asarray(yarn_freqs())
    pack = 2 * GROUPS
    params = (block_start, freqs, keys, values, depth_k, point_k, depth_v, point_v)
    own, mem = call(
        prep_kernel,
        (shape(pack * TOK, HD), shape(NEAR, pack * SLOTS, HD)),
        [pltpu.VMEM((TOK, GROUPS, HD), F32), pltpu.VMEM((pack * SLOTS, HD), F32)]
        + [(pltpu.SMEM if i == 0 else pltpu.VMEM)(x.shape, x.dtype) for i, x in enumerate(params)]
        + [pltpu.SemaphoreType.DMA((len(params),))],
        10**9,
        (HB,) * len(params),
        *params,
        grant=60,
    )
    row1, row2 = (
        lax.ppermute(own, "ctx", [((i - d) % BLOCKS, i) for i in range(BLOCKS)])
        for d in (RING, 2 * RING)
    )
    mem = lax.all_to_all(mem, "ctx", 0, 0, axis_index_groups=near)
    rotq = call(
        query_kernel, shape(HEADS, TOK, HD), [pltpu.VMEM((TOK, HEADS, HD), F32)], 10**9,
        (SM, VM, VM),
        block_start, freqs, queries,
    )
    bias = call(bias_kernel, shape(KEYS, TOK), [], 10**3, (SM,), block_start)
    far = call(
        far_kernel, shape(FAR, pack * PIECE, HD),
        [pltpu.VMEM((NEAR, pack * SLOTS, HD), F32)], 10**3, (VM,) + (pl.ANY,) * 4, mem, row1, row2, rotq, bias,
    )
    mem = lax.all_to_all(far, "ctx", 0, 0, axis_index_groups=strided)
    rings = call(
        ring_kernel, tuple(shape(TOKP if s == 2 else 2 * TOKP, HD) for s in ORDER), [], 10**3, (VM,) * 3 + (pl.ANY,),
        own, row1, row2, far,
    )
    turned = {
        s: lax.ppermute(
            x, "ctx", [(i, i // RING * RING + (i + s) % RING) for i in range(BLOCKS)]
        )
        for s, x in zip(ORDER, rings)
    }
    passed = lax.ppermute(
        turned[3][TOKP:], "ctx", [(i, i // RING * RING + (i + 3) % RING) for i in range(BLOCKS)]
    )
    rings = [turned[s] for s in (1, 2, 3)] + [passed]
    parts = {}
    for offs in ((3, 2), (1, 0)):
        got = call(
            functools.partial(chunk_kernel, offs), (shape(ROWS, HEADS * HD),) * len(offs),
            [pltpu.VMEM((GROUPS, len(offs) * HEADS // GROUPS * ROWS, KEYS), F32)], 10**6,
            (VM,) * 10, rotq, bias, own, row1, row2, *rings, mem,
        )
        for off, part in zip(offs, got):
            if off:
                part = lax.ppermute(part, "kv", [(i, i ^ off) for i in range(KV)])
            parts[off] = part
    return call(
        join_kernel, shape(ROWS, KV * HEADS * HD), [pltpu.SemaphoreType.DMA((KV,))], 10**8,
        (VM,) * 4, *(parts[i] for i in range(KV)), out_space=HB,
    )


def solution(mesh):
    placed = (
        P("ctx", "kv", None),
        P("ctx", "kv", None),
        P("ctx", "kv", None),
        P(),
        P(),
        P(),
        P(),
        P(),
    )
    return jax.shard_map(
        shards, mesh=mesh, in_specs=placed, out_specs=P(("ctx", "kv"), None), check_vma=False
    )
```

```python
import functools
import math

import jax
import jax.numpy as jnp
import numpy as np
from jax import lax
from jax.experimental import pallas as pl
from jax.experimental.pallas import tpu as pltpu
from jax.sharding import PartitionSpec as P

HD = 128
TOK = 128
STRIDE = 32
SLOTS = TOK // STRIDE
WIN = 8
WINDOW = WIN * TOK
BLOCKS = 128
SEQ = BLOCKS * TOK
HEADS = 16
GROUPS = 2
KV = 4
RING = 4
ORDER = (3, 2, 1)
NEAR = 4
FAR = BLOCKS // NEAR
ROWS = TOK // KV
RAW = (WIN + 1) * TOK
TOKP = 2 * GROUPS * TOK
PIECE = SLOTS * NEAR
KEYS = RAW + BLOCKS * SLOTS
MSCALE = 1.0 + 0.1 * math.log(16.0)
SCALE2 = math.log2(math.e) / math.sqrt(HD)
NEG = -1e30
BF = jnp.bfloat16
F32 = jnp.float32


def yarn_freqs():
    index = np.arange(HD // 2, dtype=np.float32)
    inverse = np.exp(np.float32(-(2.0 / HD) * math.log(500000.0)) * index).astype(np.float32)
    ratio = np.float32(8192.0) * inverse / np.float32(2.0 * math.pi)
    ramp = np.clip((ratio - 1.0) / 31.0, 0.0, 1.0).astype(np.float32)
    freqs = inverse * (ramp + (1.0 - ramp) / np.float32(16.0))
    return np.tile(np.concatenate([freqs, freqs])[None, :], (8, 1)).astype(np.float32)


def turn_tables(place0, freqs):
    places = (place0 + lax.broadcasted_iota(jnp.int32, (TOK, HD), 0)).astype(F32)
    angle = places * freqs
    first = lax.broadcasted_iota(jnp.int32, (TOK, HD), 1) < HD // 2
    sine = jnp.sin(angle)
    return jnp.cos(angle), jnp.where(first, -sine, sine)


def turn(x, cosine, sine, scale=MSCALE):
    return ((x * cosine + pltpu.roll(x, HD // 2, 1) * sine) * scale).astype(BF)


def prep_kernel(bs, freqs, k, v, dk, pk, dv, pv, own, mem, *scratch):
    scr, pool, s_bs, s_freqs, s_k, s_v, s_dk, s_pk, s_dv, s_pv, sem = scratch
    pairs = (
        (bs, s_bs), (freqs, s_freqs), (k, s_k), (v, s_v),
        (dk, s_dk), (pk, s_pk), (dv, s_dv), (pv, s_pv),
    )
    copies = [pltpu.make_async_copy(a, b, sem.at[i]) for i, (a, b) in enumerate(pairs)]
    for c in copies:
        c.start()
    for c in copies:
        c.wait()
    me = lax.axis_index("ctx")
    cosine, sine = turn_tables(s_bs[me], s_freqs[0:1, :])
    scr[...] = s_k[...].astype(F32)
    for g in range(GROUPS):
        rot = turn(scr[:, g, :], cosine, sine)
        own[g * TOK : (g + 1) * TOK, :] = rot
        grouped = rot.astype(F32).reshape(SLOTS, STRIDE, HD)
        pool[g * SLOTS : (g + 1) * SLOTS, :] = jnp.sum(grouped * s_dk[...][None], axis=1)
    scr[...] = s_v[...].astype(F32)
    for g in range(GROUPS):
        val = scr[:, g, :]
        own[(GROUPS + g) * TOK : (GROUPS + g + 1) * TOK, :] = val.astype(BF)
        grouped = val.reshape(SLOTS, STRIDE, HD)
        at = (GROUPS + g) * SLOTS
        pool[at : at + SLOTS, :] = jnp.sum(grouped * s_dv[...][None], axis=1)
    half = GROUPS * SLOTS
    mk = jnp.dot(pool[:half, :], s_pk[...], precision=lax.Precision.HIGHEST, preferred_element_type=F32)
    mv = jnp.dot(pool[half:, :], s_pv[...], precision=lax.Precision.HIGHEST, preferred_element_type=F32)
    both = jnp.concatenate([mk, mv], axis=0).astype(BF)
    mem[...] = jnp.broadcast_to(both[None], mem.shape)


def query_kernel(bs, freqs, q, rotq, scr):
    me = lax.axis_index("ctx")
    cosine, sine = turn_tables(bs[me], freqs[0:1, :])
    scr[...] = q[...].astype(F32)
    for h in range(HEADS):
        rotq[h] = turn(scr[:, h, :], cosine, sine)


def far_kernel(mem, row1, row2, rotq, bias, far, scr):
    scr[...] = mem[...].astype(F32)
    kinds = 2 * GROUPS * SLOTS
    slots = jnp.concatenate([scr[:, r, :] for r in range(kinds)], axis=0).astype(BF)
    far[...] = jnp.broadcast_to(slots[None], far.shape)


def ring_kernel(own, row1, row2, far, ra, rb, rc):
    me = lax.rem(lax.axis_index("ctx"), RING)
    for s, out in zip(ORDER, (ra, rb, rc)):
        if s != 2:
            out[TOKP:, :] = row1[...]

        @pl.when(me + s < RING)
        def _():
            out[:TOKP, :] = own[...]

        @pl.when(me + s >= RING)
        def _():
            out[:TOKP, :] = row2[...]


def bias_kernel(bs, bias):
    me = lax.axis_index("ctx")
    pos = lax.rem(me, RING)
    place = bs[me] + lax.broadcasted_iota(jnp.int32, (TOK, TOK), 1)
    row = lax.broadcasted_iota(jnp.int32, (TOK, TOK), 0)
    backs = [0, RING]
    for s in range(1, RING):
        wrapped = pos < s
        backs += [jnp.where(wrapped, RING + s, s), jnp.where(wrapped, s, RING + s)]
    backs += [WIN]
    for b, back in enumerate(backs):
        there = bs[lax.rem(me - back + BLOCKS, BLOCKS)] + row
        ok = (there <= place) & (there > place - WINDOW)
        bias[b * TOK : (b + 1) * TOK, :] = jnp.where(ok, 0.0, NEG).astype(BF)
    for lo in range(0, BLOCKS * SLOTS, TOK):
        at = lo + row
        block = at // PIECE * NEAR + (at & (NEAR - 1))
        slot = (at & (PIECE - 1)) // NEAR
        ok = ((bs[0] + TOK * block) & (SEQ - 1)) + (slot + 1) * STRIDE <= place + 1
        bias[RAW + lo : RAW + lo + TOK, :] = jnp.where(ok, 0.0, NEG).astype(BF)


def key_tiles():
    half = SLOTS * BLOCKS // 2
    tiles = [(0, [("own", 0, TOK), ("row1", 0, TOK)])]
    for s in range(1, RING):
        tiles.append((2 * s * TOK, [(s, 0, TOK), ("pass", 0, TOK) if s == 2 else (s, TOKP, TOK)]))
    tiles.append((RAW, [("mem", 0, half)]))
    tiles.append((RAW + half, [("mem", half, half)]))
    tiles.append((RAW - TOK, [("row2", 0, TOK)]))
    return [(lo, sum(n for _, _, n in tile), tile) for lo, tile in tiles]


def gather_tile(refs, tile, kind):
    parts = []
    for name, lo, n in tile:
        if name == "mem":
            rows = slice(kind * PIECE, (kind + 1) * PIECE)
            parts += [refs[name][i, rows, :] for i in range(lo // PIECE, (lo + n) // PIECE)]
        else:
            at = lo + kind * TOK
            parts.append(refs[name][at : at + n, :])
    return parts[0] if len(parts) == 1 else jnp.concatenate(parts, axis=0)


def chunk_kernel(offs, rotq, bias, own, row1, row2, r1, r2, r3, passed, mem, *rest):
    refs = {"own": own, "row1": row1, "row2": row2, 1: r1, 2: r2, 3: r3, "pass": passed, "mem": mem}
    outs, s = rest[:-1], rest[-1]
    firsts = [pl.multiple_of((lax.axis_index("kv") ^ o) * ROWS, ROWS) for o in offs]
    heads = HEADS // GROUPS
    r = lax.broadcasted_iota(jnp.int32, (heads * ROWS, TOK), 0) & (ROWS - 1)
    c = lax.broadcasted_iota(jnp.int32, (heads * ROWS, TOK), 1)
    unit = jnp.concatenate([jnp.where(r + f == c, 1.0, 0.0).astype(BF) for f in firsts], axis=0)
    tops = []
    for g in range(GROUPS):
        q = jnp.concatenate(
            [rotq[g * heads + i, pl.ds(f, ROWS), :] for f in firsts for i in range(heads)], axis=0
        )
        qa = jnp.concatenate([q, unit], axis=1)
        high = None
        for lo, size, tile in key_tiles():
            k = gather_tile(refs, tile, g)
            ka = jnp.concatenate([k, bias[lo : lo + size, :]], axis=1)
            x = lax.dot_general(qa, ka, (((1,), (1,)), ((), ())), preferred_element_type=F32)
            s[g, :, lo : lo + size] = x
            for i in range(size // HD):
                part = x[:, i * HD : (i + 1) * HD]
                high = part if high is None else jnp.maximum(high, part)
        tops.append(jnp.max(high, axis=1, keepdims=True))
    for g in range(GROUPS):
        mixed = None
        for lo, size, tile in key_tiles():
            w = jnp.exp2((s[g, :, lo : lo + size] - tops[g]) * SCALE2).astype(BF)
            v = gather_tile(refs, tile, GROUPS + g)
            va = jnp.concatenate([v, jnp.ones((size, HD), BF)], axis=1)
            part = jnp.dot(w, va, preferred_element_type=F32)
            mixed = part if mixed is None else mixed + part
        res = (mixed[:, :HD] / mixed[:, HD:]).astype(BF)
        for n, out in enumerate(outs):
            for i in range(heads):
                h, at = g * heads + i, (n * heads + i) * ROWS
                out[:, h * HD : (h + 1) * HD] = res[at : at + ROWS, :]


def join_kernel(a, b, c, d, out, sem):
    me = lax.axis_index("kv")
    wide = HEADS * HD
    copies = []
    for off, part in enumerate((a, b, c, d)):
        lane = pl.multiple_of((me ^ off) * wide, wide)
        copies.append(pltpu.make_async_copy(part, out.at[:, pl.ds(lane, wide)], sem.at[off]))
    for x in copies:
        x.start()
    for x in copies:
        x.wait()


def call(kernel, out_shape, scratch, flops, spaces, *args, out_space=pltpu.VMEM, grant=32, alias=None):
    multi = isinstance(out_shape, tuple)
    vm = pl.BlockSpec(memory_space=out_space)
    return pl.pallas_call(
        kernel,
        out_shape=out_shape,
        in_specs=[pl.BlockSpec(memory_space=s) for s in spaces],
        out_specs=(vm,) * len(out_shape) if multi else vm,
        scratch_shapes=scratch,
        input_output_aliases=alias or {},
        compiler_params=pltpu.CompilerParams(vmem_limit_bytes=grant * 2**20),
        cost_estimate=pl.CostEstimate(flops=flops, bytes_accessed=2**10, transcendentals=0),
    )(*args)


def shape(*dims, dtype=BF):
    return jax.ShapeDtypeStruct(dims, dtype)


near = [[NEAR * o + p for p in range(NEAR)] for o in range(FAR)]
strided = [[NEAR * o + p for o in range(FAR)] for p in range(NEAR)]
SM, VM, HB = pltpu.SMEM, pltpu.VMEM, pltpu.HBM


def shards(queries, keys, values, block_start, depth_k, point_k, depth_v, point_v):
    freqs = jnp.asarray(yarn_freqs())
    pack = 2 * GROUPS
    params = (block_start, freqs, keys, values, depth_k, point_k, depth_v, point_v)
    own, mem = call(
        prep_kernel,
        (shape(pack * TOK, HD), shape(NEAR, pack * SLOTS, HD)),
        [pltpu.VMEM((TOK, GROUPS, HD), F32), pltpu.VMEM((pack * SLOTS, HD), F32)]
        + [(pltpu.SMEM if i == 0 else pltpu.VMEM)(x.shape, x.dtype) for i, x in enumerate(params)]
        + [pltpu.SemaphoreType.DMA((len(params),))],
        10**9,
        (HB,) * len(params),
        *params,
        grant=60,
    )
    row1, row2 = (
        lax.ppermute(own, "ctx", [((i - d) % BLOCKS, i) for i in range(BLOCKS)])
        for d in (RING, 2 * RING)
    )
    mem = lax.all_to_all(mem, "ctx", 0, 0, axis_index_groups=near)
    rotq = call(
        query_kernel, shape(HEADS, TOK, HD), [pltpu.VMEM((TOK, HEADS, HD), F32)], 10**9,
        (SM, VM, VM),
        block_start, freqs, queries,
    )
    bias = call(bias_kernel, shape(KEYS, TOK), [], 10**3, (SM,), block_start)
    far = call(
        far_kernel, shape(FAR, pack * PIECE, HD),
        [pltpu.VMEM((NEAR, pack * SLOTS, HD), F32)], 10**3, (VM,) + (pl.ANY,) * 4, mem, row1, row2, rotq, bias,
    )
    mem = lax.all_to_all(far, "ctx", 0, 0, axis_index_groups=strided)
    rings = call(
        ring_kernel, tuple(shape(TOKP if s == 2 else 2 * TOKP, HD) for s in ORDER), [], 10**3, (VM,) * 3 + (pl.ANY,),
        own, row1, row2, far,
    )
    turned = {
        s: lax.ppermute(
            x, "ctx", [(i, i // RING * RING + (i + s) % RING) for i in range(BLOCKS)]
        )
        for s, x in zip(ORDER, rings)
    }
    passed = lax.ppermute(
        turned[3][TOKP:], "ctx", [(i, i // RING * RING + (i + 3) % RING) for i in range(BLOCKS)]
    )
    rings = [turned[s] for s in (1, 2, 3)] + [passed]
    parts = {}
    for offs in ((3, 2), (1, 0)):
        got = call(
            functools.partial(chunk_kernel, offs), (shape(ROWS, HEADS * HD),) * len(offs),
            [pltpu.VMEM((GROUPS, len(offs) * HEADS // GROUPS * ROWS, KEYS), F32)], 10**6,
            (VM,) * 10, rotq, bias, own, row1, row2, *rings, mem,
        )
        for off, part in zip(offs, got):
            if off:
                part = lax.ppermute(part, "kv", [(i, i ^ off) for i in range(KV)])
            parts[off] = part
    return call(
        join_kernel, shape(ROWS, KV * HEADS * HD), [pltpu.SemaphoreType.DMA((KV,))], 10**8,
        (VM,) * 4, *(parts[i] for i in range(KV)), out_space=HB,
    )


def solution(mesh):
    placed = (
        P("ctx", "kv", None),
        P("ctx", "kv", None),
        P("ctx", "kv", None),
        P(),
        P(),
        P(),
        P(),
        P(),
    )
    return jax.shard_map(
        shards, mesh=mesh, in_specs=placed, out_specs=P(("ctx", "kv"), None), check_vma=False
    )
```
